32 devices in a mesh: dp: 4 (over z), ctx: 4 (over y, x), tp: 2 (over core).
Axes of the slice: x: 2, y: 2, z: 4, core: 2. Of those that a mesh axis runs over, the one named last changes fastest.
Arguments:
- stream_in: bfloat16 [4, 1024, 1024], P('dp', 'ctx'), may hold values from -6 to 6
- norm_gain: bfloat16 [1024], P('dp'), may hold values from 0.5 to 1.5
- in_weight: bfloat16 [2, 1024, 2048], P(None, 'dp', 'tp'), may hold values from -0.1875 to 0.1875
- out_weight: bfloat16 [2048, 1024], P('tp', 'dp'), may hold values from -0.125 to 0.125
- xproj_weight: bfloat16 [96, 2048], P('dp', 'tp'), may hold values from -0.125 to 0.125
- dt_weight: bfloat16 [64, 2048], P('dp', 'tp'), may hold values from -0.75 to 0.75
- a_log: bfloat16 [16, 2048], P('dp', 'tp'), may hold values from -6 to 0.69921875
- convolution_weight: bfloat16 [4, 2, 1024], P(None, 'tp', 'dp'), may hold values from -3 to 3
- convolution_bias: bfloat16 [2, 1024], P('tp', 'dp'), may hold values from -3 to 3
- step_size_bias: bfloat16 [2, 1024], P('tp', 'dp'), may hold values from -6 to -3
- skip_term_scale: bfloat16 [2, 1024], P('tp', 'dp'), may hold values from 0.5 to 1.5
- seg_ids: int32 [4, 1024], P('dp', 'ctx'), may hold values from 0 to 15, as said below
- pad_mask: int32 [4, 1024], P('dp', 'ctx'), may hold values from 0 to 1, as said below
- out_grad: bfloat16 [4, 1024, 1024], P('dp', 'ctx'), may hold values from -6 to 6
Outputs:
- stream_out: bfloat16 [4, 1024, 1024], P('dp', 'ctx')
- stream_grad: float32 [4, 1024, 1024], P('dp', 'ctx')
- norm_gain_grad: float32 [1024], P('dp')
- input_weight_gradient: float32 [2, 1024, 2048], P(None, 'dp', 'tp')
- out_weight_grad: float32 [2048, 1024], P('tp', 'dp')
- xproj_grad: float32 [96, 2048], P('dp', 'tp')
- dt_weight_grad: float32 [64, 2048], P('dp', 'tp')
- a_log_grad: float32 [16, 2048], P('dp', 'tp')
- conv_weight_grad: float32 [4, 2, 1024], P(None, 'tp', 'dp')
- conv_bias_grad: float32 [2, 1024], P('tp', 'dp')
- dt_bias_grad: float32 [2, 1024], P('tp', 'dp')
- skip_gain_grad: float32 [2, 1024], P('tp', 'dp')
The draws below stay inside these ranges and needn't reach their ends.
Inputs may be any that keep to these rules, and one draw needn't show every extreme that they name: `seg_ids`: along each sequence the document number starts at 0 and never falls; the last byte of every sequence has number 16 - 1; a document may span many spans of positions. `pad_mask`: in each sequence the ones form a leading run and at least one trailing byte is 0; at most 1024 // 8 bytes of a sequence are 0.
All inputs are finite; a program needn't handle non-finite values.
Results may differ from the reference program's by a relative error of at most 0.011.
Values may be sent and summed in bfloat16 or wider, within the bound.
A program may use at most 256 MiB of HBM per device.

```python
import math
import jax
import jax.numpy as jnp
from jax import lax

D = 1024
DI = 2048
DS = 16
CONV_TAP_COUNT = 4
R = 64
DOCS = 16
XW = 96
INNER_PER_SHARD = 1024
SEQS = 4
LEN = 1024
N_TP = 2


def draw_seg_ids(key, part):
    picks = jax.random.randint(jax.random.fold_in(key, 11), (SEQS, DOCS - 1), 1, LEN)
    bounds = 1 + picks * picks // LEN
    where = jnp.arange(LEN, dtype=jnp.int32)
    return jnp.sum((where[None, :, None] >= bounds[:, None, :]).astype(jnp.int32), axis=2)


def draw_pad_mask(key, part):
    cut = jax.random.randint(jax.random.fold_in(key, 23), (SEQS, 1), 1, LEN // 8 + 1)
    where = jnp.arange(LEN, dtype=jnp.int32)
    return (where[None, :] < LEN - cut).astype(jnp.int32)


def level_of(key, shape, cuts, low, largest):
    gain = 1.0
    for position, parts in cuts:
        steps = jax.random.uniform(jax.random.fold_in(jax.random.fold_in(key, 6), position), (parts,), jnp.float32, low / len(cuts), largest / len(cuts))
        gain = gain * jnp.repeat(jnp.exp(steps), shape[position] // parts).reshape((-1,) + (1,) * (len(shape) - 1 - position))
    return gain


def gaussian(own_key, dims, scale, limit, cuts=(), kind=jnp.bfloat16):
    drawn = jax.random.normal(own_key, dims, jnp.float32) * scale
    if len(cuts) > 0:
        drawn = level_of(own_key, dims, cuts, -0.22, 0.18) * drawn
    return jnp.clip(drawn, min=-limit, max=limit).astype(kind)


def setup_inputs(seed: int = 0) -> dict:
    arg_keys = jax.random.split(jax.random.key(seed), 15)
    return {
        "stream_in": gaussian(arg_keys[0], (SEQS, LEN, D), 1.0, 6.0, ((0, 4), (1, 4))),
        "norm_gain": jnp.clip(1.0 + 0.1 * jax.random.normal(arg_keys[1], (D,), jnp.float32), 0.5, 1.5).astype(jnp.bfloat16),
        "in_weight": gaussian(arg_keys[2], (2, D, DI), D ** -0.5, 0.1875, ((1, 4), (2, 2))),
        "out_weight": gaussian(arg_keys[3], (DI, D), DI ** -0.5, 0.125, ((0, 2), (1, 4))),
        "xproj_weight": gaussian(arg_keys[4], (XW, DI), DI ** -0.5, 0.125, ((0, 4), (1, 2))),
        "dt_weight": gaussian(arg_keys[5], (R, DI), R ** -0.5, 0.75, ((0, 4), (1, 2))),
        "a_log": jnp.clip(-6.0 + 6.6992188 * jax.random.uniform(arg_keys[6], (DS, DI), jnp.float32) ** level_of(arg_keys[6], (DS, DI), ((0, 4), (1, 2)), -0.2, 0.2), -6.0, 0.69921875).astype(jnp.bfloat16),
        "convolution_weight": gaussian(arg_keys[7], (CONV_TAP_COUNT, N_TP, INNER_PER_SHARD), CONV_TAP_COUNT ** -0.5, 3.0, ((1, 2), (2, 4))),
        "convolution_bias": gaussian(arg_keys[8], (N_TP, INNER_PER_SHARD), 0.5, 3.0, ((0, 2), (1, 4))),
        "step_size_bias": jnp.clip(-6.0 + 3.0 * jax.random.uniform(arg_keys[9], (N_TP, INNER_PER_SHARD), jnp.float32) ** level_of(arg_keys[9], (N_TP, INNER_PER_SHARD), ((0, 2), (1, 4)), -0.2, 0.2), -6.0, -3.0).astype(jnp.bfloat16),
        "skip_term_scale": jnp.clip(0.5 + 1.0 * jax.random.uniform(arg_keys[10], (N_TP, INNER_PER_SHARD), jnp.float32) ** level_of(arg_keys[10], (N_TP, INNER_PER_SHARD), ((0, 2), (1, 4)), -0.2, 0.2), 0.5, 1.5).astype(jnp.bfloat16),
        "seg_ids": draw_seg_ids(jax.random.fold_in(arg_keys[14], 71), 0),
        "pad_mask": draw_pad_mask(jax.random.fold_in(arg_keys[14], 71), 0),
        "out_grad": gaussian(arg_keys[13], (SEQS, LEN, D), 1.0, 6.0, ((0, 4), (1, 4))),
    }


EPS = 1e-05
HIGH = lax.Precision.HIGHEST

@jax.custom_vjp
def low(v):
    return lax.optimization_barrier(v.astype(jnp.bfloat16)).astype(jnp.float32)

@jax.custom_vjp
def low_back(v):
    return v

def low_keep(v):
    return (low(v), None)

def low_pass(kept, grad):
    return (grad,)

def back_keep(v):
    return (v, None)

def back_low(kept, grad):
    return (low(grad),)
low.defvjp(low_keep, low_pass)
low_back.defvjp(back_keep, back_low)

def link(first, second):
    return (first[0] * second[0], first[1] * second[0] + second[1])

def mixer(params, pieces):
    norm_gain, in_weight, out_weight, xproj_weight, dt_weight, a_log, convolution_weight, convolution_bias, step_size_bias, skip_term_scale = params
    stream, seg_row, mask_row = pieces
    length = stream.shape[0]
    kernel = convolution_weight.shape[0]
    channels = in_weight.shape[2]
    low_dims = dt_weight.shape[0]
    states = a_log.shape[0]
    taps = convolution_weight.reshape(kernel, channels)
    conv_shift = convolution_bias.reshape(channels)
    dt_shift = step_size_bias.reshape(channels)
    skip_vec = skip_term_scale.reshape(channels)
    rstd = lax.rsqrt(lax.optimization_barrier(jnp.mean(stream * stream, axis=1, keepdims=True)) + EPS)
    normed = low(stream * rstd * norm_gain)
    inner = low_back(low(jnp.dot(normed, in_weight[0], precision=HIGH)))
    gate = low_back(low(jnp.dot(normed, in_weight[1], precision=HIGH)))
    conv_lag = kernel - 1
    padded = jnp.concatenate([jnp.zeros((conv_lag, channels), inner.dtype), inner], axis=0)
    seg_pad = jnp.concatenate([jnp.full((conv_lag,), -1, jnp.int32), seg_row.astype(jnp.int32)])
    pre = jnp.zeros((length, channels), stream.dtype) + conv_shift
    for offset in range(kernel):
        same = (seg_pad[conv_lag - offset:conv_lag - offset + length] == seg_row).astype(stream.dtype)
        pre = pre + taps[conv_lag - offset] * padded[conv_lag - offset:conv_lag - offset + length] * same[:, None]
    keep = (seg_pad[conv_lag - 1:conv_lag - 1 + length] == seg_row).astype(stream.dtype)
    act = low(pre * jax.nn.sigmoid(pre))
    mixed = low_back(jnp.dot(act, xproj_weight.T, precision=HIGH))
    low_rank = low(mixed[:, :low_dims])
    b_in = mixed[:, low_dims:low_dims + states]
    c_out = mixed[:, low_dims + states:]
    dt_values = jax.nn.softplus(low_back(jnp.dot(low_rank, dt_weight, precision=HIGH)) + dt_shift)
    a_neg = -jnp.exp(a_log)
    block_len = math.gcd(length, 128)
    block_count = length // block_len

    def split(array):
        return array.reshape((block_count, block_len) + array.shape[1:])

    def run(start, piece):
        dt_block, act_block, b_block, c_block, keep_block = piece
        decay = jnp.exp(dt_block[:, None, :] * a_neg[None]) * keep_block[:, None, None]
        drive = (dt_block * act_block)[:, None, :] * b_block[:, :, None]
        prods, local = lax.associative_scan(link, (decay, drive), axis=0)
        hidden = local + prods * start[None]
        return (hidden[-1], lax.optimization_barrier(jnp.sum(c_block[:, :, None] * hidden, axis=1)))
    zero_state = jnp.zeros((states, channels), stream.dtype)
    _, outputs = lax.scan(jax.checkpoint(run), zero_state, (split(dt_values), split(act), split(b_in), split(c_out), split(keep)))
    y_total = outputs.reshape(length, channels) + skip_vec * act
    gated = low(y_total * gate * jax.nn.sigmoid(gate))
    branch = jnp.dot(gated, out_weight, precision=HIGH)
    return stream + mask_row[:, None] * branch

def reference(stream_in, norm_gain, in_weight, out_weight, xproj_weight, dt_weight, a_log, convolution_weight, convolution_bias, step_size_bias, skip_term_scale, seg_ids, pad_mask, out_grad):
    params = (norm_gain.astype(jnp.float32), in_weight.astype(jnp.float32), out_weight.astype(jnp.float32), xproj_weight.astype(jnp.float32), dt_weight.astype(jnp.float32), a_log.astype(jnp.float32), convolution_weight.astype(jnp.float32), convolution_bias.astype(jnp.float32), step_size_bias.astype(jnp.float32), skip_term_scale.astype(jnp.float32))
    stream = stream_in.astype(jnp.float32)
    mask_float = pad_mask.astype(jnp.float32)

    def forward(stream_all, *weights):

        def one_seq(pieces):
            return jax.checkpoint(mixer)(weights, pieces)
        return lax.map(one_seq, (stream_all, seg_ids, mask_float))
    result, pull = jax.vjp(forward, stream, *params)
    grads = pull(out_grad.astype(jnp.float32))
    return (result.astype(jnp.bfloat16), grads[0], grads[1], grads[2], grads[3], grads[4], grads[5], grads[6], grads[7], grads[8], grads[9], grads[10])
```

```python
import math

import jax
import jax.numpy as jnp
from jax import lax
from jax.experimental import pallas as pl
from jax.experimental.pallas import tpu as pltpu
from jax.sharding import PartitionSpec as P

EPS = 1e-05
VMEM_LIMIT = 63 * 2**20


def from_behind(x, axis, by):
    count = lax.axis_size(axis)
    pairs = [(i, i + by) for i in range(count) if 0 <= i + by < count]
    return lax.ppermute(x, axis, pairs)


def entering(x, axis, combine, identity, reverse):
    count, position = (lax.axis_size(axis), lax.axis_index(axis))
    everything = jax.tree.map(
        lambda part, kind: lax.all_gather(part.astype(kind), axis), x, (jnp.bfloat16, jnp.bfloat16)
    )
    start = jax.tree.map(
        lambda part, zero: jnp.broadcast_to(jnp.asarray(zero, part.dtype), part.shape), x, identity
    )

    def step(k, before):
        at = count - 1 - k if reverse else k
        reached = at > position if reverse else at < position
        new = combine(
            before, jax.tree.map(lambda part, own: part[at].astype(own.dtype), everything, x)
        )
        return jax.tree.map(lambda a, b: jnp.where(reached, a, b), new, before)

    return lax.fori_loop(0, count, step, start)


def silu_slope(value):
    sigma = jax.nn.sigmoid(value)
    return sigma * (1.0 + value * (1.0 - sigma))


def link(first, second):
    return (first[0] * second[0], first[1] * second[0] + second[1])


def chain_prefix(decay, drive, backward):
    return lax.associative_scan(link, (decay, drive), reverse=backward, axis=1)


def shards(
    stream_in,
    norm_gain,
    in_weight,
    out_weight,
    xproj_weight,
    dt_weight,
    a_log,
    convolution_weight,
    convolution_bias,
    step_size_bias,
    skip_term_scale,
    seg_ids,
    pad_mask,
    out_grad,
):
    gathered = (
        lax.all_gather(norm_gain, "dp", axis=0, tiled=True),
        lax.all_gather(in_weight, "dp", axis=1, tiled=True),
        lax.all_gather(out_weight, "dp", axis=1, tiled=True),
        lax.all_gather(xproj_weight, "dp", axis=0, tiled=True),
        lax.all_gather(dt_weight, "dp", axis=0, tiled=True),
        lax.all_gather(a_log, "dp", axis=0, tiled=True),
        lax.all_gather(convolution_weight, "dp", axis=2, tiled=True),
        lax.all_gather(convolution_bias, "dp", axis=1, tiled=True),
        lax.all_gather(step_size_bias, "dp", axis=1, tiled=True),
        lax.all_gather(skip_term_scale, "dp", axis=1, tiled=True),
    )
    (
        gain_full,
        win_full,
        wout_full,
        xproj_full,
        dtw_full,
        alog_full,
        convw_full,
        convb_full,
        dtb_full,
        skip_full,
    ) = gathered
    seq_count, tok_count, model_width = stream_in.shape
    channels = win_full.shape[2]
    low_dims = dtw_full.shape[0]
    states = alog_full.shape[0]
    kernel = convw_full.shape[0]
    conv_lag = kernel - 1
    row_count = seq_count * tok_count
    block_len = math.gcd(tok_count, 128)
    block_count = tok_count // block_len
    gain_vec = gain_full.astype(jnp.float32)
    conv_taps = convw_full.reshape(kernel, channels).astype(jnp.float32)
    conv_shift = convb_full.reshape(channels).astype(jnp.float32)
    dt_shift = dtb_full.reshape(channels).astype(jnp.float32)
    skip_vec = skip_full.reshape(channels).astype(jnp.float32)
    a_neg = -jnp.exp(alog_full.astype(jnp.float32))

    def to_blocks(array):
        shaped = array.reshape((seq_count, block_count, block_len) + array.shape[2:])
        return jnp.moveaxis(shaped, 1, 0)

    def from_blocks(array):
        return jnp.moveaxis(array, 0, 1).reshape((seq_count, tok_count) + array.shape[3:])

    def decay_of(dt_block, keep_block):
        return jnp.exp(dt_block[:, :, None, :] * a_neg) * keep_block[:, :, None, None]

    def drive_of(dt_block, act_block, b_block):
        return (dt_block * act_block)[:, :, None, :] * b_block[:, :, :, None]

    def reverse_terms(decay, rhs, carry_in):
        shifted = jnp.concatenate([decay[:, 1:], jnp.zeros_like(decay[:, :1])], axis=1)
        rhs = rhs.at[:, -1].add(carry_in)
        _, grads = chain_prefix(shifted, rhs, True)
        return (grads, decay[:, 0] * grads[:, 0])

    stream = stream_in.astype(jnp.float32)
    rstd = lax.rsqrt(jnp.mean(stream * stream, axis=2, keepdims=True) + EPS)
    normed = (stream * rstd * gain_vec).astype(jnp.bfloat16)
    normed_flat = normed.reshape(row_count, model_width)
    projected = jnp.einsum(
        "rd,kdc->krc", normed_flat, win_full, preferred_element_type=jnp.float32
    ).astype(jnp.bfloat16)
    inner = projected[0].reshape(seq_count, tok_count, channels)
    gate_vals = projected[1].astype(jnp.float32).reshape(seq_count, tok_count, channels)
    seg_low = seg_ids.astype(jnp.bfloat16)
    prev_inner, prev_seg = from_behind(
        (inner[:, tok_count - conv_lag :], seg_low[:, tok_count - conv_lag :]), "ctx", 1
    )
    inner_vals = inner.astype(jnp.float32)
    prev_vals = prev_inner.astype(jnp.float32)
    seg_float = seg_ids.astype(jnp.float32)
    prev_segf = prev_seg.astype(jnp.float32)
    windows = []
    same_list = []
    pre = jnp.zeros((seq_count, tok_count, channels), jnp.float32) + conv_shift
    for offset in range(kernel):
        if offset == 0:
            window = inner_vals
            seg_window = seg_float
        else:
            window = jnp.concatenate(
                [prev_vals[:, conv_lag - offset :], inner_vals[:, : tok_count - offset]], axis=1
            )
            seg_window = jnp.concatenate(
                [prev_segf[:, conv_lag - offset :], seg_float[:, : tok_count - offset]], axis=1
            )
        same = (seg_window == seg_float).astype(jnp.float32)
        windows.append(window)
        same_list.append(same)
        pre = pre + conv_taps[conv_lag - offset] * window * same[:, :, None]
    keep = same_list[1]
    act = (pre * jax.nn.sigmoid(pre)).astype(jnp.bfloat16)
    act_flat = act.reshape(row_count, channels)
    act_vals = act.astype(jnp.float32)
    mixed_part = jnp.einsum("rc,wc->rw", act_flat, xproj_full, preferred_element_type=jnp.float32)
    mixed = lax.psum(mixed_part, "tp")
    low_rank = mixed[:, :low_dims].astype(jnp.bfloat16)
    b_in = mixed[:, low_dims : low_dims + states].reshape(seq_count, tok_count, states)
    c_out = mixed[:, low_dims + states :].reshape(seq_count, tok_count, states)
    dt_arg = (
        jnp.dot(low_rank, dtw_full, preferred_element_type=jnp.float32).reshape(
            seq_count, tok_count, channels
        )
        + dt_shift
    )
    dt_values = jax.nn.softplus(dt_arg)

    def forward_block(carry, piece):
        start, through = carry
        dt_block, act_block, b_block, c_block, keep_block = piece
        decay = decay_of(dt_block, keep_block)
        prods, local = chain_prefix(decay, drive_of(dt_block, act_block, b_block), False)
        hidden = local + prods * start[:, None]
        outputs = jnp.sum(c_block[:, :, :, None] * hidden, axis=2)
        return ((hidden[:, -1], through * prods[:, -1]), (outputs, start, through))

    zero_state = jnp.zeros((seq_count, states, channels), jnp.float32)
    one_state = jnp.ones_like(zero_state)
    dt_blocks = to_blocks(dt_values)
    act_blocks = to_blocks(act_vals)
    b_blocks = to_blocks(b_in)
    c_blocks = to_blocks(c_out)
    keep_blocks = to_blocks(keep)
    (last_state, through), (y_blocks, local_starts, befores) = lax.scan(
        forward_block,
        (zero_state, one_state),
        (dt_blocks, act_blocks, b_blocks, c_blocks, keep_blocks),
    )
    _, entry_state = entering((through, last_state), "ctx", link, (one_state, zero_state), False)
    cum_dt = jnp.cumsum(dt_values, axis=1)
    alive = jnp.cumprod(keep, axis=1)
    cum_blocks = to_blocks(cum_dt)

    def correct(piece):
        cum_block, c_block, alive_block = piece
        carried = jnp.exp(cum_block[:, :, None, :] * a_neg) * entry_state[:, None]
        return alive_block[:, :, None] * jnp.sum(c_block[:, :, :, None] * carried, axis=2)

    corrections = from_blocks(lax.map(correct, (cum_blocks, c_blocks, to_blocks(alive))))
    y_total = from_blocks(y_blocks) + corrections + skip_vec * act_vals
    gate_act = gate_vals * jax.nn.sigmoid(gate_vals)
    gated_flat = (y_total * gate_act).astype(jnp.bfloat16).reshape(row_count, channels)
    branch_part = jnp.dot(gated_flat, wout_full, preferred_element_type=jnp.float32)
    branch = (
        lax.psum(branch_part.astype(jnp.bfloat16), "tp")
        .astype(jnp.float32)
        .reshape(seq_count, tok_count, model_width)
    )
    mask_float = pad_mask.astype(jnp.float32)
    stream_out = (stream + mask_float[:, :, None] * branch).astype(jnp.bfloat16)
    masked_flat = (out_grad * pad_mask[:, :, None].astype(jnp.bfloat16)).reshape(
        row_count, model_width
    )
    grad_wout = jnp.einsum("rc,rd->cd", gated_flat, masked_flat, preferred_element_type=jnp.float32)
    grad_gated = jnp.einsum(
        "rd,cd->rc", masked_flat, wout_full, preferred_element_type=jnp.float32
    ).reshape(seq_count, tok_count, channels)
    grad_y = grad_gated * gate_act
    grad_gate = (grad_gated * y_total * silu_slope(gate_vals)).astype(jnp.bfloat16)
    grad_skip = jnp.sum(grad_y * act_vals, axis=(0, 1))
    gy_blocks = to_blocks(grad_y)
    true_starts = local_starts + befores * entry_state[None]

    def back_core(carry_in, piece):
        dt_block, act_block, b_block, c_block, keep_block, gy_block, start = piece
        decay = decay_of(dt_block, keep_block)
        prods, local = chain_prefix(decay, drive_of(dt_block, act_block, b_block), False)
        hidden = local + prods * start[:, None]
        earlier = jnp.concatenate([start[:, None], hidden[:, :-1]], axis=1)
        grads, carry_out = reverse_terms(
            decay, c_block[:, :, :, None] * gy_block[:, :, None, :], carry_in
        )
        stepped = earlier * decay
        weighted = grads * stepped
        along_b = jnp.sum(grads * b_block[:, :, :, None], axis=2)
        grad_dt = jnp.sum(weighted * a_neg, axis=2) + along_b * act_block
        grad_act = along_b * dt_block
        grad_b = jnp.sum(grads * (dt_block * act_block)[:, :, None, :], axis=3)
        grad_c = jnp.sum(gy_block[:, :, None, :] * hidden, axis=3)
        return (carry_out, weighted, stepped, (grad_dt, grad_act, grad_b, grad_c))

    back_pieces = (dt_blocks, act_blocks, b_blocks, c_blocks, keep_blocks, gy_blocks, true_starts)
    zero_acc = jnp.zeros((states, channels), jnp.float32)
    cum_end = cum_dt[:, -1]
    suffix = jnp.flip(jnp.cumprod(jnp.flip(keep, axis=1), axis=1), axis=1)
    rest = jnp.concatenate([suffix[:, 1:], jnp.ones((seq_count, 1), jnp.float32)], axis=1)
    rest_blocks = to_blocks(rest)

    def reach_of(cum_block, rest_block):
        return (
            jnp.exp((cum_end[:, None, None, :] - cum_block[:, :, None, :]) * a_neg)
            * rest_block[:, :, None, None]
        )

    def kept_back(carry, piece):
        carry_in, a_acc, q_acc = carry
        core_piece = piece[:7]
        carry_out, weighted, stepped, terms = back_core(carry_in, core_piece)
        dt_block = core_piece[0]
        along = stepped * reach_of(piece[7], piece[8])
        a_acc = a_acc + jnp.sum(weighted * dt_block[:, :, None, :], axis=(0, 1))
        q_acc = q_acc + jnp.sum(along * dt_block[:, :, None, :], axis=1)
        return ((carry_out, a_acc, q_acc), terms + (along,))

    (edge_grad, a_local, q_total), (base_dt, base_act, base_b, grad_c_blocks, along_blocks) = (
        lax.scan(
            kept_back,
            (zero_state, zero_acc, zero_state),
            back_pieces + (cum_blocks, rest_blocks),
            reverse=True,
        )
    )
    _, after_grad = entering((through, edge_grad), "ctx", link, (one_state, zero_state), True)

    def adjust(piece):
        dt_block, act_block, b_block, cum_block, rest_block, along = piece
        extra = reach_of(cum_block, rest_block) * after_grad[:, None]
        along_b = jnp.sum(extra * b_block[:, :, :, None], axis=2)
        grad_dt = jnp.sum(along * after_grad[:, None] * a_neg, axis=2) + along_b * act_block
        grad_act = along_b * dt_block
        grad_b = jnp.sum(extra * (dt_block * act_block)[:, :, None, :], axis=3)
        return (grad_dt, grad_act, grad_b)

    add_dt, add_act, add_b = lax.map(
        adjust, (dt_blocks, act_blocks, b_blocks, cum_blocks, rest_blocks, along_blocks)
    )
    grad_dt_blocks = base_dt + add_dt
    grad_act_blocks = base_act + add_act
    grad_b_blocks = base_b + add_b
    a_total = a_local + jnp.sum(q_total * after_grad, axis=0)
    grad_lin = from_blocks(grad_dt_blocks) * jax.nn.sigmoid(dt_arg)
    grad_dtb = jnp.sum(grad_lin, axis=(0, 1))
    grad_lin_low = grad_lin.reshape(row_count, channels).astype(jnp.bfloat16)
    grad_dtw = jnp.einsum("rk,rc->kc", low_rank, grad_lin_low, preferred_element_type=jnp.float32)
    grad_rank = jnp.einsum("rc,kc->rk", grad_lin_low, dtw_full, preferred_element_type=jnp.float32)
    grad_mixed_part = jnp.concatenate(
        [
            grad_rank,
            from_blocks(grad_b_blocks).reshape(row_count, states),
            from_blocks(grad_c_blocks).reshape(row_count, states),
        ],
        axis=1,
    )
    grad_mixed = lax.psum(grad_mixed_part, "tp").astype(jnp.bfloat16)
    grad_xproj = jnp.einsum("rw,rc->wc", grad_mixed, act_flat, preferred_element_type=jnp.float32)
    grad_act_total = (
        grad_y * skip_vec
        + from_blocks(grad_act_blocks)
        + jnp.dot(grad_mixed, xproj_full, preferred_element_type=jnp.float32).reshape(
            seq_count, tok_count, channels
        )
    )
    grad_pre = grad_act_total * silu_slope(pre)
    grad_convb = jnp.sum(grad_pre, axis=(0, 1))
    tap_grads = [None] * kernel
    grad_inner = jnp.zeros((seq_count, tok_count, channels), jnp.float32)
    tail_grad = jnp.zeros((seq_count, conv_lag, channels), jnp.float32)
    for offset in range(kernel):
        weighted_pre = grad_pre * same_list[offset][:, :, None]
        tap_grads[conv_lag - offset] = jnp.sum(weighted_pre * windows[offset], axis=(0, 1))
        scaled_pre = weighted_pre * conv_taps[conv_lag - offset]
        if offset == 0:
            grad_inner = grad_inner + scaled_pre
        else:
            grad_inner = grad_inner + jnp.concatenate(
                [scaled_pre[:, offset:], jnp.zeros((seq_count, offset, channels), jnp.float32)],
                axis=1,
            )
            tail_grad = tail_grad.at[:, conv_lag - offset :].add(scaled_pre[:, :offset])
    grad_convw = jnp.stack(tap_grads)
    sent_back = from_behind(tail_grad, "ctx", -1)
    grad_inner = grad_inner.at[:, tok_count - conv_lag :].add(sent_back)
    grad_proj = jnp.stack(
        [
            grad_inner.astype(jnp.bfloat16).reshape(row_count, channels),
            grad_gate.reshape(row_count, channels),
        ]
    )
    grad_win = jnp.einsum("rd,krc->kdc", normed_flat, grad_proj, preferred_element_type=jnp.float32)
    grad_norm_part = jnp.einsum(
        "krc,kdc->rd", grad_proj, win_full, preferred_element_type=jnp.float32
    )
    grad_norm = lax.psum(grad_norm_part, "tp").reshape(seq_count, tok_count, model_width)
    grad_gain = jnp.sum(grad_norm * stream * rstd, axis=(0, 1))
    scaled = grad_norm * gain_vec
    stream_grad = (
        out_grad.astype(jnp.float32)
        + rstd * scaled
        - stream * (rstd * rstd * rstd) * jnp.mean(scaled * stream, axis=2, keepdims=True)
    )
    grad_alog = a_total * a_neg
    local_grads = (
        grad_gain,
        grad_win,
        grad_wout,
        grad_xproj,
        grad_dtw,
        grad_alog,
        grad_convw.reshape(kernel, 1, channels),
        grad_convb.reshape(1, channels),
        grad_dtb.reshape(1, channels),
        grad_skip.reshape(1, channels),
    )
    summed = lax.psum(
        (
            local_grads[0],
            local_grads[1],
            local_grads[2],
            local_grads[3],
            local_grads[4],
            local_grads[5],
            local_grads[6],
            local_grads[7],
            local_grads[8],
            local_grads[9],
        ),
        "ctx",
    )
    owned = (
        lax.psum_scatter(summed[0], "dp", scatter_dimension=0, tiled=True),
        lax.psum_scatter(summed[1], "dp", scatter_dimension=1, tiled=True),
        lax.psum_scatter(summed[2], "dp", scatter_dimension=1, tiled=True),
        lax.psum_scatter(summed[3], "dp", scatter_dimension=0, tiled=True),
        lax.psum_scatter(summed[4], "dp", scatter_dimension=0, tiled=True),
        lax.psum_scatter(summed[5], "dp", scatter_dimension=0, tiled=True),
        lax.psum_scatter(summed[6], "dp", scatter_dimension=2, tiled=True),
        lax.psum_scatter(summed[7], "dp", scatter_dimension=1, tiled=True),
        lax.psum_scatter(summed[8], "dp", scatter_dimension=1, tiled=True),
        lax.psum_scatter(summed[9], "dp", scatter_dimension=1, tiled=True),
    )
    return (
        stream_out,
        stream_grad,
        owned[0],
        owned[1],
        owned[2],
        owned[3],
        owned[4],
        owned[5],
        owned[6],
        owned[7],
        owned[8],
        owned[9],
    )


F32 = jnp.float32
BF16 = jnp.bfloat16
MESH = pl.DeviceIdType.MESH
LOG2E = math.log2(math.e)
LN2 = math.log(2.0)
KILL = 1e30
SUB = 8
LANES = 128
PAD = 24
ROWS = 64
XP, DTW, ALOG, CONVW, CONVB, DTB, SKIP, GAIN = 0, 24, 40, 44, 48, 49, 50, 51
NT = (((1,), (1,)), ((), ()))
TN = (((0,), (0,)), ((), ()))


def dot(a, b):
    return jnp.dot(a, b, preferred_element_type=F32)


def dot_nt(a, b):
    return lax.dot_general(a, b, NT, preferred_element_type=F32)


def dot_tn(a, b):
    return lax.dot_general(a, b, TN, preferred_element_type=F32)


def at8(start, size):
    return pl.ds(pl.multiple_of(start, 8), size)


def one_less_exp(v):
    series = v * (1.0 - v * (0.5 - v * (1.0 / 6.0 - v * (1.0 / 24.0 - v * (1.0 / 120.0)))))
    return jnp.where(v < 0.1, series, 1.0 - jnp.exp(-v))


def prefix_of(ends, prods):
    row = lax.broadcasted_iota(jnp.int32, ends.shape, 0)
    for gap in (1, 2, 4):
        ok = row >= gap
        ends = ends + prods * jnp.where(ok, pltpu.roll(ends, gap, 0), 0.0)
        prods = prods * jnp.where(ok, pltpu.roll(prods, gap, 0), 1.0)
    return jnp.where(row >= 1, pltpu.roll(ends, 1, 0), 0.0)


def suffix_of(ends, prods):
    row = lax.broadcasted_iota(jnp.int32, ends.shape, 0)
    for gap in (1, 2, 4):
        ok = row < SUB - gap
        ends = ends + prods * jnp.where(ok, pltpu.roll(ends, SUB - gap, 0), 0.0)
        prods = prods * jnp.where(ok, pltpu.roll(prods, SUB - gap, 0), 1.0)
    return jnp.where(row < SUB - 1, pltpu.roll(ends, SUB - 1, 0), 0.0)


def fused_kernel(
    x_ref, og_ref, win_ref, wout_ref, xproj_ref, dtw_ref, alog_ref, convw_ref, convb_ref, dtb_ref,
    skip_ref, gain_ref, seg_ref, mask_ref,
    so_out, sg_out, wg_out, wo_out, sm_out, cv_out, gg_out,
    xf, mg, w_s, wo_s, pk_f, pk_s, segs, segp, maskc, nat, inner, slope, act, gate, dt, yg, y,
    bc, h, a2b, st, gin, cum, alg, full, full2, mp, sum_a, recv_a, recv_b, xp, dtwp,
    big_send, big_keep, big_recv, big_rb, gpart, zrecv, gres, gnat, znat, spart, srecv, sfull, sown, ggs,
    sg_s, ssem, rsem, lsem,
):
    z, c, k = lax.axis_index("dp"), lax.axis_index("ctx"), lax.axis_index("tp")
    nz = lax.axis_size("dp")
    px, py = lax.rem(c, 2), c // 2
    sib = (z, c, 1 - k)
    plane = [None, py * 2 + (1 - px), (1 - py) * 2 + px, (1 - py) * 2 + (1 - px)]
    peers = [None] + [(z, plane[p], k) for p in (1, 2, 3)]
    toward = [None] + [lax.rem(z + d, nz) for d in (1, 2, 3)]
    behind = [None] + [lax.rem(z + nz - d, nz) for d in (1, 2, 3)]
    lines = [None] + [(toward[d], c, k) for d in (1, 2, 3)]
    count = [0]
    local_count = [0]
    pending = []

    def send(src, dst, device):
        i = count[0]
        count[0] += 1
        copy = pltpu.make_async_remote_copy(
            src_ref=src, dst_ref=dst, send_sem=ssem.at[i], recv_sem=rsem.at[i],
            device_id=device, device_id_type=MESH,
        )
        copy.start()
        pending.append(copy)
        return copy

    def local(src, dst):
        i = local_count[0]
        local_count[0] += 1
        copy = pltpu.make_async_copy(src, dst, lsem.at[i])
        copy.start()
        return copy

    def flush(copies):
        for copy in copies:
            copy.wait_send()
            pending[:] = [other for other in pending if other is not copy]

    tok = x_ref.shape[0]
    half = tok // 2
    total = xf.shape[0]
    width = xf.shape[1]
    steps = total // SUB
    states = h.shape[1]
    wide = 2 * LANES
    block = w_s.shape[1] // 4
    tiles = (0, 1)
    rb = 128
    nblk = total // rb

    def lanes(t):
        return slice(t * LANES, (t + 1) * LANES)

    def blk(i):
        return pl.ds(pl.multiple_of(i * rb, rb), rb)

    def tau_rows(tau):
        return at8(tau * SUB, SUB)

    def loop(n, body, unroll=1):
        def step(i, carry):
            body(i)
            return carry

        lax.fori_loop(0, n, step, 0, unroll=unroll)

    barrier = pltpu.get_barrier_semaphore()
    everyone = [sib] + peers[1:] + [(z, plane[p], 1 - k) for p in (1, 2, 3)] + lines[1:]
    for device in everyone:
        pl.semaphore_signal(barrier, inc=1, device_id=device, device_id_type=MESH)
    chans = pl.ds(pl.multiple_of(c * wide, wide), wide)
    spart[...] = jnp.zeros_like(spart)
    spart[0, XP : XP + 24, :] = xproj_ref[:, chans].astype(F32)
    spart[0, DTW : DTW + 16, :] = dtw_ref[:, chans].astype(F32)
    spart[0, ALOG : ALOG + 4, :] = alog_ref[:, chans].astype(F32)
    spart[0, CONVW : CONVW + 4, :] = convw_ref[...].astype(F32)
    spart[0, CONVB : CONVB + 1, :] = convb_ref[...].astype(F32)
    spart[0, DTB : DTB + 1, :] = dtb_ref[...].astype(F32)
    spart[0, SKIP : SKIP + 1, :] = skip_ref[...].astype(F32)
    spart[0, GAIN : GAIN + 1, :] = gain_ref[...].astype(F32)
    pk_s[z] = spart[0].astype(BF16)
    segs[c] = jnp.broadcast_to(seg_ref[...], (SUB, tok))
    pl.semaphore_wait(barrier, len(everyone))

    s_pack = [send(pk_s.at[z], pk_s.at[z], lines[d]) for d in (1, 2, 3)]
    s_seg = [send(segs.at[c], segs.at[c], peers[p]) for p in (1, 2, 3)]
    my_half = pl.ds(pl.multiple_of(c * tok + k * half, half), half)
    s_x = [send(x_ref.at[pl.ds(pl.multiple_of(k * half, half), half)], xf.at[my_half], peers[p]) for p in (3, 1, 2)]

    zrows = pl.ds(pl.multiple_of(z * block, block), block)

    def weight(which):
        return [
            send(win_ref.at[which, :, chans], w_s.at[which, zrows, :], lines[d]) for d in (1, 2, 3)
        ]

    s_wx = weight(0)
    own_w = [local(win_ref.at[i, :, chans], w_s.at[i, zrows, :]) for i in (0, 1)]
    zcols = pl.ds(pl.multiple_of(z * block, block), block)
    own_wo = local(wout_ref.at[chans, :], wo_s.at[:, zcols])

    own_rows = pl.ds(pl.multiple_of(c * tok, tok), tok)
    xf[own_rows, :] = x_ref[...]
    mrow = mask_ref[...].astype(F32)
    for b in range(tok // LANES):
        rows = slice(b * LANES, (b + 1) * LANES)
        maskc[rows, :] = jnp.broadcast_to(mrow[:, rows], (LANES, LANES)).T
    mcol = jnp.concatenate([maskc[...]] * (width // LANES), axis=1)
    mg[own_rows, :] = (og_ref[...].astype(F32) * mcol).astype(BF16)

    def halves(copies, buf):
        relays = []
        for copy, p in zip(copies, (3, 1, 2)):
            copy.wait_recv()
            rows = pl.ds(pl.multiple_of(plane[p] * tok + k * half, half), half)
            relays.append(send(buf.at[rows], buf.at[rows], sib))
        return relays

    r_x = halves(s_x, xf)
    s_mg = [send(mg.at[my_half], mg.at[my_half], peers[p]) for p in (3, 1, 2)]

    for copy in s_pack:
        copy.wait_recv()
    for i in range(4):
        pk_f[i] = pk_s[i].astype(F32)
    for i in range(4):
        alg[4 * i : 4 * i + 4, :] = pk_f[i, ALOG : ALOG + 4, :]
    xp_rows = jnp.concatenate([pk_f[i, XP : XP + 24, :] for i in range(4)] + [jnp.zeros((32, wide), F32)], axis=0)
    xp[...] = xp_rows.astype(BF16)
    dt_rows = jnp.concatenate([pk_f[i, DTW : DTW + 16, :] for i in range(4)] + [jnp.zeros((64, wide), F32)], axis=0)
    dtwp[...] = dt_rows.astype(BF16)
    a2v = -jnp.exp(alg[...]) * LOG2E
    for n in range(states):
        for t in tiles:
            a2b[t, n] = jnp.broadcast_to(a2v[n : n + 1, lanes(t)], (SUB, LANES))
    gain_row = jnp.concatenate([pk_f[i, GAIN : GAIN + 1, :] for i in range(4)], axis=1)
    sown[...] = pk_f[c]

    def param(row, t):
        return sown[row : row + 1, lanes(t)]

    for copy in s_seg:
        copy.wait_recv()
    for i in range(4):
        srow = segs[i, 0:1, :].astype(F32)
        for b in range(tok // LANES):
            rows = slice(b * LANES, (b + 1) * LANES)
            nat[0, i * tok + b * LANES : i * tok + (b + 1) * LANES, :] = jnp.broadcast_to(
                srow[:, rows], (LANES, LANES)
            ).T

    def seg_in(tau):
        segp[at8(PAD + tau * SUB, SUB), :] = nat[0, pl.ds(tau, SUB, stride=steps), :]

    loop(steps, seg_in, 8)
    sub_row = lax.broadcasted_iota(jnp.int32, (SUB, LANES), 0)

    def from_before(v, fill):
        return jnp.where(sub_row >= 1, pltpu.roll(v, 1, 0), fill)

    def from_after(v, fill):
        return jnp.where(sub_row < SUB - 1, pltpu.roll(v, SUB - 1, 0), fill)

    for j in range(3):
        segp[j * SUB : (j + 1) * SUB, :] = from_before(segp[total + j * SUB : total + (j + 1) * SUB, :], -1.0)
        segp[PAD + total + j * SUB : PAD + total + (j + 1) * SUB, :] = from_after(
            segp[PAD + j * SUB : PAD + (j + 1) * SUB, :], -2.0
        )

    for copy in r_x:
        copy.wait_recv()

    def norm(i):
        v = xf[blk(i), :].astype(F32)
        r = lax.rsqrt(jnp.mean(v * v, axis=1, keepdims=True) + EPS)
        xf[blk(i), :] = (v * r * gain_row).astype(BF16)

    flush(s_x + r_x)
    loop(nblk, norm)

    def project(which, dst, off):
        def body(i):
            v = dot(xf[blk(i), :], w_s[which]).astype(BF16).astype(F32)
            for t in tiles:
                nat[t, blk(i), :] = v[:, lanes(t)]

        loop(nblk, body)
        permute_in(dst, off)

    def permute_in(dst, off):
        def body(tau):
            for t in tiles:
                dst[t, at8(off + tau * SUB, SUB), :] = nat[t, pl.ds(tau, SUB, stride=steps), :]

        loop(steps, body, 8)

    def permute_out(src, dst):
        def body(i):
            for s in range(SUB):
                for t in tiles:
                    nat[t, at8(s * steps + i * SUB, SUB), :] = src[t, pl.ds(i * SUB * SUB + s, SUB, stride=SUB), :]

        loop(steps // SUB, body)

        def cast(i):
            dst[blk(i), :] = jnp.concatenate([nat[t, blk(i), :] for t in tiles], axis=1).astype(BF16)

        loop(nblk, cast)

    for copy in s_wx:
        copy.wait_recv()
    own_w[0].wait()
    s_wz = weight(1)
    project(0, inner, PAD)
    for t in tiles:
        for j in range(3):
            inner[t, j * SUB : (j + 1) * SUB, :] = from_before(inner[t, total + j * SUB : total + (j + 1) * SUB, :], 0.0)

    def conv(i):
        for t in tiles:
            mine = segp[at8(PAD + i * rb, rb), :]
            pre = jnp.zeros((rb, LANES), F32) + param(CONVB, t)
            for j in range(4):
                window = inner[t, at8(PAD + i * rb - j * SUB, rb), :]
                if j:
                    window = jnp.where(segp[at8(PAD + i * rb - j * SUB, rb), :] == mine, window, 0.0)
                pre = pre + param(CONVW + 3 - j, t) * window
            s = jax.nn.sigmoid(pre)
            act[t, blk(i), :] = (pre * s).astype(BF16).astype(F32)
            slope[t, blk(i), :] = s * (1.0 + pre * (1.0 - s))

    loop(nblk, conv)

    def tiles_bf(ref, i):
        return jnp.concatenate([ref[t, blk(i), :] for t in tiles], axis=1).astype(BF16)

    def mix(i):
        mp[i] = dot_nt(tiles_bf(act, i), xp[...])

    loop(nblk, mix)

    def plane_sum(out, between):
        first = send(mp.at[pl.ds((1 - k) * 4, 4)], recv_a, sib)
        between[0]()
        first.wait_recv()
        for i in range(4):
            sum_a[i] = mp[k * 4 + i] + recv_a[i]
        second = [send(sum_a.at[plane[p]], recv_b.at[p - 1], peers[p]) for p in (3, 1, 2)]
        between[1]()
        for copy in second:
            copy.wait_recv()
        mine = k * 4 + c
        out[mine] = sum_a[c] + recv_b[0] + recv_b[1] + recv_b[2]
        third = [send(out.at[mine], out.at[mine], peers[p]) for p in (3, 1, 2)]
        third.append(send(out.at[mine], out.at[mine], sib))
        between[2]()
        fourth = []
        for copy, p in zip(third, (3, 1, 2)):
            copy.wait_recv()
            there = k * 4 + plane[p]
            fourth.append(send(out.at[there], out.at[there], sib))
        between[3]()
        for copy in [third[3]] + fourth:
            copy.wait_recv()
        flush([first] + second + third + fourth)

    late = {}
    mm = gnat

    def gates():
        for copy in s_wz:
            copy.wait_recv()
        own_w[1].wait()
        late["wo"] = [send(wout_ref.at[chans, :], wo_s.at[:, zcols], lines[d]) for d in (1, 2, 3)]
        project(1, gate, 0)

    def nothing():
        pass

    def relay_mg():
        late["mg"] = halves(s_mg, mg)

    plane_sum(full, [nothing, relay_mg, gates, nothing])

    def steps_of(i):
        arg = dot(full[i].astype(BF16), dtwp[...])
        for t in tiles:
            v = arg[:, lanes(t)] + param(DTB, t)
            dt[t, blk(i), :] = jnp.maximum(v, 0.0) + jnp.log1p(jnp.exp(-jnp.abs(v)))
        hi = full[i].astype(BF16)
        lo = (full[i] - hi.astype(F32)).astype(BF16)
        mm[blk(i), :] = jnp.concatenate([hi, lo], axis=1)

    loop(nblk, steps_of)

    def spread(g):
        row = lax.rem(lax.broadcasted_iota(jnp.int32, (wide, 4 * LANES), 0), LANES)
        col = lax.broadcasted_iota(jnp.int32, (wide, 4 * LANES), 1) // LANES
        pick = jnp.where(row == 64 + g * 4 + col, 1.0, 0.0).astype(BF16)
        for i in range(total // 256):
            v = dot(mm[i * 256 : (i + 1) * 256, :], pick)
            for q in range(4):
                bc[g * 4 + q, i * 256 : (i + 1) * 256, :] = v[:, lanes(q)]

    loop(2 * states // 4, spread)

    def dts(t, tau):
        v = dt[t, tau_rows(tau), :]
        r = at8(PAD + tau * SUB, SUB)
        p = at8(PAD + tau * SUB - SUB, SUB)
        return v, jnp.where(segp[r, :] == segp[p, :], v, KILL)

    for t in tiles:

        def ends(tau, carry, t=t):
            v, killed = dts(t, tau)
            drive = v * act[t, tau_rows(tau), :]
            new = [
                carry[n] * jnp.exp2(killed * a2b[t, n]) + drive * bc[n, tau_rows(tau), :] for n in range(states)
            ]
            return tuple(new) + (carry[states] + killed,)

        zero = jnp.zeros((SUB, LANES), F32)
        got = lax.fori_loop(0, steps, ends, (zero,) * (states + 1), unroll=4)
        cum[t] = got[states]
        for n in range(states):
            st[t, n] = prefix_of(got[n], jnp.exp2(got[states] * a2b[t, n]))

    for t in tiles:
        for n in range(states):
            h[t, n, 0:SUB, :] = st[t, n]

        def forward(tau, carry, t=t):
            v, killed = dts(t, tau)
            drive = v * act[t, tau_rows(tau), :]
            new, parts = [], [None] * 4
            for n in range(states):
                s = carry[n] * jnp.exp2(killed * a2b[t, n]) + drive * bc[n, tau_rows(tau), :]
                h[t, n, at8(tau * SUB + SUB, SUB), :] = s
                o = s * bc[states + n, tau_rows(tau), :]
                parts[n % 4] = o if parts[n % 4] is None else parts[n % 4] + o
                new.append(s)
            y[t, tau_rows(tau), :] = (parts[0] + parts[1]) + (parts[2] + parts[3])
            return tuple(new)

        lax.fori_loop(0, steps, forward, tuple(st[t, n] for n in range(states)), unroll=4)

    for copy in late["mg"] + late["wo"]:
        copy.wait_recv()
    own_wo.wait()

    def ograd(i):
        v = dot_nt(mg[blk(i), :], wo_s[...])
        for t in tiles:
            nat[t, blk(i), :] = v[:, lanes(t)]

    loop(nblk, ograd)
    gb = SUB * SUB

    def strided(t, i):
        return jnp.concatenate([nat[t, pl.ds(i * SUB + u, SUB, stride=steps), :] for u in range(SUB)], axis=0)

    def gating(i, carry):
        new = []
        rows = pl.ds(pl.multiple_of(i * gb, gb), gb)
        for t in tiles:
            gv, ov, av = gate[t, rows, :], strided(t, i), act[t, rows, :]
            s = jax.nn.sigmoid(gv)
            ytot = y[t, rows, :] + param(SKIP, t) * av
            gy = ov * (gv * s)
            yg[t, rows, :] = gy
            y[t, rows, :] = ytot * (gv * s)
            gate[t, rows, :] = ov * ytot * (s * (1.0 + gv * (1.0 - s)))
            new.append(carry[t] + jnp.sum((gy * av).reshape(SUB, SUB, LANES), axis=0))
        return tuple(new)

    zero = jnp.zeros((SUB, LANES), F32)
    skip_sum = lax.fori_loop(0, total // gb, gating, (zero, zero))
    permute_out(y, gnat)
    permute_out(gate, znat)

    def owner_rows(i, q):
        return pl.ds(pl.multiple_of(i * tok + q * half, half), half)

    def start_rows(partial):
        def other(i):
            big_send[i] = partial(owner_rows(i, 1 - k)).astype(BF16)

        loop(4, other)
        first = send(big_send, big_recv, sib)

        def mine(i):
            big_keep[i] = partial(owner_rows(i, k)).astype(BF16)

        loop(4, mine)
        return first

    def middle_rows(first):
        first.wait_recv()

        def add(i):
            big_keep[i] = (big_keep[i].astype(F32) + big_recv[i].astype(F32)).astype(BF16)

        loop(4, add)
        return [send(big_keep.at[plane[p]], big_rb.at[p - 1], peers[p]) for p in (3, 1, 2)]

    def end_rows(second):
        for copy in second:
            copy.wait_recv()
        v = big_keep[c].astype(F32)
        for p in range(3):
            v = v + big_rb[p].astype(F32)
        return v

    branch_a = start_rows(lambda r: dot(gnat[r, :], wo_s[...]))

    def weight_grad(slot, left, right):
        gpart[slot % 2] = dot_tn(left[...], right[...]).astype(BF16)
        return [
            send(
                gpart.at[slot % 2, :, pl.ds(pl.multiple_of(toward[d] * block, block), block)],
                zrecv.at[slot, d - 1],
                lines[d],
            )
            for d in (1, 2, 3)
        ]

    def owned_grad(slot, copies):
        for copy in copies:
            copy.wait_recv()
        v = gpart[slot % 2, :, zcols].astype(F32)
        for d in range(3):
            v = v + zrecv[slot, d].astype(F32)
        return v

    def share(slot, dst):
        return [local(gres.at[slot], dst)] + [send(gres.at[slot], dst, peers[p]) for p in (3, 1, 2)]

    z_wo = weight_grad(2, gnat, mg)
    z_wz = weight_grad(1, znat, xf)

    for t in tiles:

        def back_ends(i, carry, t=t):
            tau = steps - 1 - i
            _, killed = dts(t, tau)
            gy = yg[t, tau_rows(tau), :]
            return tuple(
                (carry[n] + gy * bc[states + n, tau_rows(tau), :]) * jnp.exp2(killed * a2b[t, n])
                for n in range(states)
            )

        got = lax.fori_loop(0, steps, back_ends, (zero,) * states, unroll=4)
        for n in range(states):
            gin[t, n] = suffix_of(got[n], jnp.exp2(cum[t] * a2b[t, n]))

    branch_b = middle_rows(branch_a)
    flush([branch_a])
    so_s = big_send.at[0]

    gsum, dsum = gate, y
    part = states // 2
    for lo in (0, part):
        names = list(range(lo, lo + part))

        def back(i, carry, names=names, lo=lo):
            grads, acc = carry
            tau = steps - 1 - i
            r = tau_rows(tau)
            pair = [dts(t, tau) for t in tiles]
            drive = [pair[t][0] * act[t, r, :] for t in tiles]
            gy = [yg[t, r, :] for t in tiles]
            along = [None, None]
            down = [None, None]
            new_g, new_a = [], []
            for q, n in enumerate(names):
                bv, cv = bc[n, r, :], bc[states + n, r, :]
                pb = pc = None
                for t in tiles:
                    a2 = a2b[t, n]
                    decay = jnp.exp2(pair[t][1] * a2)
                    g = grads[2 * q + t] + gy[t] * cv
                    gb = g * bv
                    along[t] = gb if along[t] is None else along[t] + gb
                    v = g * drive[t]
                    pb = v if pb is None else pb + v
                    v = gy[t] * h[t, n, at8(tau * SUB + SUB, SUB), :]
                    pc = v if pc is None else pc + v
                    gd = g * decay
                    dla = gd * h[t, n, r, :]
                    v = dla * a2
                    down[t] = v if down[t] is None else down[t] + v
                    new_a.append(acc[2 * q + t] + dla * pair[t][0])
                    new_g.append(gd)
                bc[n, r, :] = pb
                bc[states + n, r, :] = pc
            for t in tiles:
                if lo == 0:
                    gsum[t, r, :] = along[t]
                    dsum[t, r, :] = down[t]
                else:
                    gsum[t, r, :] = gsum[t, r, :] + along[t]
                    dsum[t, r, :] = dsum[t, r, :] + down[t]
            return tuple(new_g), tuple(new_a)

        start = tuple(gin[t, n] for n in names for t in tiles)
        _, acc = lax.fori_loop(0, steps, back, (start, (zero,) * (2 * part)), unroll=2)
        for q, n in enumerate(names):
            for t in tiles:
                alg[n : n + 1, lanes(t)] = (
                    jnp.sum(acc[2 * q + t], axis=0, keepdims=True) * a2b[t, n][0:1, :] * LN2
                )

    def lin(i, carry):
        new = []
        rank = []
        for t in tiles:
            av, gv = act[t, blk(i), :], gsum[t, blk(i), :]
            v = (dsum[t, blk(i), :] * LN2 + av * gv) * one_less_exp(dt[t, blk(i), :])
            new.append(carry[t] + jnp.sum(v.reshape(rb // SUB, SUB, LANES), axis=0))
            low = v.astype(BF16)
            rank.append(low)
            dsum[t, blk(i), :] = low.astype(F32)
            gsum[t, blk(i), :] = dt[t, blk(i), :] * gv + param(SKIP, t) * yg[t, blk(i), :]
        mp[i] = dot_nt(jnp.concatenate(rank, axis=1), dtwp[...])
        return tuple(new)

    dtb_sum = lax.fori_loop(0, nblk, lin, (zero, zero))

    def collect(i):
        v = mp[i]
        for n in range(0, 2 * states, 2):
            row = lax.broadcasted_iota(jnp.int32, (wide, LANES), 0) // LANES
            col = lax.broadcasted_iota(jnp.int32, (wide, LANES), 1)
            pick = jnp.where(col == 64 + n + row, 1.0, 0.0).astype(BF16)
            pair = jnp.concatenate([bc[n, blk(i), :], bc[n + 1, blk(i), :]], axis=1).astype(BF16)
            v = v + dot(pair, pick)
        mp[i] = v

    loop(nblk, collect)

    def finish_early():
        v = end_rows(branch_b)
        rows = pl.ds(pl.multiple_of(k * half, half), half)
        mk = jnp.concatenate([maskc[rows, :]] * (width // LANES), axis=1)
        so_s[...] = (x_ref[rows, :].astype(F32) + mk * v).astype(BF16)
        late["so"] = [local(so_s, so_out.at[rows, :]), send(so_s, so_out.at[rows, :], sib)]
        v = owned_grad(2, z_wo)
        gres[2] = v.astype(BF16)
        late["gwo"] = share(2, wo_out.at[chans, :])

    def finish_wz():
        v = owned_grad(1, z_wz).T
        gres[1] = v.astype(BF16)
        late["gwz"] = share(1, wg_out.at[1, :, chans])
        late["gain"] = v * w_s[1, zrows, :].astype(F32)

    def dtw_grad():
        low = jnp.concatenate([full[i].astype(BF16) for i in range(nblk)], axis=0)
        linv = jnp.concatenate([tiles_bf(dsum, i) for i in range(nblk)], axis=0)
        g = dot_tn(low, linv)
        for i in range(4):
            spart[i, DTW : DTW + 16, :] = g[i * 16 : i * 16 + 16, :]

    plane_sum(full2, [dtw_grad, finish_early, finish_wz, nothing])

    pg = slope

    def pre_grad(i, carry):
        mixg = full2[i].astype(BF16)
        back_x = dot(mixg, xp[...])
        new = []
        for t in tiles:
            v = (gsum[t, blk(i), :] + back_x[:, lanes(t)]) * pg[t, blk(i), :]
            pg[t, blk(i), :] = v
            mine = segp[at8(PAD + i * rb, rb), :]
            new.append(carry[5 * t] + jnp.sum(v.reshape(rb // SUB, SUB, LANES), axis=0))
            for j in range(4):
                window = inner[t, at8(PAD + i * rb - j * SUB, rb), :]
                if j:
                    window = jnp.where(segp[at8(PAD + i * rb - j * SUB, rb), :] == mine, window, 0.0)
                new.append(carry[5 * t + 1 + j] + jnp.sum((v * window).reshape(rb // SUB, SUB, LANES), axis=0))
        return tuple(new)

    conv_sum = lax.fori_loop(0, nblk, pre_grad, (zero,) * 10)
    for t in tiles:
        for j in range(3):
            pg[t, total + j * SUB : total + (j + 1) * SUB, :] = from_after(pg[t, j * SUB : (j + 1) * SUB, :], 0.0)

    def inner_grad(i):
        for t in tiles:
            mine = segp[at8(PAD + i * rb, rb), :]
            v = pg[t, blk(i), :] * param(CONVW + 3, t)
            for j in range(1, 4):
                later = pg[t, at8(i * rb + j * SUB, rb), :]
                same = segp[at8(PAD + i * rb + j * SUB, rb), :] == mine
                v = v + jnp.where(same, later, 0.0) * param(CONVW + 3 - j, t)
            dsum[t, blk(i), :] = v

    loop(nblk, inner_grad)
    permute_out(dsum, gnat)
    flush(z_wo)
    z_wx = weight_grad(0, gnat, xf)

    flush(late["so"][1:] + branch_b)
    late["so"][0].wait()
    norm_a = start_rows(lambda r: dot_nt(gnat[r, :], w_s[0]) + dot_nt(znat[r, :], w_s[1]))

    mixv = jnp.concatenate([full2[i].astype(BF16) for i in range(nblk)], axis=0)
    actv = jnp.concatenate([tiles_bf(act, i) for i in range(nblk)], axis=0)
    gx = dot_tn(mixv, actv)
    for i in range(4):
        spart[i, XP : XP + 24, :] = gx[i * 24 : i * 24 + 24, :]
        spart[i, ALOG : ALOG + 4, :] = alg[i * 4 : i * 4 + 4, :]
        for t in tiles:
            for j in range(4):
                spart[i, CONVW + 3 - j : CONVW + 4 - j, lanes(t)] = jnp.sum(
                    conv_sum[5 * t + 1 + j], axis=0, keepdims=True
                )
            spart[i, CONVB : CONVB + 1, lanes(t)] = jnp.sum(conv_sum[5 * t], axis=0, keepdims=True)
            spart[i, DTB : DTB + 1, lanes(t)] = jnp.sum(dtb_sum[t], axis=0, keepdims=True)
            spart[i, SKIP : SKIP + 1, lanes(t)] = jnp.sum(skip_sum[t], axis=0, keepdims=True)
    z_small = [send(spart.at[toward[d]], srecv.at[d - 1], lines[d]) for d in (1, 2, 3)]

    norm_b = middle_rows(norm_a)

    for copy in z_small:
        copy.wait_recv()
    sfull[c] = spart[z] + srecv[0] + srecv[1] + srecv[2]
    g_small = [send(sfull.at[c], sfull.at[c], peers[p]) for p in (3, 1, 2)]

    v = owned_grad(0, z_wx).T
    gres[0] = v.astype(BF16)
    late["gwx"] = share(0, wg_out.at[0, :, chans])
    v = late["gain"] + v * w_s[0, zrows, :].astype(F32)
    v = v[:, :LANES] + v[:, LANES:]
    for b in range(block // LANES):
        col = v[b * LANES : (b + 1) * LANES, :].T
        ggs[0, :, lanes(b)] = jnp.broadcast_to(jnp.sum(col, axis=0, keepdims=True), (SUB, LANES))
    s_gain = [send(ggs.at[0], ggs.at[p], peers[p]) for p in (1, 2, 3)]
    s_gain += [send(ggs.at[0], ggs.at[3 + p], (z, plane[p], 1 - k)) for p in (1, 2, 3)]
    s_gain.append(send(ggs.at[0], ggs.at[7], sib))

    ng = end_rows(norm_b)
    rows = pl.ds(pl.multiple_of(k * half, half), half)
    xv = x_ref[rows, :].astype(F32)
    r = lax.rsqrt(jnp.mean(xv * xv, axis=1, keepdims=True) + EPS)
    sg = ng * gain_row
    sg_s[...] = (
        og_ref[rows, :].astype(F32) + r * sg - xv * (r * r * r) * jnp.mean(sg * xv, axis=1, keepdims=True)
    )
    last = [local(sg_s, sg_out.at[rows, :]), send(sg_s, sg_out.at[rows, :], sib)]

    for copy in g_small:
        copy.wait_recv()
    for i in range(4):
        sm_out[:, i * wide : (i + 1) * wide] = sfull[i]
    cv_out[...] = sfull[z, CONVW : CONVW + 8, :]
    for copy in s_gain:
        copy.wait_recv()
    v = ggs[0]
    for i in range(1, 8):
        v = v + ggs[i]
    gg_out[...] = v[0:1, :] / gain_ref[...].astype(F32)

    late["so"][1].wait_recv()
    for name in ("gwo", "gwz", "gwx"):
        late[name][0].wait()
        for copy in late[name][1:]:
            copy.wait_recv()
    last[0].wait()
    last[1].wait_recv()
    flush(list(pending))


def fused(
    stream_in, norm_gain, in_weight, out_weight, xproj_weight, dt_weight, a_log, convolution_weight,
    convolution_bias, step_size_bias, skip_term_scale, seg_ids, pad_mask, out_grad,
):
    _, tok, width = stream_in.shape
    wide = 2 * LANES
    total = 4 * tok
    block = width // 4
    states = 4 * a_log.shape[0]
    vm = pl.BlockSpec(memory_space=pltpu.VMEM)
    hbm = pl.BlockSpec(memory_space=pl.ANY)
    f, b = (lambda *s: pltpu.VMEM(s, F32)), (lambda *s: pltpu.VMEM(s, BF16))
    scan = f(2, total, LANES)
    scratch = dict(
        xf=b(total, width), mg=b(total, width), w_s=b(2, width, wide), wo_s=b(wide, width),
        pk_f=f(4, ROWS, wide), pk_s=b(4, ROWS, wide), segs=pltpu.VMEM((4, SUB, tok), jnp.int32),
        segp=f(total + 2 * PAD, LANES), maskc=f(tok, LANES), nat=scan, inner=f(2, total + PAD, LANES),
        slope=f(2, total + PAD, LANES), act=scan, gate=scan, dt=scan, yg=scan, y=scan,
        bc=f(2 * states, total, LANES), h=f(2, states, total + SUB, LANES), a2b=f(2, states, SUB, LANES),
        st=f(2, states, SUB, LANES), gin=f(2, states, SUB, LANES), cum=f(2, SUB, LANES), alg=f(states, wide),
        full=f(8, 128, LANES), full2=f(8, 128, LANES), mp=f(8, 128, LANES), sum_a=f(4, 128, LANES),
        recv_a=f(4, 128, LANES), recv_b=f(3, 128, LANES), xp=b(LANES, wide), dtwp=b(LANES, wide),
        big_send=b(4, tok // 2, width), big_keep=b(4, tok // 2, width),
        big_recv=b(4, tok // 2, width), big_rb=b(3, tok // 2, width), gpart=b(2, wide, width),
        zrecv=b(3, 3, wide, block), gres=b(3, block, wide), gnat=b(total, wide), znat=b(total, wide),
        spart=f(4, ROWS, wide), srecv=f(3, ROWS, wide), sfull=f(4, ROWS, wide), sown=f(ROWS, wide),
        ggs=f(8, SUB, block), sg_s=f(tok // 2, width),
        ssem=pltpu.SemaphoreType.DMA((112,)), rsem=pltpu.SemaphoreType.DMA((112,)),
        lsem=pltpu.SemaphoreType.DMA((12,)),
    )
    outs = pl.pallas_call(
        fused_kernel,
        out_shape=[
            jax.ShapeDtypeStruct((tok, width), BF16),
            jax.ShapeDtypeStruct((tok, width), F32),
            jax.ShapeDtypeStruct((2, block, 4 * wide), BF16),
            jax.ShapeDtypeStruct((4 * wide, block), BF16),
            jax.ShapeDtypeStruct((ROWS, 4 * wide), F32),
            jax.ShapeDtypeStruct((8, wide), F32),
            jax.ShapeDtypeStruct((1, block), F32),
        ],
        in_specs=[vm, vm, hbm, hbm] + [vm] * 10,
        out_specs=[hbm] * 4 + [vm] * 3,
        scratch_shapes=list(scratch.values()),
        compiler_params=pltpu.CompilerParams(
            collective_id=0, has_side_effects=True, vmem_limit_bytes=VMEM_LIMIT
        ),
    )(
        stream_in.reshape(tok, width), out_grad.reshape(tok, width), in_weight, out_weight, xproj_weight,
        dt_weight, a_log, convolution_weight.reshape(4, block), convolution_bias, step_size_bias,
        skip_term_scale, norm_gain.reshape(1, block), seg_ids, pad_mask,
    )
    so, sg, wg, wo, sm, cv, gg = outs
    return (
        so.reshape(1, tok, width),
        sg.reshape(1, tok, width),
        gg.reshape(block),
        wg.astype(F32),
        wo.astype(F32),
        sm[XP : XP + 24],
        sm[DTW : DTW + 16],
        sm[ALOG : ALOG + 4],
        cv[0:4].reshape(4, 1, wide),
        cv[4:5],
        cv[5:6],
        cv[6:7],
    )


def solution(mesh):
    in_specs = (
        P("dp", "ctx", None),
        P("dp"),
        P(None, "dp", "tp"),
        P("tp", "dp"),
        P("dp", "tp"),
        P("dp", "tp"),
        P("dp", "tp"),
        P(None, "tp", "dp"),
        P("tp", "dp"),
        P("tp", "dp"),
        P("tp", "dp"),
        P("dp", "ctx"),
        P("dp", "ctx"),
        P("dp", "ctx", None),
    )
    out_specs = (
        P("dp", "ctx", None),
        P("dp", "ctx", None),
        P("dp"),
        P(None, "dp", "tp"),
        P("tp", "dp"),
        P("dp", "tp"),
        P("dp", "tp"),
        P("dp", "tp"),
        P(None, "tp", "dp"),
        P("tp", "dp"),
        P("tp", "dp"),
        P("tp", "dp"),
    )

    def run(*args):
        stream, weight = args[0].shape, args[2].shape
        plane_fits = (mesh.shape["dp"], mesh.shape["ctx"], mesh.shape["tp"]) == (4, 4, 2)
        sizes_fit = stream == (4, 1024, 1024) and weight == (2, 1024, 2048)
        part = fused if plane_fits and sizes_fit else shards
        return jax.shard_map(
            part, mesh=mesh, in_specs=in_specs, out_specs=out_specs, check_vma=False
        )(*args)

    return run
```

```python
import math

import jax
import jax.numpy as jnp
from jax import lax
from jax.experimental import pallas as pl
from jax.experimental.pallas import tpu as pltpu
from jax.sharding import PartitionSpec as P

EPS = 1e-05
VMEM_LIMIT = 63 * 2**20


def from_behind(x, axis, by):
    count = lax.axis_size(axis)
    pairs = [(i, i + by) for i in range(count) if 0 <= i + by < count]
    return lax.ppermute(x, axis, pairs)


def entering(x, axis, combine, identity, reverse):
    count, position = (lax.axis_size(axis), lax.axis_index(axis))
    everything = jax.tree.map(
        lambda part, kind: lax.all_gather(part.astype(kind), axis), x, (jnp.bfloat16, jnp.bfloat16)
    )
    start = jax.tree.map(
        lambda part, zero: jnp.broadcast_to(jnp.asarray(zero, part.dtype), part.shape), x, identity
    )

    def step(k, before):
        at = count - 1 - k if reverse else k
        reached = at > position if reverse else at < position
        new = combine(
            before, jax.tree.map(lambda part, own: part[at].astype(own.dtype), everything, x)
        )
        return jax.tree.map(lambda a, b: jnp.where(reached, a, b), new, before)

    return lax.fori_loop(0, count, step, start)


def silu_slope(value):
    sigma = jax.nn.sigmoid(value)
    return sigma * (1.0 + value * (1.0 - sigma))


def link(first, second):
    return (first[0] * second[0], first[1] * second[0] + second[1])


def chain_prefix(decay, drive, backward):
    return lax.associative_scan(link, (decay, drive), reverse=backward, axis=1)


def shards(
    stream_in,
    norm_gain,
    in_weight,
    out_weight,
    xproj_weight,
    dt_weight,
    a_log,
    convolution_weight,
    convolution_bias,
    step_size_bias,
    skip_term_scale,
    seg_ids,
    pad_mask,
    out_grad,
):
    gathered = (
        lax.all_gather(norm_gain, "dp", axis=0, tiled=True),
        lax.all_gather(in_weight, "dp", axis=1, tiled=True),
        lax.all_gather(out_weight, "dp", axis=1, tiled=True),
        lax.all_gather(xproj_weight, "dp", axis=0, tiled=True),
        lax.all_gather(dt_weight, "dp", axis=0, tiled=True),
        lax.all_gather(a_log, "dp", axis=0, tiled=True),
        lax.all_gather(convolution_weight, "dp", axis=2, tiled=True),
        lax.all_gather(convolution_bias, "dp", axis=1, tiled=True),
        lax.all_gather(step_size_bias, "dp", axis=1, tiled=True),
        lax.all_gather(skip_term_scale, "dp", axis=1, tiled=True),
    )
    (
        gain_full,
        win_full,
        wout_full,
        xproj_full,
        dtw_full,
        alog_full,
        convw_full,
        convb_full,
        dtb_full,
        skip_full,
    ) = gathered
    seq_count, tok_count, model_width = stream_in.shape
    channels = win_full.shape[2]
    low_dims = dtw_full.shape[0]
    states = alog_full.shape[0]
    kernel = convw_full.shape[0]
    conv_lag = kernel - 1
    row_count = seq_count * tok_count
    block_len = math.gcd(tok_count, 128)
    block_count = tok_count // block_len
    gain_vec = gain_full.astype(jnp.float32)
    conv_taps = convw_full.reshape(kernel, channels).astype(jnp.float32)
    conv_shift = convb_full.reshape(channels).astype(jnp.float32)
    dt_shift = dtb_full.reshape(channels).astype(jnp.float32)
    skip_vec = skip_full.reshape(channels).astype(jnp.float32)
    a_neg = -jnp.exp(alog_full.astype(jnp.float32))

    def to_blocks(array):
        shaped = array.reshape((seq_count, block_count, block_len) + array.shape[2:])
        return jnp.moveaxis(shaped, 1, 0)

    def from_blocks(array):
        return jnp.moveaxis(array, 0, 1).reshape((seq_count, tok_count) + array.shape[3:])

    def decay_of(dt_block, keep_block):
        return jnp.exp(dt_block[:, :, None, :] * a_neg) * keep_block[:, :, None, None]

    def drive_of(dt_block, act_block, b_block):
        return (dt_block * act_block)[:, :, None, :] * b_block[:, :, :, None]

    def reverse_terms(decay, rhs, carry_in):
        shifted = jnp.concatenate([decay[:, 1:], jnp.zeros_like(decay[:, :1])], axis=1)
        rhs = rhs.at[:, -1].add(carry_in)
        _, grads = chain_prefix(shifted, rhs, True)
        return (grads, decay[:, 0] * grads[:, 0])

    stream = stream_in.astype(jnp.float32)
    rstd = lax.rsqrt(jnp.mean(stream * stream, axis=2, keepdims=True) + EPS)
    normed = (stream * rstd * gain_vec).astype(jnp.bfloat16)
    normed_flat = normed.reshape(row_count, model_width)
    projected = jnp.einsum(
        "rd,kdc->krc", normed_flat, win_full, preferred_element_type=jnp.float32
    ).astype(jnp.bfloat16)
    inner = projected[0].reshape(seq_count, tok_count, channels)
    gate_vals = projected[1].astype(jnp.float32).reshape(seq_count, tok_count, channels)
    seg_low = seg_ids.astype(jnp.bfloat16)
    prev_inner, prev_seg = from_behind(
        (inner[:, tok_count - conv_lag :], seg_low[:, tok_count - conv_lag :]), "ctx", 1
    )
    inner_vals = inner.astype(jnp.float32)
    prev_vals = prev_inner.astype(jnp.float32)
    seg_float = seg_ids.astype(jnp.float32)
    prev_segf = prev_seg.astype(jnp.float32)
    windows = []
    same_list = []
    pre = jnp.zeros((seq_count, tok_count, channels), jnp.float32) + conv_shift
    for offset in range(kernel):
        if offset == 0:
            window = inner_vals
            seg_window = seg_float
        else:
            window = jnp.concatenate(
                [prev_vals[:, conv_lag - offset :], inner_vals[:, : tok_count - offset]], axis=1
            )
            seg_window = jnp.concatenate(
                [prev_segf[:, conv_lag - offset :], seg_float[:, : tok_count - offset]], axis=1
            )
        same = (seg_window == seg_float).astype(jnp.float32)
        windows.append(window)
        same_list.append(same)
        pre = pre + conv_taps[conv_lag - offset] * window * same[:, :, None]
    keep = same_list[1]
    act = (pre * jax.nn.sigmoid(pre)).astype(jnp.bfloat16)
    act_flat = act.reshape(row_count, channels)
    act_vals = act.astype(jnp.float32)
    mixed_part = jnp.einsum("rc,wc->rw", act_flat, xproj_full, preferred_element_type=jnp.float32)
    mixed = lax.psum(mixed_part, "tp")
    low_rank = mixed[:, :low_dims].astype(jnp.bfloat16)
    b_in = mixed[:, low_dims : low_dims + states].reshape(seq_count, tok_count, states)
    c_out = mixed[:, low_dims + states :].reshape(seq_count, tok_count, states)
    dt_arg = (
        jnp.dot(low_rank, dtw_full, preferred_element_type=jnp.float32).reshape(
            seq_count, tok_count, channels
        )
        + dt_shift
    )
    dt_values = jax.nn.softplus(dt_arg)

    def forward_block(carry, piece):
        start, through = carry
        dt_block, act_block, b_block, c_block, keep_block = piece
        decay = decay_of(dt_block, keep_block)
        prods, local = chain_prefix(decay, drive_of(dt_block, act_block, b_block), False)
        hidden = local + prods * start[:, None]
        outputs = jnp.sum(c_block[:, :, :, None] * hidden, axis=2)
        return ((hidden[:, -1], through * prods[:, -1]), (outputs, start, through))

    zero_state = jnp.zeros((seq_count, states, channels), jnp.float32)
    one_state = jnp.ones_like(zero_state)
    dt_blocks = to_blocks(dt_values)
    act_blocks = to_blocks(act_vals)
    b_blocks = to_blocks(b_in)
    c_blocks = to_blocks(c_out)
    keep_blocks = to_blocks(keep)
    (last_state, through), (y_blocks, local_starts, befores) = lax.scan(
        forward_block,
        (zero_state, one_state),
        (dt_blocks, act_blocks, b_blocks, c_blocks, keep_blocks),
    )
    _, entry_state = entering((through, last_state), "ctx", link, (one_state, zero_state), False)
    cum_dt = jnp.cumsum(dt_values, axis=1)
    alive = jnp.cumprod(keep, axis=1)
    cum_blocks = to_blocks(cum_dt)

    def correct(piece):
        cum_block, c_block, alive_block = piece
        carried = jnp.exp(cum_block[:, :, None, :] * a_neg) * entry_state[:, None]
        return alive_block[:, :, None] * jnp.sum(c_block[:, :, :, None] * carried, axis=2)

    corrections = from_blocks(lax.map(correct, (cum_blocks, c_blocks, to_blocks(alive))))
    y_total = from_blocks(y_blocks) + corrections + skip_vec * act_vals
    gate_act = gate_vals * jax.nn.sigmoid(gate_vals)
    gated_flat = (y_total * gate_act).astype(jnp.bfloat16).reshape(row_count, channels)
    branch_part = jnp.dot(gated_flat, wout_full, preferred_element_type=jnp.float32)
    branch = (
        lax.psum(branch_part.astype(jnp.bfloat16), "tp")
        .astype(jnp.float32)
        .reshape(seq_count, tok_count, model_width)
    )
    mask_float = pad_mask.astype(jnp.float32)
    stream_out = (stream + mask_float[:, :, None] * branch).astype(jnp.bfloat16)
    masked_flat = (out_grad * pad_mask[:, :, None].astype(jnp.bfloat16)).reshape(
        row_count, model_width
    )
    grad_wout = jnp.einsum("rc,rd->cd", gated_flat, masked_flat, preferred_element_type=jnp.float32)
    grad_gated = jnp.einsum(
        "rd,cd->rc", masked_flat, wout_full, preferred_element_type=jnp.float32
    ).reshape(seq_count, tok_count, channels)
    grad_y = grad_gated * gate_act
    grad_gate = (grad_gated * y_total * silu_slope(gate_vals)).astype(jnp.bfloat16)
    grad_skip = jnp.sum(grad_y * act_vals, axis=(0, 1))
    gy_blocks = to_blocks(grad_y)
    true_starts = local_starts + befores * entry_state[None]

    def back_core(carry_in, piece):
        dt_block, act_block, b_block, c_block, keep_block, gy_block, start = piece
        decay = decay_of(dt_block, keep_block)
        prods, local = chain_prefix(decay, drive_of(dt_block, act_block, b_block), False)
        hidden = local + prods * start[:, None]
        earlier = jnp.concatenate([start[:, None], hidden[:, :-1]], axis=1)
        grads, carry_out = reverse_terms(
            decay, c_block[:, :, :, None] * gy_block[:, :, None, :], carry_in
        )
        stepped = earlier * decay
        weighted = grads * stepped
        along_b = jnp.sum(grads * b_block[:, :, :, None], axis=2)
        grad_dt = jnp.sum(weighted * a_neg, axis=2) + along_b * act_block
        grad_act = along_b * dt_block
        grad_b = jnp.sum(grads * (dt_block * act_block)[:, :, None, :], axis=3)
        grad_c = jnp.sum(gy_block[:, :, None, :] * hidden, axis=3)
        return (carry_out, weighted, stepped, (grad_dt, grad_act, grad_b, grad_c))

    back_pieces = (dt_blocks, act_blocks, b_blocks, c_blocks, keep_blocks, gy_blocks, true_starts)
    zero_acc = jnp.zeros((states, channels), jnp.float32)
    cum_end = cum_dt[:, -1]
    suffix = jnp.flip(jnp.cumprod(jnp.flip(keep, axis=1), axis=1), axis=1)
    rest = jnp.concatenate([suffix[:, 1:], jnp.ones((seq_count, 1), jnp.float32)], axis=1)
    rest_blocks = to_blocks(rest)

    def reach_of(cum_block, rest_block):
        return (
            jnp.exp((cum_end[:, None, None, :] - cum_block[:, :, None, :]) * a_neg)
            * rest_block[:, :, None, None]
        )

    def kept_back(carry, piece):
        carry_in, a_acc, q_acc = carry
        core_piece = piece[:7]
        carry_out, weighted, stepped, terms = back_core(carry_in, core_piece)
        dt_block = core_piece[0]
        along = stepped * reach_of(piece[7], piece[8])
        a_acc = a_acc + jnp.sum(weighted * dt_block[:, :, None, :], axis=(0, 1))
        q_acc = q_acc + jnp.sum(along * dt_block[:, :, None, :], axis=1)
        return ((carry_out, a_acc, q_acc), terms + (along,))

    (edge_grad, a_local, q_total), (base_dt, base_act, base_b, grad_c_blocks, along_blocks) = (
        lax.scan(
            kept_back,
            (zero_state, zero_acc, zero_state),
            back_pieces + (cum_blocks, rest_blocks),
            reverse=True,
        )
    )
    _, after_grad = entering((through, edge_grad), "ctx", link, (one_state, zero_state), True)

    def adjust(piece):
        dt_block, act_block, b_block, cum_block, rest_block, along = piece
        extra = reach_of(cum_block, rest_block) * after_grad[:, None]
        along_b = jnp.sum(extra * b_block[:, :, :, None], axis=2)
        grad_dt = jnp.sum(along * after_grad[:, None] * a_neg, axis=2) + along_b * act_block
        grad_act = along_b * dt_block
        grad_b = jnp.sum(extra * (dt_block * act_block)[:, :, None, :], axis=3)
        return (grad_dt, grad_act, grad_b)

    add_dt, add_act, add_b = lax.map(
        adjust, (dt_blocks, act_blocks, b_blocks, cum_blocks, rest_blocks, along_blocks)
    )
    grad_dt_blocks = base_dt + add_dt
    grad_act_blocks = base_act + add_act
    grad_b_blocks = base_b + add_b
    a_total = a_local + jnp.sum(q_total * after_grad, axis=0)
    grad_lin = from_blocks(grad_dt_blocks) * jax.nn.sigmoid(dt_arg)
    grad_dtb = jnp.sum(grad_lin, axis=(0, 1))
    grad_lin_low = grad_lin.reshape(row_count, channels).astype(jnp.bfloat16)
    grad_dtw = jnp.einsum("rk,rc->kc", low_rank, grad_lin_low, preferred_element_type=jnp.float32)
    grad_rank = jnp.einsum("rc,kc->rk", grad_lin_low, dtw_full, preferred_element_type=jnp.float32)
    grad_mixed_part = jnp.concatenate(
        [
            grad_rank,
            from_blocks(grad_b_blocks).reshape(row_count, states),
            from_blocks(grad_c_blocks).reshape(row_count, states),
        ],
        axis=1,
    )
    grad_mixed = lax.psum(grad_mixed_part, "tp").astype(jnp.bfloat16)
    grad_xproj = jnp.einsum("rw,rc->wc", grad_mixed, act_flat, preferred_element_type=jnp.float32)
    grad_act_total = (
        grad_y * skip_vec
        + from_blocks(grad_act_blocks)
        + jnp.dot(grad_mixed, xproj_full, preferred_element_type=jnp.float32).reshape(
            seq_count, tok_count, channels
        )
    )
    grad_pre = grad_act_total * silu_slope(pre)
    grad_convb = jnp.sum(grad_pre, axis=(0, 1))
    tap_grads = [None] * kernel
    grad_inner = jnp.zeros((seq_count, tok_count, channels), jnp.float32)
    tail_grad = jnp.zeros((seq_count, conv_lag, channels), jnp.float32)
    for offset in range(kernel):
        weighted_pre = grad_pre * same_list[offset][:, :, None]
        tap_grads[conv_lag - offset] = jnp.sum(weighted_pre * windows[offset], axis=(0, 1))
        scaled_pre = weighted_pre * conv_taps[conv_lag - offset]
        if offset == 0:
            grad_inner = grad_inner + scaled_pre
        else:
            grad_inner = grad_inner + jnp.concatenate(
                [scaled_pre[:, offset:], jnp.zeros((seq_count, offset, channels), jnp.float32)],
                axis=1,
            )
            tail_grad = tail_grad.at[:, conv_lag - offset :].add(scaled_pre[:, :offset])
    grad_convw = jnp.stack(tap_grads)
    sent_back = from_behind(tail_grad, "ctx", -1)
    grad_inner = grad_inner.at[:, tok_count - conv_lag :].add(sent_back)
    grad_proj = jnp.stack(
        [
            grad_inner.astype(jnp.bfloat16).reshape(row_count, channels),
            grad_gate.reshape(row_count, channels),
        ]
    )
    grad_win = jnp.einsum("rd,krc->kdc", normed_flat, grad_proj, preferred_element_type=jnp.float32)
    grad_norm_part = jnp.einsum(
        "krc,kdc->rd", grad_proj, win_full, preferred_element_type=jnp.float32
    )
    grad_norm = lax.psum(grad_norm_part, "tp").reshape(seq_count, tok_count, model_width)
    grad_gain = jnp.sum(grad_norm * stream * rstd, axis=(0, 1))
    scaled = grad_norm * gain_vec
    stream_grad = (
        out_grad.astype(jnp.float32)
        + rstd * scaled
        - stream * (rstd * rstd * rstd) * jnp.mean(scaled * stream, axis=2, keepdims=True)
    )
    grad_alog = a_total * a_neg
    local_grads = (
        grad_gain,
        grad_win,
        grad_wout,
        grad_xproj,
        grad_dtw,
        grad_alog,
        grad_convw.reshape(kernel, 1, channels),
        grad_convb.reshape(1, channels),
        grad_dtb.reshape(1, channels),
        grad_skip.reshape(1, channels),
    )
    summed = lax.psum(
        (
            local_grads[0],
            local_grads[1],
            local_grads[2],
            local_grads[3],
            local_grads[4],
            local_grads[5],
            local_grads[6],
            local_grads[7],
            local_grads[8],
            local_grads[9],
        ),
        "ctx",
    )
    owned = (
        lax.psum_scatter(summed[0], "dp", scatter_dimension=0, tiled=True),
        lax.psum_scatter(summed[1], "dp", scatter_dimension=1, tiled=True),
        lax.psum_scatter(summed[2], "dp", scatter_dimension=1, tiled=True),
        lax.psum_scatter(summed[3], "dp", scatter_dimension=0, tiled=True),
        lax.psum_scatter(summed[4], "dp", scatter_dimension=0, tiled=True),
        lax.psum_scatter(summed[5], "dp", scatter_dimension=0, tiled=True),
        lax.psum_scatter(summed[6], "dp", scatter_dimension=2, tiled=True),
        lax.psum_scatter(summed[7], "dp", scatter_dimension=1, tiled=True),
        lax.psum_scatter(summed[8], "dp", scatter_dimension=1, tiled=True),
        lax.psum_scatter(summed[9], "dp", scatter_dimension=1, tiled=True),
    )
    return (
        stream_out,
        stream_grad,
        owned[0],
        owned[1],
        owned[2],
        owned[3],
        owned[4],
        owned[5],
        owned[6],
        owned[7],
        owned[8],
        owned[9],
    )


F32 = jnp.float32
BF16 = jnp.bfloat16
MESH = pl.DeviceIdType.MESH
LOG2E = math.log2(math.e)
LN2 = math.log(2.0)
KILL = 1e30
SUB = 8
LANES = 128
PAD = 24
ROWS = 64
XP, DTW, ALOG, CONVW, CONVB, DTB, SKIP, GAIN = 0, 24, 40, 44, 48, 49, 50, 51
A_DTW, A_ALOG, A_DTB, A_SKIP, A_ROWS = 0, 16, 20, 21, 24
B_XP, B_CONVW, B_CONVB, B_ROWS = 0, 24, 28, 32
NT = (((1,), (1,)), ((), ()))
TN = (((0,), (0,)), ((), ()))


def dot(a, b):
    return jnp.dot(a, b, preferred_element_type=F32)


def dot_nt(a, b):
    return lax.dot_general(a, b, NT, preferred_element_type=F32)


def dot_tn(a, b):
    return lax.dot_general(a, b, TN, preferred_element_type=F32)


def at8(start, size):
    return pl.ds(pl.multiple_of(start, 8), size)


def sigmoid(v):
    return 0.5 + 0.5 * jnp.tanh(0.5 * v)


def log_one_plus(v):
    series = v * (1.0 - v * (0.5 - v * (1.0 / 3.0 - v * 0.25)))
    return jnp.where(v < 0.01, series, jnp.log(1.0 + v))


def one_less_exp(v):
    series = v * (1.0 - v * (0.5 - v * (1.0 / 6.0 - v * (1.0 / 24.0 - v * (1.0 / 120.0)))))
    return jnp.where(v < 0.1, series, 1.0 - jnp.exp(-v))


def prefix_of(ends, prods):
    row = lax.broadcasted_iota(jnp.int32, ends.shape, 0)
    for gap in (1, 2, 4):
        ok = row >= gap
        ends = ends + prods * jnp.where(ok, pltpu.roll(ends, gap, 0), 0.0)
        prods = prods * jnp.where(ok, pltpu.roll(prods, gap, 0), 1.0)
    return jnp.where(row >= 1, pltpu.roll(ends, 1, 0), 0.0)


def suffix_of(ends, prods):
    row = lax.broadcasted_iota(jnp.int32, ends.shape, 0)
    for gap in (1, 2, 4):
        ok = row < SUB - gap
        ends = ends + prods * jnp.where(ok, pltpu.roll(ends, SUB - gap, 0), 0.0)
        prods = prods * jnp.where(ok, pltpu.roll(prods, SUB - gap, 0), 1.0)
    return jnp.where(row < SUB - 1, pltpu.roll(ends, SUB - 1, 0), 0.0)


def fused_kernel(
    x_ref, og_ref, win_ref, wout_ref, xproj_ref, dtw_ref, alog_ref, convw_ref, convb_ref, dtb_ref,
    skip_ref, gain_ref, seg_ref, mask_ref,
    so_out, sg_out, wg_out, wo_out, sm_out, cv_out, gg_out,
    x_half, og_half, xf, mg, w_s, wo_s, pk_f, pk_s, segs, segp, maskc, nat, inner, slope, act, gate, dt, yg, y,
    bc, h, a2b, st, gin, cum, alg, full, full2, mp, sum_a, recv_a, recv_b, xp, dtwp,
    big_send, big_keep, big_recv, big_rb, gpart, zrecv, gres, gnat, znat, spart, srecv, sfull, bpart, brecv, bfull, sown, ggs,
    sg_s, ssem, rsem, lsem,
):
    z, c, k = lax.axis_index("dp"), lax.axis_index("ctx"), lax.axis_index("tp")
    nz = lax.axis_size("dp")
    px, py = lax.rem(c, 2), c // 2
    sib = (z, c, 1 - k)
    plane = [None, py * 2 + (1 - px), (1 - py) * 2 + px, (1 - py) * 2 + (1 - px)]
    peers = [None] + [(z, plane[p], k) for p in (1, 2, 3)]
    toward = [None] + [lax.rem(z + d, nz) for d in (1, 2, 3)]
    behind = [None] + [lax.rem(z + nz - d, nz) for d in (1, 2, 3)]
    lines = [None] + [(toward[d], c, k) for d in (1, 2, 3)]
    count = [0]
    local_count = [0]
    pending = []

    def send(src, dst, device):
        i = count[0]
        count[0] += 1
        copy = pltpu.make_async_remote_copy(
            src_ref=src, dst_ref=dst, send_sem=ssem.at[i], recv_sem=rsem.at[i],
            device_id=device, device_id_type=MESH,
        )
        copy.start()
        pending.append(copy)
        return copy

    def local(src, dst):
        i = local_count[0]
        local_count[0] += 1
        copy = pltpu.make_async_copy(src, dst, lsem.at[i])
        copy.start()
        return copy

    def flush(copies):
        for copy in copies:
            copy.wait_send()
            pending[:] = [other for other in pending if other is not copy]

    tok = maskc.shape[0]
    half = tok // 2
    total = xf.shape[0]
    width = xf.shape[1]
    steps = total // SUB
    states = h.shape[1]
    wide = 2 * LANES
    block = w_s.shape[1] // 4
    tiles = (0, 1)
    rb = 128
    nblk = total // rb

    def lanes(t):
        return slice(t * LANES, (t + 1) * LANES)

    def blk(i):
        return pl.ds(pl.multiple_of(i * rb, rb), rb)

    wb = 512

    def wide_blk(i):
        return pl.ds(pl.multiple_of(i * wb, wb), wb)

    def tau_rows(tau):
        return at8(tau * SUB, SUB)

    def loop(n, body, unroll=1):
        def step(i, carry):
            body(i)
            return carry

        lax.fori_loop(0, n, step, 0, unroll=unroll)

    barrier = pltpu.get_barrier_semaphore()
    everyone = [sib] + peers[1:] + [(z, plane[p], 1 - k) for p in (1, 2, 3)] + lines[1:]
    for device in everyone:
        pl.semaphore_signal(barrier, inc=1, device_id=device, device_id_type=MESH)
    chans = pl.ds(pl.multiple_of(c * wide, wide), wide)
    spart[...] = jnp.zeros_like(spart)
    spart[0, XP : XP + 24, :] = xproj_ref[:, chans].astype(F32)
    spart[0, DTW : DTW + 16, :] = dtw_ref[:, chans].astype(F32)
    spart[0, ALOG : ALOG + 4, :] = alog_ref[:, chans].astype(F32)
    spart[0, CONVW : CONVW + 4, :] = convw_ref[...].astype(F32)
    spart[0, CONVB : CONVB + 1, :] = convb_ref[...].astype(F32)
    spart[0, DTB : DTB + 1, :] = dtb_ref[...].astype(F32)
    spart[0, SKIP : SKIP + 1, :] = skip_ref[...].astype(F32)
    spart[0, GAIN : GAIN + 1, :] = gain_ref[...].astype(F32).reshape(1, block)
    pk_s[z] = spart[0].astype(BF16)
    segs[c] = jnp.broadcast_to(seg_ref[...], (SUB, tok))
    pl.semaphore_wait(barrier, len(everyone))

    s_pack = [send(pk_s.at[z], pk_s.at[z], lines[d]) for d in (1, 2, 3)]
    s_seg = [send(segs.at[c], segs.at[c], peers[p]) for p in (1, 2, 3)]
    my_half = pl.ds(pl.multiple_of(c * tok + k * half, half), half)
    s_x = [send(x_ref.at[pl.ds(pl.multiple_of(k * half, half), half)], xf.at[my_half], peers[p]) for p in (3, 1, 2)]

    zrows = pl.ds(pl.multiple_of(z * block, block), block)

    def weight(which):
        return [
            send(win_ref.at[which, :, chans], w_s.at[which, zrows, :], lines[d]) for d in (1, 2, 3)
        ]

    s_wx = weight(0)
    own_w = [local(win_ref.at[i, :, chans], w_s.at[i, zrows, :]) for i in (0, 1)]
    zcols = pl.ds(pl.multiple_of(z * block, block), block)
    own_wo = local(wout_ref.at[chans, :], wo_s.at[:, zcols])

    own_rows = pl.ds(pl.multiple_of(c * tok, tok), tok)
    half_rows = pl.ds(pl.multiple_of(k * half, half), half)
    own_x = local(x_ref, xf.at[own_rows, :])
    own_og = local(og_ref, mg.at[own_rows, :])
    own_half = [local(x_ref.at[half_rows, :], x_half), local(og_ref.at[half_rows, :], og_half)]
    mrow = mask_ref[...].astype(F32)
    for b in range(tok // LANES):
        rows = slice(b * LANES, (b + 1) * LANES)
        maskc[rows, :] = jnp.broadcast_to(mrow[:, rows], (LANES, LANES)).T
    mcol = jnp.concatenate([maskc[...]] * (width // LANES), axis=1)
    own_og.wait()
    mg[own_rows, :] = (mg[own_rows, :].astype(F32) * mcol).astype(BF16)

    for copy in s_pack:
        copy.wait_recv()
    for i in range(4):
        pk_f[i] = pk_s[i].astype(F32)
    for i in range(4):
        alg[4 * i : 4 * i + 4, :] = pk_f[i, ALOG : ALOG + 4, :]
    xp_rows = jnp.concatenate([pk_f[i, XP : XP + 24, :] for i in range(4)] + [jnp.zeros((32, wide), F32)], axis=0)
    xp[...] = xp_rows.astype(BF16)
    dt_rows = jnp.concatenate([pk_f[i, DTW : DTW + 16, :] for i in range(4)] + [jnp.zeros((64, wide), F32)], axis=0)
    dtwp[...] = dt_rows.astype(BF16)
    a2v = -jnp.exp(alg[...]) * LOG2E
    for n in range(states):
        for t in tiles:
            a2b[t, n] = jnp.broadcast_to(a2v[n : n + 1, lanes(t)], (SUB, LANES))
    gain_row = jnp.concatenate([pk_f[i, GAIN : GAIN + 1, :] for i in range(4)], axis=1)
    sown[...] = pk_f[c]

    def param(row, t):
        return sown[row : row + 1, lanes(t)]

    for copy in s_seg:
        copy.wait_recv()
    for i in range(4):
        srow = segs[i, 0:1, :].astype(F32)
        for b in range(tok // LANES):
            rows = slice(b * LANES, (b + 1) * LANES)
            nat[0, i * tok + b * LANES : i * tok + (b + 1) * LANES, :] = jnp.broadcast_to(
                srow[:, rows], (LANES, LANES)
            ).T

    def seg_in(tau):
        segp[at8(PAD + tau * SUB, SUB), :] = nat[0, pl.ds(tau, SUB, stride=steps), :]

    loop(steps, seg_in, 8)
    sub_row = lax.broadcasted_iota(jnp.int32, (SUB, LANES), 0)

    def from_before(v, fill):
        return jnp.where(sub_row >= 1, pltpu.roll(v, 1, 0), fill)

    def from_after(v, fill):
        return jnp.where(sub_row < SUB - 1, pltpu.roll(v, SUB - 1, 0), fill)

    for j in range(3):
        segp[j * SUB : (j + 1) * SUB, :] = from_before(segp[total + j * SUB : total + (j + 1) * SUB, :], -1.0)
        segp[PAD + total + j * SUB : PAD + total + (j + 1) * SUB, :] = from_after(
            segp[PAD + j * SUB : PAD + (j + 1) * SUB, :], -2.0
        )

    def halves(copies, buf):
        relays = []
        for copy, p in zip(copies, (3, 1, 2)):
            copy.wait_recv()
            rows = pl.ds(pl.multiple_of(plane[p] * tok + k * half, half), half)
            relays.append(send(buf.at[rows], buf.at[rows], sib))
        return relays

    r_x = halves(s_x, xf)
    own_x.wait()

    for copy in r_x:
        copy.wait_recv()

    def norm(i):
        v = xf[blk(i), :].astype(F32)
        r = lax.rsqrt(jnp.mean(v * v, axis=1, keepdims=True) + EPS)
        xf[blk(i), :] = (v * r * gain_row).astype(BF16)

    flush(r_x)
    loop(nblk, norm)

    def project(which, dst, off):
        def body(i):
            v = dot(xf[wide_blk(i), :], w_s[which]).astype(BF16).astype(F32)
            for t in tiles:
                nat[t, wide_blk(i), :] = v[:, lanes(t)]

        loop(total // wb, body)
        permute_in(dst, off)

    def permute_in(dst, off):
        def body(tau):
            for t in tiles:
                dst[t, at8(off + tau * SUB, SUB), :] = nat[t, pl.ds(tau, SUB, stride=steps), :]

        loop(steps, body, 8)

    def permute_out(src, dst):
        def body(i):
            for s in range(SUB):
                for t in tiles:
                    nat[t, at8(s * steps + i * SUB, SUB), :] = src[t, pl.ds(i * SUB * SUB + s, SUB, stride=SUB), :]

        loop(steps // SUB, body)

        def cast(i):
            dst[blk(i), :] = jnp.concatenate([nat[t, blk(i), :] for t in tiles], axis=1).astype(BF16)

        loop(nblk, cast)

    for copy in s_wx:
        copy.wait_recv()
    own_w[0].wait()
    s_wz = weight(1)
    project(0, inner, PAD)
    for t in tiles:
        for j in range(3):
            inner[t, j * SUB : (j + 1) * SUB, :] = from_before(inner[t, total + j * SUB : total + (j + 1) * SUB, :], 0.0)

    def conv(i):
        for t in tiles:
            mine = segp[at8(PAD + i * rb, rb), :]
            pre = jnp.zeros((rb, LANES), F32) + param(CONVB, t)
            for j in range(4):
                window = inner[t, at8(PAD + i * rb - j * SUB, rb), :]
                if j:
                    window = jnp.where(segp[at8(PAD + i * rb - j * SUB, rb), :] == mine, window, 0.0)
                pre = pre + param(CONVW + 3 - j, t) * window
            s = sigmoid(pre)
            act[t, blk(i), :] = (pre * s).astype(BF16).astype(F32)
            slope[t, blk(i), :] = s * (1.0 + pre * (1.0 - s))

    loop(nblk, conv)

    def tiles_bf(ref, i):
        return jnp.concatenate([ref[t, blk(i), :] for t in tiles], axis=1).astype(BF16)

    def mix(i):
        mp[i] = dot_nt(tiles_bf(act, i), xp[...])

    loop(nblk, mix)

    def plane_sum(out, between):
        first = send(mp.at[pl.ds((1 - k) * 4, 4)], recv_a, sib)
        between[0]()
        first.wait_recv()
        for i in range(4):
            sum_a[i] = (mp[k * 4 + i] + recv_a[i]).astype(BF16)
        second = [send(sum_a.at[plane[p]], recv_b.at[p - 1], peers[p]) for p in (3, 1, 2)]
        between[1]()
        for copy in second:
            copy.wait_recv()
        mine = k * 4 + c
        v = mp[mine] + recv_a[c]
        for p in range(3):
            v = v + recv_b[p].astype(F32)
        out[mine] = v.astype(BF16)
        third = [send(out.at[mine], out.at[mine], peers[p]) for p in (3, 1, 2)]
        third.append(send(out.at[mine], out.at[mine], sib))
        between[2]()
        fourth = []
        for copy, p in zip(third, (3, 1, 2)):
            copy.wait_recv()
            there = k * 4 + plane[p]
            fourth.append(send(out.at[there], out.at[there], sib))
        between[3]()
        for copy in [third[3]] + fourth:
            copy.wait_recv()
        return [first] + second

    late = {}

    def send_wo():
        late["wo"] = [send(wout_ref.at[chans, :], wo_s.at[:, zcols], lines[d]) for d in (1, 2, 3)]

    def gates():
        for copy in s_wz:
            copy.wait_recv()
        own_w[1].wait()
        project(1, gate, 0)

    def nothing():
        pass

    def send_mg():
        late["mg"] = [send(mg.at[my_half], mg.at[my_half], peers[p]) for p in (3, 1, 2)]

    def gap():
        send_mg()
        gates()

    first_sum = plane_sum(full, [nothing, nothing, send_wo, gap])

    def steps_of(i):
        arg = dot(full[i], dtwp[...])
        for t in tiles:
            v = arg[:, lanes(t)] + param(DTB, t)
            dt[t, blk(i), :] = jnp.maximum(v, 0.0) + log_one_plus(jnp.exp(-jnp.abs(v)))

    loop(nblk, steps_of)

    ahead = lax.broadcasted_iota(jnp.int32, (LANES, 4 * LANES), 0) - 64
    ahead = ahead - lax.broadcasted_iota(jnp.int32, (LANES, 4 * LANES), 1) // LANES

    def spread(g):
        pick = jnp.where(ahead == g * 4, 1.0, 0.0).astype(BF16)
        for i in range(nblk // 2):
            v = dot(jnp.concatenate([full[2 * i], full[2 * i + 1]], axis=0), pick)
            for q in range(4):
                bc[g * 4 + q, i * 2 * rb : (i + 1) * 2 * rb, :] = v[:, lanes(q)]

    loop(2 * states // 4, spread)

    def dts(t, tau):
        v = dt[t, tau_rows(tau), :]
        r = at8(PAD + tau * SUB, SUB)
        p = at8(PAD + tau * SUB - SUB, SUB)
        return v, jnp.where(segp[r, :] == segp[p, :], v, KILL)

    for t in tiles:

        def ends(tau, carry, t=t):
            v, killed = dts(t, tau)
            drive = v * act[t, tau_rows(tau), :]
            new = [
                carry[n] * jnp.exp2(killed * a2b[t, n]) + drive * bc[n, tau_rows(tau), :] for n in range(states)
            ]
            return tuple(new) + (carry[states] + killed,)

        zero = jnp.zeros((SUB, LANES), F32)
        got = lax.fori_loop(0, steps, ends, (zero,) * (states + 1), unroll=4)
        cum[t] = got[states]
        for n in range(states):
            st[t, n] = prefix_of(got[n], jnp.exp2(got[states] * a2b[t, n]))

    for t in tiles:
        if t:
            late["mg"] = halves(late["mg"], mg)
        for n in range(states):
            h[t, n, 0:SUB, :] = st[t, n]

        def forward(tau, carry, t=t):
            v, killed = dts(t, tau)
            drive = v * act[t, tau_rows(tau), :]
            new, parts = [], [None] * 4
            for n in range(states):
                s = carry[n] * jnp.exp2(killed * a2b[t, n]) + drive * bc[n, tau_rows(tau), :]
                h[t, n, at8(tau * SUB + SUB, SUB), :] = s
                o = s * bc[states + n, tau_rows(tau), :]
                parts[n % 4] = o if parts[n % 4] is None else parts[n % 4] + o
                new.append(s)
            y[t, tau_rows(tau), :] = (parts[0] + parts[1]) + (parts[2] + parts[3])
            return tuple(new)

        lax.fori_loop(0, steps, forward, tuple(st[t, n] for n in range(states)), unroll=4)

    for copy in late["mg"] + late["wo"]:
        copy.wait_recv()
    own_wo.wait()

    def ograd(i):
        v = dot_nt(mg[wide_blk(i), :], wo_s[...])
        for t in tiles:
            nat[t, wide_blk(i), :] = v[:, lanes(t)]

    loop(total // wb, ograd)
    gb = SUB * SUB

    def strided(t, i):
        return jnp.concatenate([nat[t, pl.ds(i * SUB + u, SUB, stride=steps), :] for u in range(SUB)], axis=0)

    def gating(i, carry):
        new = []
        rows = pl.ds(pl.multiple_of(i * gb, gb), gb)
        for t in tiles:
            gv, ov, av = gate[t, rows, :], strided(t, i), act[t, rows, :]
            s = sigmoid(gv)
            ytot = y[t, rows, :] + param(SKIP, t) * av
            gy = ov * (gv * s)
            yg[t, rows, :] = gy
            y[t, rows, :] = ytot * (gv * s)
            gate[t, rows, :] = ov * ytot * (s * (1.0 + gv * (1.0 - s)))
            new.append(carry[t] + jnp.sum((gy * av).reshape(SUB, SUB, LANES), axis=0))
        return tuple(new)

    zero = jnp.zeros((SUB, LANES), F32)
    skip_sum = lax.fori_loop(0, total // gb, gating, (zero, zero))
    permute_out(y, gnat)
    permute_out(gate, znat)

    def owner_rows(i, q):
        return pl.ds(pl.multiple_of(i * tok + q * half, half), half)

    pieces = ((3, 1, 2, 0),)

    def start_rows(lefts, right):
        def fill(dst, group, q):
            there = [plane[p] if p else c for p in group]
            rows = [jnp.concatenate([left[owner_rows(i, q), :] for i in there], axis=0) for left in lefts]

            def body(j):
                cols = pl.ds(pl.multiple_of(j * wide, wide), wide)
                v = right(rows, cols)
                for i, p in enumerate(group):
                    dst[p, :, cols] = v[i * half : (i + 1) * half, :].astype(BF16)

            loop(width // wide, body)

        first = []
        for group in pieces:
            fill(big_send, group, 1 - k)
            first += [send(big_send.at[p], big_recv.at[p], sib) for p in group]
        for group in pieces:
            fill(big_keep, group, k)
        return first

    def middle_rows(first):
        second = []
        for copy, p in zip(first, pieces[0]):
            copy.wait_recv()
            big_keep[p] = (big_keep[p].astype(F32) + big_recv[p].astype(F32)).astype(BF16)
            if p:
                second.append(send(big_keep.at[p], big_rb.at[p - 1], peers[p]))
        return second

    def end_rows(second):
        for copy in second:
            copy.wait_recv()
        v = big_keep[0].astype(F32)
        for p in range(3):
            v = v + big_rb[p].astype(F32)
        return v

    branch_a = start_rows([gnat], lambda rows, cols: dot(rows[0], wo_s[:, cols]))

    def weight_grad(slot, left, right):
        gpart[slot % 2] = dot_tn(left[...], right[...]).astype(BF16)
        return [
            send(
                gpart.at[slot % 2, :, pl.ds(pl.multiple_of(toward[d] * block, block), block)],
                zrecv.at[slot, d - 1],
                lines[d],
            )
            for d in (1, 2, 3)
        ]

    def owned_grad(slot, copies):
        for copy in copies:
            copy.wait_recv()
        v = gpart[slot % 2, :, zcols].astype(F32)
        for d in range(3):
            v = v + zrecv[slot, d].astype(F32)
        return v

    def share(slot, dst):
        return [local(gres.at[slot], dst)] + [send(gres.at[slot], dst, peers[p]) for p in (3, 1, 2)]

    z_wo = weight_grad(2, gnat, mg)
    z_wz = weight_grad(1, znat, xf)

    for t in tiles:
        if t:
            branch_b = middle_rows(branch_a)

        def back_ends(i, carry, t=t):
            tau = steps - 1 - i
            _, killed = dts(t, tau)
            gy = yg[t, tau_rows(tau), :]
            return tuple(
                (carry[n] + gy * bc[states + n, tau_rows(tau), :]) * jnp.exp2(killed * a2b[t, n])
                for n in range(states)
            )

        got = lax.fori_loop(0, steps, back_ends, (zero,) * states, unroll=4)
        for n in range(states):
            gin[t, n] = suffix_of(got[n], jnp.exp2(cum[t] * a2b[t, n]))

    flush(branch_a)
    so_s = big_send.at[0]

    gsum, dsum = gate, y
    part = states // 2
    for lo in (0, part):
        names = list(range(lo, lo + part))

        def back(i, carry, names=names, lo=lo):
            grads, acc = carry
            tau = steps - 1 - i
            r = tau_rows(tau)
            pair = [dts(t, tau) for t in tiles]
            drive = [pair[t][0] * act[t, r, :] for t in tiles]
            gy = [yg[t, r, :] for t in tiles]
            along = [None, None]
            down = [None, None]
            new_g, new_a = [], []
            for q, n in enumerate(names):
                bv, cv = bc[n, r, :], bc[states + n, r, :]
                pb = pc = None
                for t in tiles:
                    a2 = a2b[t, n]
                    decay = jnp.exp2(pair[t][1] * a2)
                    g = grads[2 * q + t] + gy[t] * cv
                    gb = g * bv
                    along[t] = gb if along[t] is None else along[t] + gb
                    v = g * drive[t]
                    pb = v if pb is None else pb + v
                    v = gy[t] * h[t, n, at8(tau * SUB + SUB, SUB), :]
                    pc = v if pc is None else pc + v
                    gd = g * decay
                    dla = gd * h[t, n, r, :]
                    v = dla * a2
                    down[t] = v if down[t] is None else down[t] + v
                    new_a.append(acc[2 * q + t] + dla * pair[t][0])
                    new_g.append(gd)
                bc[n, r, :] = pb
                bc[states + n, r, :] = pc
            for t in tiles:
                if lo == 0:
                    gsum[t, r, :] = along[t]
                    dsum[t, r, :] = down[t]
                else:
                    gsum[t, r, :] = gsum[t, r, :] + along[t]
                    dsum[t, r, :] = dsum[t, r, :] + down[t]
            return tuple(new_g), tuple(new_a)

        start = tuple(gin[t, n] for n in names for t in tiles)
        _, acc = lax.fori_loop(0, steps, back, (start, (zero,) * (2 * part)), unroll=2)
        for q, n in enumerate(names):
            for t in tiles:
                alg[n : n + 1, lanes(t)] = (
                    jnp.sum(acc[2 * q + t], axis=0, keepdims=True) * a2b[t, n][0:1, :] * LN2
                )

    gres[2] = owned_grad(2, z_wo).astype(BF16)
    late["gwo"] = share(2, wo_out.at[chans, :])

    def lin(i, carry):
        new = []
        rank = []
        for t in tiles:
            av, gv = act[t, blk(i), :], gsum[t, blk(i), :]
            v = (dsum[t, blk(i), :] * LN2 + av * gv) * one_less_exp(dt[t, blk(i), :])
            new.append(carry[t] + jnp.sum(v.reshape(rb // SUB, SUB, LANES), axis=0))
            low = v.astype(BF16)
            rank.append(low)
            dsum[t, blk(i), :] = low.astype(F32)
            gsum[t, blk(i), :] = dt[t, blk(i), :] * gv + param(SKIP, t) * yg[t, blk(i), :]
        mp[i] = dot_nt(jnp.concatenate(rank, axis=1), dtwp[...])
        return tuple(new)

    flush(first_sum)
    dtb_sum = lax.fori_loop(0, nblk, lin, (zero, zero))

    beside = lax.broadcasted_iota(jnp.int32, (wide, LANES), 1) - 64
    beside = beside - lax.broadcasted_iota(jnp.int32, (wide, LANES), 0) // LANES

    def collect(i):
        rows = pl.ds(pl.multiple_of(i * 2 * rb, 2 * rb), 2 * rb)
        v = jnp.concatenate([mp[2 * i], mp[2 * i + 1]], axis=0)
        for n in range(0, 2 * states, 2):
            pick = jnp.where(beside == n, 1.0, 0.0).astype(BF16)
            pair = jnp.concatenate([bc[n, rows, :], bc[n + 1, rows, :]], axis=1).astype(BF16)
            v = v + dot(pair, pick)
        mp[2 * i] = v[:rb, :]
        mp[2 * i + 1] = v[rb:, :]

    loop(nblk // 2, collect)

    def finish_early():
        v = end_rows(branch_b)
        mk = jnp.concatenate([maskc[half_rows, :]] * (width // LANES), axis=1)
        for copy in own_half:
            copy.wait()
        so_s[...] = (x_half[...].astype(F32) + mk * v).astype(BF16)
        late["so"] = [local(so_s, so_out.at[half_rows, :]), send(so_s, so_out.at[half_rows, :], sib)]

    def finish_z():
        v = owned_grad(1, z_wz).T
        gres[1] = v.astype(BF16)
        late["gain"] = v * w_s[1, zrows, :].astype(F32)

    def small_a():
        low = jnp.concatenate([full[i] for i in range(nblk)], axis=0)
        linv = jnp.concatenate([tiles_bf(dsum, i) for i in range(nblk)], axis=0)
        g = dot_tn(low, linv)
        for i in range(4):
            spart[i, A_DTW : A_DTW + 16, :] = g[i * 16 : i * 16 + 16, :]
            spart[i, A_ALOG : A_ALOG + 4, :] = alg[i * 4 : i * 4 + 4, :]
            for t in tiles:
                spart[i, A_DTB : A_DTB + 1, lanes(t)] = jnp.sum(dtb_sum[t], axis=0, keepdims=True)
                spart[i, A_SKIP : A_SKIP + 1, lanes(t)] = jnp.sum(skip_sum[t], axis=0, keepdims=True)
        late["za"] = [
            send(spart.at[toward[d], pl.ds(0, A_ROWS)], srecv.at[d - 1], lines[d]) for d in (1, 2, 3)
        ]

    def shares():
        late["gwz"] = share(1, wg_out.at[1, :, chans])
        for copy in late["za"]:
            copy.wait_recv()
        sfull[c] = spart[z, 0:A_ROWS, :] + srecv[0] + srecv[1] + srecv[2]
        late["ga"] = [send(sfull.at[c], sfull.at[c], peers[p]) for p in (3, 1, 2)]

    second_sum = plane_sum(full2, [small_a, finish_early, finish_z, shares])

    pg = slope

    def pre_grad(i, carry):
        mixg = full2[i]
        back_x = dot(mixg, xp[...])
        new = []
        for t in tiles:
            v = (gsum[t, blk(i), :] + back_x[:, lanes(t)]) * pg[t, blk(i), :]
            pg[t, blk(i), :] = v
            mine = segp[at8(PAD + i * rb, rb), :]
            new.append(carry[5 * t] + jnp.sum(v.reshape(rb // SUB, SUB, LANES), axis=0))
            for j in range(4):
                window = inner[t, at8(PAD + i * rb - j * SUB, rb), :]
                if j:
                    window = jnp.where(segp[at8(PAD + i * rb - j * SUB, rb), :] == mine, window, 0.0)
                new.append(carry[5 * t + 1 + j] + jnp.sum((v * window).reshape(rb // SUB, SUB, LANES), axis=0))
        return tuple(new)

    conv_sum = lax.fori_loop(0, nblk, pre_grad, (zero,) * 10)
    for t in tiles:
        for j in range(3):
            pg[t, total + j * SUB : total + (j + 1) * SUB, :] = from_after(pg[t, j * SUB : (j + 1) * SUB, :], 0.0)

    mixv = jnp.concatenate([full2[i] for i in range(nblk)], axis=0)
    actv = jnp.concatenate([tiles_bf(act, i) for i in range(nblk)], axis=0)
    gx = dot_tn(mixv, actv)
    for i in range(4):
        conv_rows = [
            jnp.concatenate([jnp.sum(conv_sum[5 * t + j], axis=0, keepdims=True) for t in tiles], axis=1)
            for j in (4, 3, 2, 1, 0)
        ]
        bpart[i] = jnp.concatenate(
            [gx[i * 24 : i * 24 + 24, :]] + conv_rows + [jnp.zeros((3, wide), F32)], axis=0
        ).astype(BF16)
    z_b = [send(bpart.at[toward[d]], brecv.at[d - 1], lines[d]) for d in (1, 2, 3)]

    def inner_grad(i):
        for t in tiles:
            mine = segp[at8(PAD + i * rb, rb), :]
            v = pg[t, blk(i), :] * param(CONVW + 3, t)
            for j in range(1, 4):
                later = pg[t, at8(i * rb + j * SUB, rb), :]
                same = segp[at8(PAD + i * rb + j * SUB, rb), :] == mine
                v = v + jnp.where(same, later, 0.0) * param(CONVW + 3 - j, t)
            dsum[t, blk(i), :] = v

    loop(nblk, inner_grad)
    permute_out(dsum, gnat)
    flush(z_wo)
    z_wx = weight_grad(0, gnat, xf)

    flush(late["so"][1:] + branch_b)
    late["so"][0].wait()
    norm_a = start_rows(
        [gnat, znat], lambda rows, cols: dot_nt(rows[0], w_s[0, cols, :]) + dot_nt(rows[1], w_s[1, cols, :])
    )

    norm_b = middle_rows(norm_a)

    for copy in z_b:
        copy.wait_recv()
    v = bpart[z].astype(F32)
    for d in range(3):
        v = v + brecv[d].astype(F32)
    bfull[c] = v.astype(BF16)
    g_b = [send(bfull.at[c], bfull.at[c], peers[p]) for p in (3, 1, 2)]

    v = owned_grad(0, z_wx).T
    gres[0] = v.astype(BF16)
    v = late["gain"] + v * w_s[0, zrows, :].astype(F32)
    v = v[:, :LANES] + v[:, LANES:]
    for b in range(block // LANES):
        col = v[b * LANES : (b + 1) * LANES, :].T
        ggs[0, :, lanes(b)] = jnp.broadcast_to(jnp.sum(col, axis=0, keepdims=True), (SUB, LANES))
    s_gain = [send(ggs.at[0], ggs.at[p], peers[p]) for p in (1, 2, 3)]
    s_gain += [send(ggs.at[0], ggs.at[3 + p], (z, plane[p], 1 - k)) for p in (1, 2, 3)]
    s_gain.append(send(ggs.at[0], ggs.at[7], sib))

    late["gwx"] = share(0, wg_out.at[0, :, chans])

    ng = end_rows(norm_b)
    xv = x_half[...].astype(F32)
    r = lax.rsqrt(jnp.mean(xv * xv, axis=1, keepdims=True) + EPS)
    sg = ng * gain_row
    sg_s[...] = (
        og_half[...].astype(F32) + r * sg - xv * (r * r * r) * jnp.mean(sg * xv, axis=1, keepdims=True)
    )
    last = [local(sg_s, sg_out.at[half_rows, :]), send(sg_s, sg_out.at[half_rows, :], sib)]

    for copy in late["ga"] + g_b:
        copy.wait_recv()
    for i in range(4):
        cols = slice(i * wide, (i + 1) * wide)
        sm_out[0:24, cols] = bfull[i, B_XP : B_XP + 24, :].astype(F32)
        sm_out[24:44, cols] = sfull[i, A_DTW : A_ALOG + 4, :]
    cv_out[0:5, :] = bfull[z, B_CONVW : B_CONVB + 1, :].astype(F32)
    cv_out[5:7, :] = sfull[z, A_DTB : A_SKIP + 1, :]
    for copy in s_gain:
        copy.wait_recv()
    v = ggs[0]
    for i in range(1, 8):
        v = v + ggs[i]
    gg_out[...] = v[0:1, :] / pk_f[z, GAIN : GAIN + 1, :]

    late["so"][1].wait_recv()
    for name in ("gwo", "gwz", "gwx"):
        late[name][0].wait()
        for copy in late[name][1:]:
            copy.wait_recv()
    last[0].wait()
    last[1].wait_recv()
    flush(list(pending))


def fused(
    stream_in, norm_gain, in_weight, out_weight, xproj_weight, dt_weight, a_log, convolution_weight,
    convolution_bias, step_size_bias, skip_term_scale, seg_ids, pad_mask, out_grad,
):
    _, tok, width = stream_in.shape
    wide = 2 * LANES
    total = 4 * tok
    block = width // 4
    states = 4 * a_log.shape[0]
    vm = pl.BlockSpec(memory_space=pltpu.VMEM)
    hbm = pl.BlockSpec(memory_space=pl.ANY)
    f, b = (lambda *s: pltpu.VMEM(s, F32)), (lambda *s: pltpu.VMEM(s, BF16))
    scan = f(2, total, LANES)
    scratch = dict(
        x_half=b(tok // 2, width), og_half=b(tok // 2, width), xf=b(total, width), mg=b(total, width), w_s=b(2, width, wide), wo_s=b(wide, width),
        pk_f=f(4, ROWS, wide), pk_s=b(4, ROWS, wide), segs=pltpu.VMEM((4, SUB, tok), jnp.int32),
        segp=f(total + 2 * PAD, LANES), maskc=f(tok, LANES), nat=scan, inner=f(2, total + PAD, LANES),
        slope=f(2, total + PAD, LANES), act=scan, gate=scan, dt=scan, yg=scan, y=scan,
        bc=f(2 * states, total, LANES), h=f(2, states, total + SUB, LANES), a2b=f(2, states, SUB, LANES),
        st=f(2, states, SUB, LANES), gin=f(2, states, SUB, LANES), cum=f(2, SUB, LANES), alg=f(states, wide),
        full=b(8, 128, LANES), full2=b(8, 128, LANES), mp=f(8, 128, LANES), sum_a=b(4, 128, LANES),
        recv_a=f(4, 128, LANES), recv_b=b(3, 128, LANES), xp=b(LANES, wide), dtwp=b(LANES, wide),
        big_send=b(4, tok // 2, width), big_keep=b(4, tok // 2, width),
        big_recv=b(4, tok // 2, width), big_rb=b(3, tok // 2, width), gpart=b(2, wide, width),
        zrecv=b(3, 3, wide, block), gres=b(3, block, wide), gnat=b(total, wide), znat=b(total, wide),
        spart=f(4, ROWS, wide), srecv=f(3, A_ROWS, wide), sfull=f(4, A_ROWS, wide),
        bpart=b(4, B_ROWS, wide), brecv=b(3, B_ROWS, wide), bfull=b(4, B_ROWS, wide), sown=f(ROWS, wide),
        ggs=f(8, SUB, block), sg_s=f(tok // 2, width),
        ssem=pltpu.SemaphoreType.DMA((112,)), rsem=pltpu.SemaphoreType.DMA((112,)),
        lsem=pltpu.SemaphoreType.DMA((12,)),
    )
    outs = pl.pallas_call(
        fused_kernel,
        out_shape=[
            jax.ShapeDtypeStruct((tok, width), BF16),
            jax.ShapeDtypeStruct((tok, width), F32),
            jax.ShapeDtypeStruct((2, block, 4 * wide), BF16),
            jax.ShapeDtypeStruct((4 * wide, block), BF16),
            jax.ShapeDtypeStruct((48, 4 * wide), F32),
            jax.ShapeDtypeStruct((8, wide), F32),
            jax.ShapeDtypeStruct((1, block), F32),
        ],
        in_specs=[hbm] * 4 + [vm] * 10,
        out_specs=[hbm] * 4 + [vm] * 3,
        scratch_shapes=list(scratch.values()),
        compiler_params=pltpu.CompilerParams(
            collective_id=0, has_side_effects=True, vmem_limit_bytes=VMEM_LIMIT
        ),
    )(
        stream_in.reshape(tok, width), out_grad.reshape(tok, width), in_weight, out_weight, xproj_weight,
        dt_weight, a_log, convolution_weight.reshape(4, block), convolution_bias, step_size_bias,
        skip_term_scale, norm_gain, seg_ids, pad_mask,
    )
    steps = 2
    part = tok // steps

    def whole(*shape):
        return pl.BlockSpec(shape, lambda i: (0,) * len(shape))

    return pl.pallas_call(
        finish_kernel,
        grid=(steps,),
        out_shape=[
            jax.ShapeDtypeStruct((1, tok, width), BF16),
            jax.ShapeDtypeStruct((1, tok, width), F32),
            jax.ShapeDtypeStruct((block,), F32),
            jax.ShapeDtypeStruct((2, block, 4 * wide), F32),
            jax.ShapeDtypeStruct((4 * wide, block), F32),
            jax.ShapeDtypeStruct((24, 4 * wide), F32),
            jax.ShapeDtypeStruct((16, 4 * wide), F32),
            jax.ShapeDtypeStruct((4, 4 * wide), F32),
            jax.ShapeDtypeStruct((4, 1, wide), F32),
            jax.ShapeDtypeStruct((1, wide), F32),
            jax.ShapeDtypeStruct((1, wide), F32),
            jax.ShapeDtypeStruct((1, wide), F32),
        ],
        in_specs=[
            pl.BlockSpec((part, width), lambda i: (i, 0)),
            pl.BlockSpec((part, width), lambda i: (i, 0)),
            pl.BlockSpec((2, block // steps, 4 * wide), lambda i: (0, i, 0)),
            pl.BlockSpec((4 * wide // steps, block), lambda i: (i, 0)),
            whole(48, 4 * wide),
            whole(8, wide),
            whole(1, block),
        ],
        out_specs=[
            pl.BlockSpec((1, part, width), lambda i: (0, i, 0)),
            pl.BlockSpec((1, part, width), lambda i: (0, i, 0)),
            whole(block),
            pl.BlockSpec((2, block // steps, 4 * wide), lambda i: (0, i, 0)),
            pl.BlockSpec((4 * wide // steps, block), lambda i: (i, 0)),
            whole(24, 4 * wide),
            whole(16, 4 * wide),
            whole(4, 4 * wide),
            whole(4, 1, wide),
            whole(1, wide),
            whole(1, wide),
            whole(1, wide),
        ],
        compiler_params=pltpu.CompilerParams(vmem_limit_bytes=VMEM_LIMIT),
    )(*outs)


def finish_kernel(
    so_ref, sg_ref, wg_ref, wo_ref, sm_ref, cv_ref, gg_ref,
    so_out, sg_out, gg_out, wg_out, wo_out, xp_out, dtw_out, alog_out, cw_out, cb_out, dtb_out, skip_out,
):
    so_out[0] = so_ref[...]
    sg_out[0] = sg_ref[...]
    wg_out[...] = wg_ref[...].astype(F32)
    wo_out[...] = wo_ref[...].astype(F32)

    @pl.when(pl.program_id(0) == 0)
    def _():
        gg_out[...] = gg_ref[0]
        xp_out[...] = sm_ref[0:24, :]
        dtw_out[...] = sm_ref[24:40, :]
        alog_out[...] = sm_ref[40:44, :]
        for j in range(4):
            cw_out[j] = cv_ref[j : j + 1, :]
        cb_out[...] = cv_ref[4:5, :]
        dtb_out[...] = cv_ref[5:6, :]
        skip_out[...] = cv_ref[6:7, :]


def solution(mesh):
    in_specs = (
        P("dp", "ctx", None),
        P("dp"),
        P(None, "dp", "tp"),
        P("tp", "dp"),
        P("dp", "tp"),
        P("dp", "tp"),
        P("dp", "tp"),
        P(None, "tp", "dp"),
        P("tp", "dp"),
        P("tp", "dp"),
        P("tp", "dp"),
        P("dp", "ctx"),
        P("dp", "ctx"),
        P("dp", "ctx", None),
    )
    out_specs = (
        P("dp", "ctx", None),
        P("dp", "ctx", None),
        P("dp"),
        P(None, "dp", "tp"),
        P("tp", "dp"),
        P("dp", "tp"),
        P("dp", "tp"),
        P("dp", "tp"),
        P(None, "tp", "dp"),
        P("tp", "dp"),
        P("tp", "dp"),
        P("tp", "dp"),
    )

    def run(*args):
        stream, weight = args[0].shape, args[2].shape
        plane_fits = (mesh.shape["dp"], mesh.shape["ctx"], mesh.shape["tp"]) == (4, 4, 2)
        sizes_fit = stream == (4, 1024, 1024) and weight == (2, 1024, 2048)
        part = fused if plane_fits and sizes_fit else shards
        return jax.shard_map(
            part, mesh=mesh, in_specs=in_specs, out_specs=out_specs, check_vma=False
        )(*args)

    return run
```

```python
import math

import jax
import jax.numpy as jnp
from jax import lax
from jax.experimental import pallas as pl
from jax.experimental.pallas import tpu as pltpu
from jax.sharding import PartitionSpec as P

EPS = 1e-05
VMEM_LIMIT = 63 * 2**20


def from_behind(x, axis, by):
    count = lax.axis_size(axis)
    pairs = [(i, i + by) for i in range(count) if 0 <= i + by < count]
    return lax.ppermute(x, axis, pairs)


def entering(x, axis, combine, identity, reverse):
    count, position = (lax.axis_size(axis), lax.axis_index(axis))
    everything = jax.tree.map(
        lambda part, kind: lax.all_gather(part.astype(kind), axis), x, (jnp.bfloat16, jnp.bfloat16)
    )
    start = jax.tree.map(
        lambda part, zero: jnp.broadcast_to(jnp.asarray(zero, part.dtype), part.shape), x, identity
    )

    def step(k, before):
        at = count - 1 - k if reverse else k
        reached = at > position if reverse else at < position
        new = combine(
            before, jax.tree.map(lambda part, own: part[at].astype(own.dtype), everything, x)
        )
        return jax.tree.map(lambda a, b: jnp.where(reached, a, b), new, before)

    return lax.fori_loop(0, count, step, start)


def silu_slope(value):
    sigma = jax.nn.sigmoid(value)
    return sigma * (1.0 + value * (1.0 - sigma))


def link(first, second):
    return (first[0] * second[0], first[1] * second[0] + second[1])


def chain_prefix(decay, drive, backward):
    return lax.associative_scan(link, (decay, drive), reverse=backward, axis=1)


def shards(
    stream_in,
    norm_gain,
    in_weight,
    out_weight,
    xproj_weight,
    dt_weight,
    a_log,
    convolution_weight,
    convolution_bias,
    step_size_bias,
    skip_term_scale,
    seg_ids,
    pad_mask,
    out_grad,
):
    gathered = (
        lax.all_gather(norm_gain, "dp", axis=0, tiled=True),
        lax.all_gather(in_weight, "dp", axis=1, tiled=True),
        lax.all_gather(out_weight, "dp", axis=1, tiled=True),
        lax.all_gather(xproj_weight, "dp", axis=0, tiled=True),
        lax.all_gather(dt_weight, "dp", axis=0, tiled=True),
        lax.all_gather(a_log, "dp", axis=0, tiled=True),
        lax.all_gather(convolution_weight, "dp", axis=2, tiled=True),
        lax.all_gather(convolution_bias, "dp", axis=1, tiled=True),
        lax.all_gather(step_size_bias, "dp", axis=1, tiled=True),
        lax.all_gather(skip_term_scale, "dp", axis=1, tiled=True),
    )
    (
        gain_full,
        win_full,
        wout_full,
        xproj_full,
        dtw_full,
        alog_full,
        convw_full,
        convb_full,
        dtb_full,
        skip_full,
    ) = gathered
    seq_count, tok_count, model_width = stream_in.shape
    channels = win_full.shape[2]
    low_dims = dtw_full.shape[0]
    states = alog_full.shape[0]
    kernel = convw_full.shape[0]
    conv_lag = kernel - 1
    row_count = seq_count * tok_count
    block_len = math.gcd(tok_count, 128)
    block_count = tok_count // block_len
    gain_vec = gain_full.astype(jnp.float32)
    conv_taps = convw_full.reshape(kernel, channels).astype(jnp.float32)
    conv_shift = convb_full.reshape(channels).astype(jnp.float32)
    dt_shift = dtb_full.reshape(channels).astype(jnp.float32)
    skip_vec = skip_full.reshape(channels).astype(jnp.float32)
    a_neg = -jnp.exp(alog_full.astype(jnp.float32))

    def to_blocks(array):
        shaped = array.reshape((seq_count, block_count, block_len) + array.shape[2:])
        return jnp.moveaxis(shaped, 1, 0)

    def from_blocks(array):
        return jnp.moveaxis(array, 0, 1).reshape((seq_count, tok_count) + array.shape[3:])

    def decay_of(dt_block, keep_block):
        return jnp.exp(dt_block[:, :, None, :] * a_neg) * keep_block[:, :, None, None]

    def drive_of(dt_block, act_block, b_block):
        return (dt_block * act_block)[:, :, None, :] * b_block[:, :, :, None]

    def reverse_terms(decay, rhs, carry_in):
        shifted = jnp.concatenate([decay[:, 1:], jnp.zeros_like(decay[:, :1])], axis=1)
        rhs = rhs.at[:, -1].add(carry_in)
        _, grads = chain_prefix(shifted, rhs, True)
        return (grads, decay[:, 0] * grads[:, 0])

    stream = stream_in.astype(jnp.float32)
    rstd = lax.rsqrt(jnp.mean(stream * stream, axis=2, keepdims=True) + EPS)
    normed = (stream * rstd * gain_vec).astype(jnp.bfloat16)
    normed_flat = normed.reshape(row_count, model_width)
    projected = jnp.einsum(
        "rd,kdc->krc", normed_flat, win_full, preferred_element_type=jnp.float32
    ).astype(jnp.bfloat16)
    inner = projected[0].reshape(seq_count, tok_count, channels)
    gate_vals = projected[1].astype(jnp.float32).reshape(seq_count, tok_count, channels)
    seg_low = seg_ids.astype(jnp.bfloat16)
    prev_inner, prev_seg = from_behind(
        (inner[:, tok_count - conv_lag :], seg_low[:, tok_count - conv_lag :]), "ctx", 1
    )
    inner_vals = inner.astype(jnp.float32)
    prev_vals = prev_inner.astype(jnp.float32)
    seg_float = seg_ids.astype(jnp.float32)
    prev_segf = prev_seg.astype(jnp.float32)
    windows = []
    same_list = []
    pre = jnp.zeros((seq_count, tok_count, channels), jnp.float32) + conv_shift
    for offset in range(kernel):
        if offset == 0:
            window = inner_vals
            seg_window = seg_float
        else:
            window = jnp.concatenate(
                [prev_vals[:, conv_lag - offset :], inner_vals[:, : tok_count - offset]], axis=1
            )
            seg_window = jnp.concatenate(
                [prev_segf[:, conv_lag - offset :], seg_float[:, : tok_count - offset]], axis=1
            )
        same = (seg_window == seg_float).astype(jnp.float32)
        windows.append(window)
        same_list.append(same)
        pre = pre + conv_taps[conv_lag - offset] * window * same[:, :, None]
    keep = same_list[1]
    act = (pre * jax.nn.sigmoid(pre)).astype(jnp.bfloat16)
    act_flat = act.reshape(row_count, channels)
    act_vals = act.astype(jnp.float32)
    mixed_part = jnp.einsum("rc,wc->rw", act_flat, xproj_full, preferred_element_type=jnp.float32)
    mixed = lax.psum(mixed_part, "tp")
    low_rank = mixed[:, :low_dims].astype(jnp.bfloat16)
    b_in = mixed[:, low_dims : low_dims + states].reshape(seq_count, tok_count, states)
    c_out = mixed[:, low_dims + states :].reshape(seq_count, tok_count, states)
    dt_arg = (
        jnp.dot(low_rank, dtw_full, preferred_element_type=jnp.float32).reshape(
            seq_count, tok_count, channels
        )
        + dt_shift
    )
    dt_values = jax.nn.softplus(dt_arg)

    def forward_block(carry, piece):
        start, through = carry
        dt_block, act_block, b_block, c_block, keep_block = piece
        decay = decay_of(dt_block, keep_block)
        prods, local = chain_prefix(decay, drive_of(dt_block, act_block, b_block), False)
        hidden = local + prods * start[:, None]
        outputs = jnp.sum(c_block[:, :, :, None] * hidden, axis=2)
        return ((hidden[:, -1], through * prods[:, -1]), (outputs, start, through))

    zero_state = jnp.zeros((seq_count, states, channels), jnp.float32)
    one_state = jnp.ones_like(zero_state)
    dt_blocks = to_blocks(dt_values)
    act_blocks = to_blocks(act_vals)
    b_blocks = to_blocks(b_in)
    c_blocks = to_blocks(c_out)
    keep_blocks = to_blocks(keep)
    (last_state, through), (y_blocks, local_starts, befores) = lax.scan(
        forward_block,
        (zero_state, one_state),
        (dt_blocks, act_blocks, b_blocks, c_blocks, keep_blocks),
    )
    _, entry_state = entering((through, last_state), "ctx", link, (one_state, zero_state), False)
    cum_dt = jnp.cumsum(dt_values, axis=1)
    alive = jnp.cumprod(keep, axis=1)
    cum_blocks = to_blocks(cum_dt)

    def correct(piece):
        cum_block, c_block, alive_block = piece
        carried = jnp.exp(cum_block[:, :, None, :] * a_neg) * entry_state[:, None]
        return alive_block[:, :, None] * jnp.sum(c_block[:, :, :, None] * carried, axis=2)

    corrections = from_blocks(lax.map(correct, (cum_blocks, c_blocks, to_blocks(alive))))
    y_total = from_blocks(y_blocks) + corrections + skip_vec * act_vals
    gate_act = gate_vals * jax.nn.sigmoid(gate_vals)
    gated_flat = (y_total * gate_act).astype(jnp.bfloat16).reshape(row_count, channels)
    branch_part = jnp.dot(gated_flat, wout_full, preferred_element_type=jnp.float32)
    branch = (
        lax.psum(branch_part.astype(jnp.bfloat16), "tp")
        .astype(jnp.float32)
        .reshape(seq_count, tok_count, model_width)
    )
    mask_float = pad_mask.astype(jnp.float32)
    stream_out = (stream + mask_float[:, :, None] * branch).astype(jnp.bfloat16)
    masked_flat = (out_grad * pad_mask[:, :, None].astype(jnp.bfloat16)).reshape(
        row_count, model_width
    )
    grad_wout = jnp.einsum("rc,rd->cd", gated_flat, masked_flat, preferred_element_type=jnp.float32)
    grad_gated = jnp.einsum(
        "rd,cd->rc", masked_flat, wout_full, preferred_element_type=jnp.float32
    ).reshape(seq_count, tok_count, channels)
    grad_y = grad_gated * gate_act
    grad_gate = (grad_gated * y_total * silu_slope(gate_vals)).astype(jnp.bfloat16)
    grad_skip = jnp.sum(grad_y * act_vals, axis=(0, 1))
    gy_blocks = to_blocks(grad_y)
    true_starts = local_starts + befores * entry_state[None]

    def back_core(carry_in, piece):
        dt_block, act_block, b_block, c_block, keep_block, gy_block, start = piece
        decay = decay_of(dt_block, keep_block)
        prods, local = chain_prefix(decay, drive_of(dt_block, act_block, b_block), False)
        hidden = local + prods * start[:, None]
        earlier = jnp.concatenate([start[:, None], hidden[:, :-1]], axis=1)
        grads, carry_out = reverse_terms(
            decay, c_block[:, :, :, None] * gy_block[:, :, None, :], carry_in
        )
        stepped = earlier * decay
        weighted = grads * stepped
        along_b = jnp.sum(grads * b_block[:, :, :, None], axis=2)
        grad_dt = jnp.sum(weighted * a_neg, axis=2) + along_b * act_block
        grad_act = along_b * dt_block
        grad_b = jnp.sum(grads * (dt_block * act_block)[:, :, None, :], axis=3)
        grad_c = jnp.sum(gy_block[:, :, None, :] * hidden, axis=3)
        return (carry_out, weighted, stepped, (grad_dt, grad_act, grad_b, grad_c))

    back_pieces = (dt_blocks, act_blocks, b_blocks, c_blocks, keep_blocks, gy_blocks, true_starts)
    zero_acc = jnp.zeros((states, channels), jnp.float32)
    cum_end = cum_dt[:, -1]
    suffix = jnp.flip(jnp.cumprod(jnp.flip(keep, axis=1), axis=1), axis=1)
    rest = jnp.concatenate([suffix[:, 1:], jnp.ones((seq_count, 1), jnp.float32)], axis=1)
    rest_blocks = to_blocks(rest)

    def reach_of(cum_block, rest_block):
        return (
            jnp.exp((cum_end[:, None, None, :] - cum_block[:, :, None, :]) * a_neg)
            * rest_block[:, :, None, None]
        )

    def kept_back(carry, piece):
        carry_in, a_acc, q_acc = carry
        core_piece = piece[:7]
        carry_out, weighted, stepped, terms = back_core(carry_in, core_piece)
        dt_block = core_piece[0]
        along = stepped * reach_of(piece[7], piece[8])
        a_acc = a_acc + jnp.sum(weighted * dt_block[:, :, None, :], axis=(0, 1))
        q_acc = q_acc + jnp.sum(along * dt_block[:, :, None, :], axis=1)
        return ((carry_out, a_acc, q_acc), terms + (along,))

    (edge_grad, a_local, q_total), (base_dt, base_act, base_b, grad_c_blocks, along_blocks) = (
        lax.scan(
            kept_back,
            (zero_state, zero_acc, zero_state),
            back_pieces + (cum_blocks, rest_blocks),
            reverse=True,
        )
    )
    _, after_grad = entering((through, edge_grad), "ctx", link, (one_state, zero_state), True)

    def adjust(piece):
        dt_block, act_block, b_block, cum_block, rest_block, along = piece
        extra = reach_of(cum_block, rest_block) * after_grad[:, None]
        along_b = jnp.sum(extra * b_block[:, :, :, None], axis=2)
        grad_dt = jnp.sum(along * after_grad[:, None] * a_neg, axis=2) + along_b * act_block
        grad_act = along_b * dt_block
        grad_b = jnp.sum(extra * (dt_block * act_block)[:, :, None, :], axis=3)
        return (grad_dt, grad_act, grad_b)

    add_dt, add_act, add_b = lax.map(
        adjust, (dt_blocks, act_blocks, b_blocks, cum_blocks, rest_blocks, along_blocks)
    )
    grad_dt_blocks = base_dt + add_dt
    grad_act_blocks = base_act + add_act
    grad_b_blocks = base_b + add_b
    a_total = a_local + jnp.sum(q_total * after_grad, axis=0)
    grad_lin = from_blocks(grad_dt_blocks) * jax.nn.sigmoid(dt_arg)
    grad_dtb = jnp.sum(grad_lin, axis=(0, 1))
    grad_lin_low = grad_lin.reshape(row_count, channels).astype(jnp.bfloat16)
    grad_dtw = jnp.einsum("rk,rc->kc", low_rank, grad_lin_low, preferred_element_type=jnp.float32)
    grad_rank = jnp.einsum("rc,kc->rk", grad_lin_low, dtw_full, preferred_element_type=jnp.float32)
    grad_mixed_part = jnp.concatenate(
        [
            grad_rank,
            from_blocks(grad_b_blocks).reshape(row_count, states),
            from_blocks(grad_c_blocks).reshape(row_count, states),
        ],
        axis=1,
    )
    grad_mixed = lax.psum(grad_mixed_part, "tp").astype(jnp.bfloat16)
    grad_xproj = jnp.einsum("rw,rc->wc", grad_mixed, act_flat, preferred_element_type=jnp.float32)
    grad_act_total = (
        grad_y * skip_vec
        + from_blocks(grad_act_blocks)
        + jnp.dot(grad_mixed, xproj_full, preferred_element_type=jnp.float32).reshape(
            seq_count, tok_count, channels
        )
    )
    grad_pre = grad_act_total * silu_slope(pre)
    grad_convb = jnp.sum(grad_pre, axis=(0, 1))
    tap_grads = [None] * kernel
    grad_inner = jnp.zeros((seq_count, tok_count, channels), jnp.float32)
    tail_grad = jnp.zeros((seq_count, conv_lag, channels), jnp.float32)
    for offset in range(kernel):
        weighted_pre = grad_pre * same_list[offset][:, :, None]
        tap_grads[conv_lag - offset] = jnp.sum(weighted_pre * windows[offset], axis=(0, 1))
        scaled_pre = weighted_pre * conv_taps[conv_lag - offset]
        if offset == 0:
            grad_inner = grad_inner + scaled_pre
        else:
            grad_inner = grad_inner + jnp.concatenate(
                [scaled_pre[:, offset:], jnp.zeros((seq_count, offset, channels), jnp.float32)],
                axis=1,
            )
            tail_grad = tail_grad.at[:, conv_lag - offset :].add(scaled_pre[:, :offset])
    grad_convw = jnp.stack(tap_grads)
    sent_back = from_behind(tail_grad, "ctx", -1)
    grad_inner = grad_inner.at[:, tok_count - conv_lag :].add(sent_back)
    grad_proj = jnp.stack(
        [
            grad_inner.astype(jnp.bfloat16).reshape(row_count, channels),
            grad_gate.reshape(row_count, channels),
        ]
    )
    grad_win = jnp.einsum("rd,krc->kdc", normed_flat, grad_proj, preferred_element_type=jnp.float32)
    grad_norm_part = jnp.einsum(
        "krc,kdc->rd", grad_proj, win_full, preferred_element_type=jnp.float32
    )
    grad_norm = lax.psum(grad_norm_part, "tp").reshape(seq_count, tok_count, model_width)
    grad_gain = jnp.sum(grad_norm * stream * rstd, axis=(0, 1))
    scaled = grad_norm * gain_vec
    stream_grad = (
        out_grad.astype(jnp.float32)
        + rstd * scaled
        - stream * (rstd * rstd * rstd) * jnp.mean(scaled * stream, axis=2, keepdims=True)
    )
    grad_alog = a_total * a_neg
    local_grads = (
        grad_gain,
        grad_win,
        grad_wout,
        grad_xproj,
        grad_dtw,
        grad_alog,
        grad_convw.reshape(kernel, 1, channels),
        grad_convb.reshape(1, channels),
        grad_dtb.reshape(1, channels),
        grad_skip.reshape(1, channels),
    )
    summed = lax.psum(
        (
            local_grads[0],
            local_grads[1],
            local_grads[2],
            local_grads[3],
            local_grads[4],
            local_grads[5],
            local_grads[6],
            local_grads[7],
            local_grads[8],
            local_grads[9],
        ),
        "ctx",
    )
    owned = (
        lax.psum_scatter(summed[0], "dp", scatter_dimension=0, tiled=True),
        lax.psum_scatter(summed[1], "dp", scatter_dimension=1, tiled=True),
        lax.psum_scatter(summed[2], "dp", scatter_dimension=1, tiled=True),
        lax.psum_scatter(summed[3], "dp", scatter_dimension=0, tiled=True),
        lax.psum_scatter(summed[4], "dp", scatter_dimension=0, tiled=True),
        lax.psum_scatter(summed[5], "dp", scatter_dimension=0, tiled=True),
        lax.psum_scatter(summed[6], "dp", scatter_dimension=2, tiled=True),
        lax.psum_scatter(summed[7], "dp", scatter_dimension=1, tiled=True),
        lax.psum_scatter(summed[8], "dp", scatter_dimension=1, tiled=True),
        lax.psum_scatter(summed[9], "dp", scatter_dimension=1, tiled=True),
    )
    return (
        stream_out,
        stream_grad,
        owned[0],
        owned[1],
        owned[2],
        owned[3],
        owned[4],
        owned[5],
        owned[6],
        owned[7],
        owned[8],
        owned[9],
    )


F32 = jnp.float32
BF16 = jnp.bfloat16
MESH = pl.DeviceIdType.MESH
LOG2E = math.log2(math.e)
LN2 = math.log(2.0)
KILL = 1e30
SUB = 8
LANES = 128
PAD = 24
ROWS = 64
XP, DTW, ALOG, ROWS_P = 0, 24, 40, 48
CONVW, CONVB, DTB, SKIP, GAIN = 0, 4, 5, 6, 7
A_DTW, A_ALOG, A_DTB, A_SKIP, A_ROWS = 0, 16, 20, 21, 24
B_XP, B_CONVW, B_CONVB, B_ROWS = 0, 24, 28, 32
NT = (((1,), (1,)), ((), ()))
TN = (((0,), (0,)), ((), ()))


def dot(a, b):
    return jnp.dot(a, b, preferred_element_type=F32)


def dot_nt(a, b):
    return lax.dot_general(a, b, NT, preferred_element_type=F32)


def dot_tn(a, b):
    return lax.dot_general(a, b, TN, preferred_element_type=F32)


def at8(start, size):
    return pl.ds(pl.multiple_of(start, 8), size)


def sigmoid(v):
    return 0.5 + 0.5 * jnp.tanh(0.5 * v)


def log_one_plus(v):
    series = v * (1.0 - v * (0.5 - v * (1.0 / 3.0 - v * 0.25)))
    return jnp.where(v < 0.01, series, jnp.log(1.0 + v))


def one_less_exp(v):
    series = v * (1.0 - v * (0.5 - v * (1.0 / 6.0 - v * (1.0 / 24.0 - v * (1.0 / 120.0)))))
    return jnp.where(v < 0.1, series, 1.0 - jnp.exp(-v))


def prefix_of(ends, prods):
    row = lax.broadcasted_iota(jnp.int32, ends.shape, 0)
    for gap in (1, 2, 4):
        ok = row >= gap
        ends = ends + prods * jnp.where(ok, pltpu.roll(ends, gap, 0), 0.0)
        prods = prods * jnp.where(ok, pltpu.roll(prods, gap, 0), 1.0)
    return jnp.where(row >= 1, pltpu.roll(ends, 1, 0), 0.0)


def suffix_of(ends, prods):
    row = lax.broadcasted_iota(jnp.int32, ends.shape, 0)
    for gap in (1, 2, 4):
        ok = row < SUB - gap
        ends = ends + prods * jnp.where(ok, pltpu.roll(ends, SUB - gap, 0), 0.0)
        prods = prods * jnp.where(ok, pltpu.roll(prods, SUB - gap, 0), 1.0)
    return jnp.where(row < SUB - 1, pltpu.roll(ends, SUB - 1, 0), 0.0)


def fused_kernel(
    x_ref, og_ref, win_ref, wout_ref, xproj_ref, dtw_ref, alog_ref, convw_ref, convb_ref, dtb_ref,
    skip_ref, gain_ref, seg_ref, mask_ref,
    so_out, sg_out, wg_out, wo_out, sm_out, cv_out, gg_out,
    x_half, og_half, xf, mg, w_s, wo_s, early, pk_f, pk_s, segs, segp, maskc, nat, inner, slope, act, gate, dt, yg, y,
    bc, h, a2b, st, gin, cum, alg, full, full2, mp, sum_a, recv_a, recv_b, xp, dtwp,
    big_send, big_keep, big_recv, big_rb, gpart, zrecv, gres, gnat, znat, spart, srecv, sfull, bpart, brecv, bfull, sown, ggs,
    sg_s, ssem, rsem, lsem,
):
    z, c, k = lax.axis_index("dp"), lax.axis_index("ctx"), lax.axis_index("tp")
    nz = lax.axis_size("dp")
    px, py = lax.rem(c, 2), c // 2
    sib = (z, c, 1 - k)
    plane = [None, py * 2 + (1 - px), (1 - py) * 2 + px, (1 - py) * 2 + (1 - px)]
    peers = [None] + [(z, plane[p], k) for p in (1, 2, 3)]
    toward = [None] + [lax.rem(z + d, nz) for d in (1, 2, 3)]
    behind = [None] + [lax.rem(z + nz - d, nz) for d in (1, 2, 3)]
    lines = [None] + [(toward[d], c, k) for d in (1, 2, 3)]
    count = [0]
    local_count = [0]
    pending = []

    def send(src, dst, device):
        i = count[0]
        count[0] += 1
        copy = pltpu.make_async_remote_copy(
            src_ref=src, dst_ref=dst, send_sem=ssem.at[i], recv_sem=rsem.at[i],
            device_id=device, device_id_type=MESH,
        )
        copy.start()
        pending.append(copy)
        return copy

    def local(src, dst):
        i = local_count[0]
        local_count[0] += 1
        copy = pltpu.make_async_copy(src, dst, lsem.at[i])
        copy.start()
        return copy

    def flush(copies):
        for copy in copies:
            copy.wait_send()
            pending[:] = [other for other in pending if other is not copy]

    tok = maskc.shape[0]
    half = tok // 2
    total = xf.shape[0]
    width = xf.shape[1]
    steps = total // SUB
    states = h.shape[1]
    wide = 2 * LANES
    block = w_s.shape[1] // 4
    tiles = (0, 1)
    rb = 128
    nblk = total // rb

    def lanes(t):
        return slice(t * LANES, (t + 1) * LANES)

    def blk(i):
        return pl.ds(pl.multiple_of(i * rb, rb), rb)

    wb = 512

    def wide_blk(i):
        return pl.ds(pl.multiple_of(i * wb, wb), wb)

    def tau_rows(tau):
        return at8(tau * SUB, SUB)

    def loop(n, body, unroll=1):
        def step(i, carry):
            body(i)
            return carry

        lax.fori_loop(0, n, step, 0, unroll=unroll)

    barrier = pltpu.get_barrier_semaphore()
    everyone = [sib] + peers[1:] + [(z, plane[p], 1 - k) for p in (1, 2, 3)] + lines[1:]
    for device in everyone:
        pl.semaphore_signal(barrier, inc=1, device_id=device, device_id_type=MESH)
    chans = pl.ds(pl.multiple_of(c * wide, wide), wide)
    spart[...] = jnp.zeros_like(spart)
    spart[0, XP : XP + 24, :] = xproj_ref[:, chans].astype(F32)
    spart[0, DTW : DTW + 16, :] = dtw_ref[:, chans].astype(F32)
    spart[0, ALOG : ALOG + 4, :] = alog_ref[:, chans].astype(F32)
    early[z, CONVW : CONVW + 4, :] = convw_ref[...].astype(F32)
    early[z, CONVB : CONVB + 1, :] = convb_ref[...].astype(F32)
    early[z, DTB : DTB + 1, :] = dtb_ref[...].astype(F32)
    early[z, SKIP : SKIP + 1, :] = skip_ref[...].astype(F32)
    early[z, GAIN : GAIN + 1, :] = gain_ref[...].astype(F32).reshape(1, block)
    pk_s[z] = spart[0, 0:ROWS_P, :].astype(BF16)
    segs[c] = jnp.broadcast_to(seg_ref[...], (SUB, tok))
    pl.semaphore_wait(barrier, len(everyone))

    s_early = [send(early.at[z], early.at[z], lines[d]) for d in (1, 2, 3)]
    s_seg = [send(segs.at[c], segs.at[c], peers[p]) for p in (1, 2, 3)]
    my_half = pl.ds(pl.multiple_of(c * tok + k * half, half), half)
    s_x = [send(x_ref.at[pl.ds(pl.multiple_of(k * half, half), half)], xf.at[my_half], peers[p]) for p in (3, 1, 2)]

    zrows = pl.ds(pl.multiple_of(z * block, block), block)

    def weight(which):
        return [
            send(win_ref.at[which, :, chans], w_s.at[which, zrows, :], lines[d]) for d in (1, 2, 3)
        ]

    s_wx = weight(0)
    s_pack = [send(pk_s.at[z], pk_s.at[z], lines[d]) for d in (1, 2, 3)]
    own_w = [local(win_ref.at[i, :, chans], w_s.at[i, zrows, :]) for i in (0, 1)]
    zcols = pl.ds(pl.multiple_of(z * block, block), block)
    own_wo = local(wout_ref.at[chans, :], wo_s.at[:, zcols])

    own_rows = pl.ds(pl.multiple_of(c * tok, tok), tok)
    half_rows = pl.ds(pl.multiple_of(k * half, half), half)
    own_x = local(x_ref, xf.at[own_rows, :])
    own_og = local(og_ref, mg.at[own_rows, :])
    own_half = [local(x_ref.at[half_rows, :], x_half), local(og_ref.at[half_rows, :], og_half)]
    mrow = mask_ref[...].astype(F32)
    for b in range(tok // LANES):
        rows = slice(b * LANES, (b + 1) * LANES)
        maskc[rows, :] = jnp.broadcast_to(mrow[:, rows], (LANES, LANES)).T
    mcol = jnp.concatenate([maskc[...]] * (width // LANES), axis=1)
    own_og.wait()
    mg[own_rows, :] = (mg[own_rows, :].astype(F32) * mcol).astype(BF16)

    for copy in s_early:
        copy.wait_recv()
    gain_row = jnp.concatenate([early[i, GAIN : GAIN + 1, :] for i in range(4)], axis=1)
    sown[...] = early[c]

    def param(row, t):
        return sown[row : row + 1, lanes(t)]

    for copy in s_seg:
        copy.wait_recv()
    for i in range(4):
        srow = segs[i, 0:1, :].astype(F32)
        for b in range(tok // LANES):
            rows = slice(b * LANES, (b + 1) * LANES)
            nat[0, i * tok + b * LANES : i * tok + (b + 1) * LANES, :] = jnp.broadcast_to(
                srow[:, rows], (LANES, LANES)
            ).T

    def seg_in(tau):
        segp[at8(PAD + tau * SUB, SUB), :] = nat[0, pl.ds(tau, SUB, stride=steps), :]

    loop(steps, seg_in, 8)
    sub_row = lax.broadcasted_iota(jnp.int32, (SUB, LANES), 0)

    def from_before(v, fill):
        return jnp.where(sub_row >= 1, pltpu.roll(v, 1, 0), fill)

    def from_after(v, fill):
        return jnp.where(sub_row < SUB - 1, pltpu.roll(v, SUB - 1, 0), fill)

    for j in range(3):
        segp[j * SUB : (j + 1) * SUB, :] = from_before(segp[total + j * SUB : total + (j + 1) * SUB, :], -1.0)
        segp[PAD + total + j * SUB : PAD + total + (j + 1) * SUB, :] = from_after(
            segp[PAD + j * SUB : PAD + (j + 1) * SUB, :], -2.0
        )

    def halves(copies, buf):
        relays = []
        for copy, p in zip(copies, (3, 1, 2)):
            copy.wait_recv()
            rows = pl.ds(pl.multiple_of(plane[p] * tok + k * half, half), half)
            relays.append(send(buf.at[rows], buf.at[rows], sib))
        return relays

    def norm(i):
        rows = pl.ds(pl.multiple_of(i * rb, rb), rb)
        v = xf[rows, :].astype(F32)
        r = lax.rsqrt(jnp.mean(v * v, axis=1, keepdims=True) + EPS)
        xf[rows, :] = (v * r * gain_row).astype(BF16)

    def project_block(i):
        rows = pl.ds(pl.multiple_of(i * tok, tok), tok)
        v = dot(xf[rows, :], w_s[0])
        for t in tiles:
            nat[t, rows, :] = v[:, lanes(t)]

    per = tok // rb
    own_x.wait()
    loop(per, lambda i: norm(c * per + i))
    r_x = halves(s_x, xf)
    for copy in s_wx:
        copy.wait_recv()
    own_w[0].wait()
    s_wz = weight(1)
    project_block(c)
    for copy, sent, p in zip(r_x, s_x, (3, 1, 2)):
        copy.wait_recv()
        flush([copy])
        loop(per, lambda i, p=p: norm(plane[p] * per + i))
        project_block(plane[p])

    def project(which, dst, off):
        def body(i):
            v = dot(xf[wide_blk(i), :], w_s[which])
            for t in tiles:
                nat[t, wide_blk(i), :] = v[:, lanes(t)]

        loop(total // wb, body)
        permute_in(dst, off, True)

    def permute_in(dst, off, rounded=False):
        def body(tau):
            for t in tiles:
                v = nat[t, pl.ds(tau, SUB, stride=steps), :]
                dst[t, at8(off + tau * SUB, SUB), :] = v.astype(BF16).astype(F32) if rounded else v

        loop(steps, body, 8)

    def permute_out(src, dst):
        def body(i):
            for s in range(SUB):
                for t in tiles:
                    nat[t, at8(s * steps + i * SUB, SUB), :] = src[t, pl.ds(i * SUB * SUB + s, SUB, stride=SUB), :]

        loop(steps // SUB, body)

        def cast(i):
            dst[blk(i), :] = jnp.concatenate([nat[t, blk(i), :] for t in tiles], axis=1).astype(BF16)

        loop(nblk, cast)

    permute_in(inner, PAD, True)
    for t in tiles:
        for j in range(3):
            inner[t, j * SUB : (j + 1) * SUB, :] = from_before(inner[t, total + j * SUB : total + (j + 1) * SUB, :], 0.0)

    def conv(i):
        for t in tiles:
            mine = segp[at8(PAD + i * rb, rb), :]
            pre = jnp.zeros((rb, LANES), F32) + param(CONVB, t)
            for j in range(4):
                window = inner[t, at8(PAD + i * rb - j * SUB, rb), :]
                if j:
                    window = jnp.where(segp[at8(PAD + i * rb - j * SUB, rb), :] == mine, window, 0.0)
                pre = pre + param(CONVW + 3 - j, t) * window
            s = sigmoid(pre)
            act[t, blk(i), :] = (pre * s).astype(BF16).astype(F32)
            slope[t, blk(i), :] = s * (1.0 + pre * (1.0 - s))

    loop(nblk, conv)

    def tiles_bf(ref, i):
        return jnp.concatenate([ref[t, blk(i), :] for t in tiles], axis=1).astype(BF16)

    for copy in s_pack:
        copy.wait_recv()
    for i in range(4):
        pk_f[i] = pk_s[i].astype(F32)
    for i in range(4):
        alg[4 * i : 4 * i + 4, :] = pk_f[i, ALOG : ALOG + 4, :]
    xp_rows = jnp.concatenate([pk_f[i, XP : XP + 24, :] for i in range(4)] + [jnp.zeros((32, wide), F32)], axis=0)
    xp[...] = xp_rows.astype(BF16)
    dt_rows = jnp.concatenate([pk_f[i, DTW : DTW + 16, :] for i in range(4)] + [jnp.zeros((64, wide), F32)], axis=0)
    dtwp[...] = dt_rows.astype(BF16)
    a2v = -jnp.exp(alg[...]) * LOG2E
    for n in range(states):
        for t in tiles:
            a2b[t, n] = jnp.broadcast_to(a2v[n : n + 1, lanes(t)], (SUB, LANES))

    def mix(i):
        mp[i] = dot_nt(tiles_bf(act, i), xp[...])

    loop(nblk, mix)

    def plane_sum(out, between):
        first = send(mp.at[pl.ds((1 - k) * 4, 4)], recv_a, sib)
        between[0]()
        first.wait_recv()
        for i in range(4):
            sum_a[i] = (mp[k * 4 + i] + recv_a[i]).astype(BF16)
        second = [send(sum_a.at[plane[p]], recv_b.at[p - 1], peers[p]) for p in (3, 1, 2)]
        between[1]()
        for copy in second:
            copy.wait_recv()
        mine = k * 4 + c
        v = mp[mine] + recv_a[c]
        for p in range(3):
            v = v + recv_b[p].astype(F32)
        out[mine] = v.astype(BF16)
        third = [send(out.at[mine], out.at[mine], peers[p]) for p in (3, 1, 2)]
        third.append(send(out.at[mine], out.at[mine], sib))
        between[2]()
        fourth = []
        for copy, p in zip(third, (3, 1, 2)):
            copy.wait_recv()
            there = k * 4 + plane[p]
            fourth.append(send(out.at[there], out.at[there], sib))
        between[3]()
        for copy in [third[3]] + fourth:
            copy.wait_recv()
        return [first] + second

    late = {}

    def send_wo():
        for copy in s_wz:
            copy.wait_recv()
        own_w[1].wait()
        late["wo"] = [send(wout_ref.at[chans, :], wo_s.at[:, zcols], lines[d]) for d in (1, 2, 3)]

    def gates():
        project(1, gate, 0)

    def nothing():
        pass

    def send_mg():
        late["mg"] = [send(mg.at[my_half], mg.at[my_half], peers[p]) for p in (3, 1, 2)]

    def gap():
        send_mg()
        send_wo()
        gates()

    first_sum = plane_sum(full, [nothing, nothing, nothing, gap])

    def steps_of(i):
        arg = dot(full[i], dtwp[...])
        for t in tiles:
            v = arg[:, lanes(t)] + param(DTB, t)
            dt[t, blk(i), :] = jnp.maximum(v, 0.0) + log_one_plus(jnp.exp(-jnp.abs(v)))

    loop(nblk, steps_of)

    flat = full[...].reshape(total, LANES)
    row = lax.broadcasted_iota(jnp.int32, (LANES, wide), 0)
    col = lax.broadcasted_iota(jnp.int32, (LANES, wide), 1) // LANES
    for n in range(0, 2 * states, 2):
        v = dot(flat, jnp.where(row == 64 + n + col, 1.0, 0.0).astype(BF16))
        for t in tiles:
            bc[n + t] = v[:, lanes(t)]

    def dts(t, tau):
        v = dt[t, tau_rows(tau), :]
        r = at8(PAD + tau * SUB, SUB)
        p = at8(PAD + tau * SUB - SUB, SUB)
        return v, jnp.where(segp[r, :] == segp[p, :], v, KILL)

    for t in tiles:

        def ends(tau, carry, t=t):
            v, killed = dts(t, tau)
            drive = v * act[t, tau_rows(tau), :]
            new = [
                carry[n] * jnp.exp2(killed * a2b[t, n]) + drive * bc[n, tau_rows(tau), :] for n in range(states)
            ]
            return tuple(new) + (carry[states] + killed,)

        zero = jnp.zeros((SUB, LANES), F32)
        got = lax.fori_loop(0, steps, ends, (zero,) * (states + 1), unroll=4)
        cum[t] = got[states]
        for n in range(states):
            st[t, n] = prefix_of(got[n], jnp.exp2(got[states] * a2b[t, n]))

    for t in tiles:
        if t:
            late["mg"] = halves(late["mg"], mg)
        for n in range(states):
            h[t, n, 0:SUB, :] = st[t, n]

        def forward(tau, carry, t=t):
            v, killed = dts(t, tau)
            drive = v * act[t, tau_rows(tau), :]
            new, parts = [], [None] * 4
            for n in range(states):
                s = carry[n] * jnp.exp2(killed * a2b[t, n]) + drive * bc[n, tau_rows(tau), :]
                h[t, n, at8(tau * SUB + SUB, SUB), :] = s
                o = s * bc[states + n, tau_rows(tau), :]
                parts[n % 4] = o if parts[n % 4] is None else parts[n % 4] + o
                new.append(s)
            y[t, tau_rows(tau), :] = (parts[0] + parts[1]) + (parts[2] + parts[3])
            return tuple(new)

        lax.fori_loop(0, steps, forward, tuple(st[t, n] for n in range(states)), unroll=4)

    for copy in late["mg"] + late["wo"]:
        copy.wait_recv()
    own_wo.wait()

    def ograd(i):
        v = dot_nt(mg[wide_blk(i), :], wo_s[...])
        for t in tiles:
            nat[t, wide_blk(i), :] = v[:, lanes(t)]

    loop(total // wb, ograd)
    gb = SUB * SUB

    def strided(t, i):
        return jnp.concatenate([nat[t, pl.ds(i * SUB + u, SUB, stride=steps), :] for u in range(SUB)], axis=0)

    def gating(i, carry):
        new = []
        rows = pl.ds(pl.multiple_of(i * gb, gb), gb)
        for t in tiles:
            gv, ov, av = gate[t, rows, :], strided(t, i), act[t, rows, :]
            s = sigmoid(gv)
            ytot = y[t, rows, :] + param(SKIP, t) * av
            gy = ov * (gv * s)
            yg[t, rows, :] = gy
            y[t, rows, :] = ytot * (gv * s)
            gate[t, rows, :] = ov * ytot * (s * (1.0 + gv * (1.0 - s)))
            new.append(carry[t] + jnp.sum((gy * av).reshape(SUB, SUB, LANES), axis=0))
        return tuple(new)

    zero = jnp.zeros((SUB, LANES), F32)
    skip_sum = lax.fori_loop(0, total // gb, gating, (zero, zero))
    permute_out(y, gnat)
    permute_out(gate, znat)

    def owner_rows(i, q):
        return pl.ds(pl.multiple_of(i * tok + q * half, half), half)

    order = (3, 1, 2, 0)
    groups = width // wide

    def fill(dst, j, q, lefts, right):
        cols = slice(j * wide, (j + 1) * wide)
        there = [plane[p] if p else c for p in order]
        rows = [jnp.concatenate([left[owner_rows(i, q), :] for i in there], axis=0) for left in lefts]
        v = right(rows, cols)
        for i, p in enumerate(order):
            dst[p, :, cols] = v[i * half : (i + 1) * half, :].astype(BF16)

    def start_rows(lefts, right):
        first = []
        for j in range(groups):
            cols = slice(j * wide, (j + 1) * wide)
            fill(big_send, j, 1 - k, lefts, right)
            first.append(send(big_send.at[:, :, cols], big_recv.at[:, :, cols], sib))
        return first

    def middle_rows(first, lefts=None, right=None):
        second = []
        for j in range(groups):
            cols = slice(j * wide, (j + 1) * wide)
            if lefts:
                fill(big_keep, j, k, lefts, right)
            first[j].wait_recv()
            for p in order:
                big_keep[p, :, cols] = (big_keep[p, :, cols].astype(F32) + big_recv[p, :, cols].astype(F32)).astype(BF16)
                if p:
                    second.append(send(big_keep.at[p, :, cols], big_rb.at[p - 1, :, cols], peers[p]))
        return second

    def end_rows(second):
        for copy in second:
            copy.wait_recv()
        v = big_keep[0].astype(F32)
        for p in range(3):
            v = v + big_rb[p].astype(F32)
        return v

    def branch_part(rows, cols):
        return dot(rows[0], wo_s[:, cols])

    branch_a = start_rows([gnat], branch_part)
    for j in range(groups):
        fill(big_keep, j, k, [gnat], branch_part)

    def weight_grad(slot, left, right):
        gpart[slot % 2] = dot_tn(left[...], right[...]).astype(BF16)

    def spread_grad(slot):
        return [
            send(
                gpart.at[slot % 2, :, pl.ds(pl.multiple_of(toward[d] * block, block), block)],
                zrecv.at[slot, d - 1],
                lines[d],
            )
            for d in (1, 2, 3)
        ]

    def owned_grad(slot, copies):
        for copy in copies:
            copy.wait_recv()
        v = gpart[slot % 2, :, zcols].astype(F32)
        for d in range(3):
            v = v + zrecv[slot, d].astype(F32)
        return v

    def share(slot, dst):
        return [local(gres.at[slot], dst)] + [send(gres.at[slot], dst, peers[p]) for p in (3, 1, 2)]

    weight_grad(2, gnat, mg)
    z_wo = spread_grad(2)
    weight_grad(1, znat, xf)

    for t in tiles:
        if t:
            branch_b = middle_rows(branch_a)

        def back_ends(i, carry, t=t):
            tau = steps - 1 - i
            _, killed = dts(t, tau)
            gy = yg[t, tau_rows(tau), :]
            return tuple(
                (carry[n] + gy * bc[states + n, tau_rows(tau), :]) * jnp.exp2(killed * a2b[t, n])
                for n in range(states)
            )

        got = lax.fori_loop(0, steps, back_ends, (zero,) * states, unroll=4)
        for n in range(states):
            gin[t, n] = suffix_of(got[n], jnp.exp2(cum[t] * a2b[t, n]))

    flush(branch_a)
    so_s = big_send.at[0]

    gsum, dsum = gate, y
    part = states // 2
    for lo in (0, part):
        names = list(range(lo, lo + part))
        if lo:
            z_wz = spread_grad(1)

        def back(i, carry, names=names, lo=lo):
            grads, acc = carry
            tau = steps - 1 - i
            r = tau_rows(tau)
            pair = [dts(t, tau) for t in tiles]
            drive = [pair[t][0] * act[t, r, :] for t in tiles]
            gy = [yg[t, r, :] for t in tiles]
            along = [None, None]
            down = [None, None]
            new_g, new_a = [], []
            for q, n in enumerate(names):
                bv, cv = bc[n, r, :], bc[states + n, r, :]
                pb = pc = None
                for t in tiles:
                    a2 = a2b[t, n]
                    decay = jnp.exp2(pair[t][1] * a2)
                    g = grads[2 * q + t] + gy[t] * cv
                    gb = g * bv
                    along[t] = gb if along[t] is None else along[t] + gb
                    v = g * drive[t]
                    pb = v if pb is None else pb + v
                    v = gy[t] * h[t, n, at8(tau * SUB + SUB, SUB), :]
                    pc = v if pc is None else pc + v
                    gd = g * decay
                    dla = gd * h[t, n, r, :]
                    v = dla * a2
                    down[t] = v if down[t] is None else down[t] + v
                    new_a.append(acc[2 * q + t] + dla * pair[t][0])
                    new_g.append(gd)
                bc[n, r, :] = pb
                bc[states + n, r, :] = pc
            for t in tiles:
                if lo == 0:
                    gsum[t, r, :] = along[t]
                    dsum[t, r, :] = down[t]
                else:
                    gsum[t, r, :] = gsum[t, r, :] + along[t]
                    dsum[t, r, :] = dsum[t, r, :] + down[t]
            return tuple(new_g), tuple(new_a)

        start = tuple(gin[t, n] for n in names for t in tiles)
        _, acc = lax.fori_loop(0, steps, back, (start, (zero,) * (2 * part)), unroll=2)
        for q, n in enumerate(names):
            for t in tiles:
                alg[n : n + 1, lanes(t)] = (
                    jnp.sum(acc[2 * q + t], axis=0, keepdims=True) * a2b[t, n][0:1, :] * LN2
                )

    gres[2] = owned_grad(2, z_wo).astype(BF16)
    late["gwo"] = share(2, wo_out.at[chans, :])

    def lin(i, carry):
        new = []
        rank = []
        for t in tiles:
            av, gv = act[t, blk(i), :], gsum[t, blk(i), :]
            v = (dsum[t, blk(i), :] * LN2 + av * gv) * one_less_exp(dt[t, blk(i), :])
            new.append(carry[t] + jnp.sum(v.reshape(rb // SUB, SUB, LANES), axis=0))
            low = v.astype(BF16)
            rank.append(low)
            dsum[t, blk(i), :] = low.astype(F32)
            gsum[t, blk(i), :] = dt[t, blk(i), :] * gv + param(SKIP, t) * yg[t, blk(i), :]
        mp[i] = dot_nt(jnp.concatenate(rank, axis=1), dtwp[...])
        return tuple(new)

    flush(first_sum)
    dtb_sum = lax.fori_loop(0, nblk, lin, (zero, zero))

    beside = lax.broadcasted_iota(jnp.int32, (wide, LANES), 1) - 64
    beside = beside - lax.broadcasted_iota(jnp.int32, (wide, LANES), 0) // LANES

    def collect(i):
        rows = pl.ds(pl.multiple_of(i * 2 * rb, 2 * rb), 2 * rb)
        v = jnp.concatenate([mp[2 * i], mp[2 * i + 1]], axis=0)
        for n in range(0, 2 * states, 2):
            pick = jnp.where(beside == n, 1.0, 0.0).astype(BF16)
            pair = jnp.concatenate([bc[n, rows, :], bc[n + 1, rows, :]], axis=1).astype(BF16)
            v = v + dot(pair, pick)
        mp[2 * i] = v[:rb, :]
        mp[2 * i + 1] = v[rb:, :]

    loop(nblk // 2, collect)

    def finish_early():
        v = end_rows(branch_b)
        mk = jnp.concatenate([maskc[half_rows, :]] * (width // LANES), axis=1)
        for copy in own_half:
            copy.wait()
        so_s[...] = (x_half[...].astype(F32) + mk * v).astype(BF16)
        late["so"] = [local(so_s, so_out.at[half_rows, :]), send(so_s, so_out.at[half_rows, :], sib)]

    def finish_z():
        v = owned_grad(1, z_wz).T
        gres[1] = v.astype(BF16)
        v = v * w_s[1, zrows, :].astype(F32)
        late["gain"] = v[:, :LANES] + v[:, LANES:]

    def small_a():
        low = jnp.concatenate([full[i] for i in range(nblk)], axis=0)
        linv = jnp.concatenate([tiles_bf(dsum, i) for i in range(nblk)], axis=0)
        g = dot_tn(low, linv)
        for i in range(4):
            spart[i, A_DTW : A_DTW + 16, :] = g[i * 16 : i * 16 + 16, :]
            spart[i, A_ALOG : A_ALOG + 4, :] = alg[i * 4 : i * 4 + 4, :]
            for t in tiles:
                spart[i, A_DTB : A_DTB + 1, lanes(t)] = jnp.sum(dtb_sum[t], axis=0, keepdims=True)
                spart[i, A_SKIP : A_SKIP + 1, lanes(t)] = jnp.sum(skip_sum[t], axis=0, keepdims=True)
        late["za"] = [
            send(spart.at[toward[d], pl.ds(0, A_ROWS)], srecv.at[d - 1], lines[d]) for d in (1, 2, 3)
        ]

    def shares():
        late["gwz"] = share(1, wg_out.at[1, :, chans])
        for copy in late["za"]:
            copy.wait_recv()
        sfull[c] = spart[z, 0:A_ROWS, :] + srecv[0] + srecv[1] + srecv[2]
        late["ga"] = [send(sfull.at[c], sfull.at[c], peers[p]) for p in (3, 1, 2)]

    second_sum = plane_sum(full2, [small_a, finish_early, finish_z, shares])

    pg = slope

    def pre_grad(i, carry):
        mixg = full2[i]
        back_x = dot(mixg, xp[...])
        new = []
        for t in tiles:
            v = (gsum[t, blk(i), :] + back_x[:, lanes(t)]) * pg[t, blk(i), :]
            pg[t, blk(i), :] = v
            mine = segp[at8(PAD + i * rb, rb), :]
            new.append(carry[5 * t] + jnp.sum(v.reshape(rb // SUB, SUB, LANES), axis=0))
            for j in range(4):
                window = inner[t, at8(PAD + i * rb - j * SUB, rb), :]
                if j:
                    window = jnp.where(segp[at8(PAD + i * rb - j * SUB, rb), :] == mine, window, 0.0)
                new.append(carry[5 * t + 1 + j] + jnp.sum((v * window).reshape(rb // SUB, SUB, LANES), axis=0))
        return tuple(new)

    conv_sum = lax.fori_loop(0, nblk, pre_grad, (zero,) * 10)
    for t in tiles:
        for j in range(3):
            pg[t, total + j * SUB : total + (j + 1) * SUB, :] = from_after(pg[t, j * SUB : (j + 1) * SUB, :], 0.0)

    def inner_grad(i):
        for t in tiles:
            mine = segp[at8(PAD + i * rb, rb), :]
            v = pg[t, blk(i), :] * param(CONVW + 3, t)
            for j in range(1, 4):
                later = pg[t, at8(i * rb + j * SUB, rb), :]
                same = segp[at8(PAD + i * rb + j * SUB, rb), :] == mine
                v = v + jnp.where(same, later, 0.0) * param(CONVW + 3 - j, t)
            dsum[t, blk(i), :] = v

    loop(nblk, inner_grad)
    permute_out(dsum, gnat)
    flush(z_wo)
    z_wx = []
    for q in range(2):
        gpart[0, q * LANES : (q + 1) * LANES, :] = dot_tn(gnat[:, lanes(q)], xf[...]).astype(BF16)
        z_wx.append(
            [
                send(
                    gpart.at[0, pl.ds(q * LANES, LANES), pl.ds(pl.multiple_of(toward[d] * block, block), block)],
                    zrecv.at[0, d - 1, pl.ds(q * LANES, LANES)],
                    lines[d],
                )
                for d in (1, 2, 3)
            ]
        )

    flush(late["so"][1:] + branch_b)
    late["so"][0].wait()
    def norm_part(rows, cols):
        return dot_nt(rows[0], w_s[0, cols, :]) + dot_nt(rows[1], w_s[1, cols, :])

    norm_a = start_rows([gnat, znat], norm_part)
    mixv = jnp.concatenate([full2[i] for i in range(nblk)], axis=0)
    actv = jnp.concatenate([tiles_bf(act, i) for i in range(nblk)], axis=0)
    gx = dot_tn(mixv, actv)
    for i in range(4):
        conv_rows = [
            jnp.concatenate([jnp.sum(conv_sum[5 * t + j], axis=0, keepdims=True) for t in tiles], axis=1)
            for j in (4, 3, 2, 1, 0)
        ]
        bpart[i] = jnp.concatenate(
            [gx[i * 24 : i * 24 + 24, :]] + conv_rows + [jnp.zeros((3, wide), F32)], axis=0
        ).astype(BF16)
    z_b = [send(bpart.at[toward[d]], brecv.at[d - 1], lines[d]) for d in (1, 2, 3)]

    norm_b = middle_rows(norm_a, [gnat, znat], norm_part)
    gain_sum = late["gain"]
    late["gwx"] = [[], []]
    for q in range(2):
        for copy in z_wx[q]:
            copy.wait_recv()
        rows = slice(q * LANES, (q + 1) * LANES)
        v = gpart[0, rows, zcols].astype(F32)
        for d in range(3):
            v = v + zrecv[0, d, rows, :].astype(F32)
        v = v.T
        gres[0, :, rows] = v.astype(BF16)
        dst = wg_out.at[0, :, pl.ds(pl.multiple_of(c * wide + q * LANES, LANES), LANES)]
        got = [local(gres.at[0, :, rows], dst)] + [send(gres.at[0, :, rows], dst, peers[p]) for p in (3, 1, 2)]
        late["gwx"][0].append(got[0])
        late["gwx"][1].extend(got[1:])
        gain_sum = gain_sum + v * w_s[0, zrows, rows].astype(F32)
        if q == 0:
            for copy in z_b:
                copy.wait_recv()
            v = bpart[z].astype(F32)
            for d in range(3):
                v = v + brecv[d].astype(F32)
            bfull[c] = v.astype(BF16)
            g_b = [send(bfull.at[c], bfull.at[c], peers[p]) for p in (3, 1, 2)]
    for b in range(block // LANES):
        col = gain_sum[b * LANES : (b + 1) * LANES, :].T
        ggs[0, :, lanes(b)] = jnp.broadcast_to(jnp.sum(col, axis=0, keepdims=True), (SUB, LANES))
    s_gain = [send(ggs.at[0], ggs.at[p], peers[p]) for p in (1, 2, 3)]
    s_gain += [send(ggs.at[0], ggs.at[3 + p], (z, plane[p], 1 - k)) for p in (1, 2, 3)]
    s_gain.append(send(ggs.at[0], ggs.at[7], sib))

    ng = end_rows(norm_b)
    xv = x_half[...].astype(F32)
    r = lax.rsqrt(jnp.mean(xv * xv, axis=1, keepdims=True) + EPS)
    sg = ng * gain_row
    sg_s[...] = (
        og_half[...].astype(F32) + r * sg - xv * (r * r * r) * jnp.mean(sg * xv, axis=1, keepdims=True)
    )
    last = [local(sg_s, sg_out.at[half_rows, :]), send(sg_s, sg_out.at[half_rows, :], sib)]

    for copy in late["ga"] + g_b:
        copy.wait_recv()
    for i in range(4):
        cols = slice(i * wide, (i + 1) * wide)
        sm_out[0:24, cols] = bfull[i, B_XP : B_XP + 24, :].astype(F32)
        sm_out[24:44, cols] = sfull[i, A_DTW : A_ALOG + 4, :]
    cv_out[0:5, :] = bfull[z, B_CONVW : B_CONVB + 1, :].astype(F32)
    cv_out[5:7, :] = sfull[z, A_DTB : A_SKIP + 1, :]
    for copy in s_gain:
        copy.wait_recv()
    v = ggs[0]
    for i in range(1, 8):
        v = v + ggs[i]
    gg_out[...] = v[0:1, :] / early[z, GAIN : GAIN + 1, :]

    late["so"][1].wait_recv()
    for name in ("gwo", "gwz"):
        late[name][0].wait()
        for copy in late[name][1:]:
            copy.wait_recv()
    for copy in late["gwx"][0]:
        copy.wait()
    for copy in late["gwx"][1]:
        copy.wait_recv()
    last[0].wait()
    last[1].wait_recv()
    flush(list(pending))


def fused(
    stream_in, norm_gain, in_weight, out_weight, xproj_weight, dt_weight, a_log, convolution_weight,
    convolution_bias, step_size_bias, skip_term_scale, seg_ids, pad_mask, out_grad,
):
    _, tok, width = stream_in.shape
    wide = 2 * LANES
    total = 4 * tok
    block = width // 4
    states = 4 * a_log.shape[0]
    vm = pl.BlockSpec(memory_space=pltpu.VMEM)
    hbm = pl.BlockSpec(memory_space=pl.ANY)
    f, b = (lambda *s: pltpu.VMEM(s, F32)), (lambda *s: pltpu.VMEM(s, BF16))
    scan = f(2, total, LANES)
    scratch = dict(
        x_half=b(tok // 2, width), og_half=b(tok // 2, width), xf=b(total, width), mg=b(total, width), w_s=b(2, width, wide), wo_s=b(wide, width),
        early=f(4, SUB, wide), pk_f=f(4, ROWS_P, wide), pk_s=b(4, ROWS_P, wide), segs=pltpu.VMEM((4, SUB, tok), jnp.int32),
        segp=f(total + 2 * PAD, LANES), maskc=f(tok, LANES), nat=scan, inner=f(2, total + PAD, LANES),
        slope=f(2, total + PAD, LANES), act=scan, gate=scan, dt=scan, yg=scan, y=scan,
        bc=f(2 * states, total, LANES), h=f(2, states, total + SUB, LANES), a2b=f(2, states, SUB, LANES),
        st=f(2, states, SUB, LANES), gin=f(2, states, SUB, LANES), cum=f(2, SUB, LANES), alg=f(states, wide),
        full=b(8, 128, LANES), full2=b(8, 128, LANES), mp=f(8, 128, LANES), sum_a=b(4, 128, LANES),
        recv_a=f(4, 128, LANES), recv_b=b(3, 128, LANES), xp=b(LANES, wide), dtwp=b(LANES, wide),
        big_send=b(4, tok // 2, width), big_keep=b(4, tok // 2, width),
        big_recv=b(4, tok // 2, width), big_rb=b(3, tok // 2, width), gpart=b(2, wide, width),
        zrecv=b(3, 3, wide, block), gres=b(3, block, wide), gnat=b(total, wide), znat=b(total, wide),
        spart=f(4, ROWS, wide), srecv=f(3, A_ROWS, wide), sfull=f(4, A_ROWS, wide),
        bpart=b(4, B_ROWS, wide), brecv=b(3, B_ROWS, wide), bfull=b(4, B_ROWS, wide), sown=f(SUB, wide),
        ggs=f(8, SUB, block), sg_s=f(tok // 2, width),
        ssem=pltpu.SemaphoreType.DMA((144,)), rsem=pltpu.SemaphoreType.DMA((144,)),
        lsem=pltpu.SemaphoreType.DMA((16,)),
    )
    outs = pl.pallas_call(
        fused_kernel,
        out_shape=[
            jax.ShapeDtypeStruct((tok, width), BF16),
            jax.ShapeDtypeStruct((tok, width), F32),
            jax.ShapeDtypeStruct((2, block, 4 * wide), BF16),
            jax.ShapeDtypeStruct((4 * wide, block), BF16),
            jax.ShapeDtypeStruct((48, 4 * wide), F32),
            jax.ShapeDtypeStruct((8, wide), F32),
            jax.ShapeDtypeStruct((1, block), F32),
        ],
        in_specs=[hbm] * 4 + [vm] * 10,
        out_specs=[hbm] * 4 + [vm] * 3,
        scratch_shapes=list(scratch.values()),
        compiler_params=pltpu.CompilerParams(
            collective_id=0, has_side_effects=True, vmem_limit_bytes=VMEM_LIMIT
        ),
    )(
        stream_in.reshape(tok, width), out_grad.reshape(tok, width), in_weight, out_weight, xproj_weight,
        dt_weight, a_log, convolution_weight.reshape(4, block), convolution_bias, step_size_bias,
        skip_term_scale, norm_gain, seg_ids, pad_mask,
    )
    steps = 2
    part = tok // steps

    def whole(*shape):
        return pl.BlockSpec(shape, lambda i: (0,) * len(shape))

    return pl.pallas_call(
        finish_kernel,
        grid=(steps,),
        out_shape=[
            jax.ShapeDtypeStruct((1, tok, width), BF16),
            jax.ShapeDtypeStruct((1, tok, width), F32),
            jax.ShapeDtypeStruct((block,), F32),
            jax.ShapeDtypeStruct((2, block, 4 * wide), F32),
            jax.ShapeDtypeStruct((4 * wide, block), F32),
            jax.ShapeDtypeStruct((24, 4 * wide), F32),
            jax.ShapeDtypeStruct((16, 4 * wide), F32),
            jax.ShapeDtypeStruct((4, 4 * wide), F32),
            jax.ShapeDtypeStruct((4, 1, wide), F32),
            jax.ShapeDtypeStruct((1, wide), F32),
            jax.ShapeDtypeStruct((1, wide), F32),
            jax.ShapeDtypeStruct((1, wide), F32),
        ],
        in_specs=[
            pl.BlockSpec((part, width), lambda i: (i, 0)),
            pl.BlockSpec((part, width), lambda i: (i, 0)),
            pl.BlockSpec((2, block // steps, 4 * wide), lambda i: (0, i, 0)),
            pl.BlockSpec((4 * wide // steps, block), lambda i: (i, 0)),
            whole(48, 4 * wide),
            whole(8, wide),
            whole(1, block),
        ],
        out_specs=[
            pl.BlockSpec((1, part, width), lambda i: (0, i, 0)),
            pl.BlockSpec((1, part, width), lambda i: (0, i, 0)),
            whole(block),
            pl.BlockSpec((2, block // steps, 4 * wide), lambda i: (0, i, 0)),
            pl.BlockSpec((4 * wide // steps, block), lambda i: (i, 0)),
            whole(24, 4 * wide),
            whole(16, 4 * wide),
            whole(4, 4 * wide),
            whole(4, 1, wide),
            whole(1, wide),
            whole(1, wide),
            whole(1, wide),
        ],
        compiler_params=pltpu.CompilerParams(vmem_limit_bytes=VMEM_LIMIT),
    )(*outs)


def finish_kernel(
    so_ref, sg_ref, wg_ref, wo_ref, sm_ref, cv_ref, gg_ref,
    so_out, sg_out, gg_out, wg_out, wo_out, xp_out, dtw_out, alog_out, cw_out, cb_out, dtb_out, skip_out,
):
    so_out[0] = so_ref[...]
    sg_out[0] = sg_ref[...]
    wg_out[...] = wg_ref[...].astype(F32)
    wo_out[...] = wo_ref[...].astype(F32)

    @pl.when(pl.program_id(0) == 0)
    def _():
        gg_out[...] = gg_ref[0]
        xp_out[...] = sm_ref[0:24, :]
        dtw_out[...] = sm_ref[24:40, :]
        alog_out[...] = sm_ref[40:44, :]
        for j in range(4):
            cw_out[j] = cv_ref[j : j + 1, :]
        cb_out[...] = cv_ref[4:5, :]
        dtb_out[...] = cv_ref[5:6, :]
        skip_out[...] = cv_ref[6:7, :]


def solution(mesh):
    in_specs = (
        P("dp", "ctx", None),
        P("dp"),
        P(None, "dp", "tp"),
        P("tp", "dp"),
        P("dp", "tp"),
        P("dp", "tp"),
        P("dp", "tp"),
        P(None, "tp", "dp"),
        P("tp", "dp"),
        P("tp", "dp"),
        P("tp", "dp"),
        P("dp", "ctx"),
        P("dp", "ctx"),
        P("dp", "ctx", None),
    )
    out_specs = (
        P("dp", "ctx", None),
        P("dp", "ctx", None),
        P("dp"),
        P(None, "dp", "tp"),
        P("tp", "dp"),
        P("dp", "tp"),
        P("dp", "tp"),
        P("dp", "tp"),
        P(None, "tp", "dp"),
        P("tp", "dp"),
        P("tp", "dp"),
        P("tp", "dp"),
    )

    def run(*args):
        stream, weight = args[0].shape, args[2].shape
        plane_fits = (mesh.shape["dp"], mesh.shape["ctx"], mesh.shape["tp"]) == (4, 4, 2)
        sizes_fit = stream == (4, 1024, 1024) and weight == (2, 1024, 2048)
        part = fused if plane_fits and sizes_fit else shards
        return jax.shard_map(
            part, mesh=mesh, in_specs=in_specs, out_specs=out_specs, check_vma=False
        )(*args)

    return run
```

```python
import math

import jax
import jax.numpy as jnp
from jax import lax
from jax.experimental import pallas as pl
from jax.experimental.pallas import tpu as pltpu
from jax.sharding import PartitionSpec as P

EPS = 1e-05
VMEM_LIMIT = 63 * 2**20


def from_behind(x, axis, by):
    count = lax.axis_size(axis)
    pairs = [(i, i + by) for i in range(count) if 0 <= i + by < count]
    return lax.ppermute(x, axis, pairs)


def entering(x, axis, combine, identity, reverse):
    count, position = (lax.axis_size(axis), lax.axis_index(axis))
    everything = jax.tree.map(
        lambda part, kind: lax.all_gather(part.astype(kind), axis), x, (jnp.bfloat16, jnp.bfloat16)
    )
    start = jax.tree.map(
        lambda part, zero: jnp.broadcast_to(jnp.asarray(zero, part.dtype), part.shape), x, identity
    )

    def step(k, before):
        at = count - 1 - k if reverse else k
        reached = at > position if reverse else at < position
        new = combine(
            before, jax.tree.map(lambda part, own: part[at].astype(own.dtype), everything, x)
        )
        return jax.tree.map(lambda a, b: jnp.where(reached, a, b), new, before)

    return lax.fori_loop(0, count, step, start)


def silu_slope(value):
    sigma = jax.nn.sigmoid(value)
    return sigma * (1.0 + value * (1.0 - sigma))


def link(first, second):
    return (first[0] * second[0], first[1] * second[0] + second[1])


def chain_prefix(decay, drive, backward):
    return lax.associative_scan(link, (decay, drive), reverse=backward, axis=1)


def shards(
    stream_in,
    norm_gain,
    in_weight,
    out_weight,
    xproj_weight,
    dt_weight,
    a_log,
    convolution_weight,
    convolution_bias,
    step_size_bias,
    skip_term_scale,
    seg_ids,
    pad_mask,
    out_grad,
):
    gathered = (
        lax.all_gather(norm_gain, "dp", axis=0, tiled=True),
        lax.all_gather(in_weight, "dp", axis=1, tiled=True),
        lax.all_gather(out_weight, "dp", axis=1, tiled=True),
        lax.all_gather(xproj_weight, "dp", axis=0, tiled=True),
        lax.all_gather(dt_weight, "dp", axis=0, tiled=True),
        lax.all_gather(a_log, "dp", axis=0, tiled=True),
        lax.all_gather(convolution_weight, "dp", axis=2, tiled=True),
        lax.all_gather(convolution_bias, "dp", axis=1, tiled=True),
        lax.all_gather(step_size_bias, "dp", axis=1, tiled=True),
        lax.all_gather(skip_term_scale, "dp", axis=1, tiled=True),
    )
    (
        gain_full,
        win_full,
        wout_full,
        xproj_full,
        dtw_full,
        alog_full,
        convw_full,
        convb_full,
        dtb_full,
        skip_full,
    ) = gathered
    seq_count, tok_count, model_width = stream_in.shape
    channels = win_full.shape[2]
    low_dims = dtw_full.shape[0]
    states = alog_full.shape[0]
    kernel = convw_full.shape[0]
    conv_lag = kernel - 1
    row_count = seq_count * tok_count
    block_len = math.gcd(tok_count, 128)
    block_count = tok_count // block_len
    gain_vec = gain_full.astype(jnp.float32)
    conv_taps = convw_full.reshape(kernel, channels).astype(jnp.float32)
    conv_shift = convb_full.reshape(channels).astype(jnp.float32)
    dt_shift = dtb_full.reshape(channels).astype(jnp.float32)
    skip_vec = skip_full.reshape(channels).astype(jnp.float32)
    a_neg = -jnp.exp(alog_full.astype(jnp.float32))

    def to_blocks(array):
        shaped = array.reshape((seq_count, block_count, block_len) + array.shape[2:])
        return jnp.moveaxis(shaped, 1, 0)

    def from_blocks(array):
        return jnp.moveaxis(array, 0, 1).reshape((seq_count, tok_count) + array.shape[3:])

    def decay_of(dt_block, keep_block):
        return jnp.exp(dt_block[:, :, None, :] * a_neg) * keep_block[:, :, None, None]

    def drive_of(dt_block, act_block, b_block):
        return (dt_block * act_block)[:, :, None, :] * b_block[:, :, :, None]

    def reverse_terms(decay, rhs, carry_in):
        shifted = jnp.concatenate([decay[:, 1:], jnp.zeros_like(decay[:, :1])], axis=1)
        rhs = rhs.at[:, -1].add(carry_in)
        _, grads = chain_prefix(shifted, rhs, True)
        return (grads, decay[:, 0] * grads[:, 0])

    stream = stream_in.astype(jnp.float32)
    rstd = lax.rsqrt(jnp.mean(stream * stream, axis=2, keepdims=True) + EPS)
    normed = (stream * rstd * gain_vec).astype(jnp.bfloat16)
    normed_flat = normed.reshape(row_count, model_width)
    projected = jnp.einsum(
        "rd,kdc->krc", normed_flat, win_full, preferred_element_type=jnp.float32
    ).astype(jnp.bfloat16)
    inner = projected[0].reshape(seq_count, tok_count, channels)
    gate_vals = projected[1].astype(jnp.float32).reshape(seq_count, tok_count, channels)
    seg_low = seg_ids.astype(jnp.bfloat16)
    prev_inner, prev_seg = from_behind(
        (inner[:, tok_count - conv_lag :], seg_low[:, tok_count - conv_lag :]), "ctx", 1
    )
    inner_vals = inner.astype(jnp.float32)
    prev_vals = prev_inner.astype(jnp.float32)
    seg_float = seg_ids.astype(jnp.float32)
    prev_segf = prev_seg.astype(jnp.float32)
    windows = []
    same_list = []
    pre = jnp.zeros((seq_count, tok_count, channels), jnp.float32) + conv_shift
    for offset in range(kernel):
        if offset == 0:
            window = inner_vals
            seg_window = seg_float
        else:
            window = jnp.concatenate(
                [prev_vals[:, conv_lag - offset :], inner_vals[:, : tok_count - offset]], axis=1
            )
            seg_window = jnp.concatenate(
                [prev_segf[:, conv_lag - offset :], seg_float[:, : tok_count - offset]], axis=1
            )
        same = (seg_window == seg_float).astype(jnp.float32)
        windows.append(window)
        same_list.append(same)
        pre = pre + conv_taps[conv_lag - offset] * window * same[:, :, None]
    keep = same_list[1]
    act = (pre * jax.nn.sigmoid(pre)).astype(jnp.bfloat16)
    act_flat = act.reshape(row_count, channels)
    act_vals = act.astype(jnp.float32)
    mixed_part = jnp.einsum("rc,wc->rw", act_flat, xproj_full, preferred_element_type=jnp.float32)
    mixed = lax.psum(mixed_part, "tp")
    low_rank = mixed[:, :low_dims].astype(jnp.bfloat16)
    b_in = mixed[:, low_dims : low_dims + states].reshape(seq_count, tok_count, states)
    c_out = mixed[:, low_dims + states :].reshape(seq_count, tok_count, states)
    dt_arg = (
        jnp.dot(low_rank, dtw_full, preferred_element_type=jnp.float32).reshape(
            seq_count, tok_count, channels
        )
        + dt_shift
    )
    dt_values = jax.nn.softplus(dt_arg)

    def forward_block(carry, piece):
        start, through = carry
        dt_block, act_block, b_block, c_block, keep_block = piece
        decay = decay_of(dt_block, keep_block)
        prods, local = chain_prefix(decay, drive_of(dt_block, act_block, b_block), False)
        hidden = local + prods * start[:, None]
        outputs = jnp.sum(c_block[:, :, :, None] * hidden, axis=2)
        return ((hidden[:, -1], through * prods[:, -1]), (outputs, start, through))

    zero_state = jnp.zeros((seq_count, states, channels), jnp.float32)
    one_state = jnp.ones_like(zero_state)
    dt_blocks = to_blocks(dt_values)
    act_blocks = to_blocks(act_vals)
    b_blocks = to_blocks(b_in)
    c_blocks = to_blocks(c_out)
    keep_blocks = to_blocks(keep)
    (last_state, through), (y_blocks, local_starts, befores) = lax.scan(
        forward_block,
        (zero_state, one_state),
        (dt_blocks, act_blocks, b_blocks, c_blocks, keep_blocks),
    )
    _, entry_state = entering((through, last_state), "ctx", link, (one_state, zero_state), False)
    cum_dt = jnp.cumsum(dt_values, axis=1)
    alive = jnp.cumprod(keep, axis=1)
    cum_blocks = to_blocks(cum_dt)

    def correct(piece):
        cum_block, c_block, alive_block = piece
        carried = jnp.exp(cum_block[:, :, None, :] * a_neg) * entry_state[:, None]
        return alive_block[:, :, None] * jnp.sum(c_block[:, :, :, None] * carried, axis=2)

    corrections = from_blocks(lax.map(correct, (cum_blocks, c_blocks, to_blocks(alive))))
    y_total = from_blocks(y_blocks) + corrections + skip_vec * act_vals
    gate_act = gate_vals * jax.nn.sigmoid(gate_vals)
    gated_flat = (y_total * gate_act).astype(jnp.bfloat16).reshape(row_count, channels)
    branch_part = jnp.dot(gated_flat, wout_full, preferred_element_type=jnp.float32)
    branch = (
        lax.psum(branch_part.astype(jnp.bfloat16), "tp")
        .astype(jnp.float32)
        .reshape(seq_count, tok_count, model_width)
    )
    mask_float = pad_mask.astype(jnp.float32)
    stream_out = (stream + mask_float[:, :, None] * branch).astype(jnp.bfloat16)
    masked_flat = (out_grad * pad_mask[:, :, None].astype(jnp.bfloat16)).reshape(
        row_count, model_width
    )
    grad_wout = jnp.einsum("rc,rd->cd", gated_flat, masked_flat, preferred_element_type=jnp.float32)
    grad_gated = jnp.einsum(
        "rd,cd->rc", masked_flat, wout_full, preferred_element_type=jnp.float32
    ).reshape(seq_count, tok_count, channels)
    grad_y = grad_gated * gate_act
    grad_gate = (grad_gated * y_total * silu_slope(gate_vals)).astype(jnp.bfloat16)
    grad_skip = jnp.sum(grad_y * act_vals, axis=(0, 1))
    gy_blocks = to_blocks(grad_y)
    true_starts = local_starts + befores * entry_state[None]

    def back_core(carry_in, piece):
        dt_block, act_block, b_block, c_block, keep_block, gy_block, start = piece
        decay = decay_of(dt_block, keep_block)
        prods, local = chain_prefix(decay, drive_of(dt_block, act_block, b_block), False)
        hidden = local + prods * start[:, None]
        earlier = jnp.concatenate([start[:, None], hidden[:, :-1]], axis=1)
        grads, carry_out = reverse_terms(
            decay, c_block[:, :, :, None] * gy_block[:, :, None, :], carry_in
        )
        stepped = earlier * decay
        weighted = grads * stepped
        along_b = jnp.sum(grads * b_block[:, :, :, None], axis=2)
        grad_dt = jnp.sum(weighted * a_neg, axis=2) + along_b * act_block
        grad_act = along_b * dt_block
        grad_b = jnp.sum(grads * (dt_block * act_block)[:, :, None, :], axis=3)
        grad_c = jnp.sum(gy_block[:, :, None, :] * hidden, axis=3)
        return (carry_out, weighted, stepped, (grad_dt, grad_act, grad_b, grad_c))

    back_pieces = (dt_blocks, act_blocks, b_blocks, c_blocks, keep_blocks, gy_blocks, true_starts)
    zero_acc = jnp.zeros((states, channels), jnp.float32)
    cum_end = cum_dt[:, -1]
    suffix = jnp.flip(jnp.cumprod(jnp.flip(keep, axis=1), axis=1), axis=1)
    rest = jnp.concatenate([suffix[:, 1:], jnp.ones((seq_count, 1), jnp.float32)], axis=1)
    rest_blocks = to_blocks(rest)

    def reach_of(cum_block, rest_block):
        return (
            jnp.exp((cum_end[:, None, None, :] - cum_block[:, :, None, :]) * a_neg)
            * rest_block[:, :, None, None]
        )

    def kept_back(carry, piece):
        carry_in, a_acc, q_acc = carry
        core_piece = piece[:7]
        carry_out, weighted, stepped, terms = back_core(carry_in, core_piece)
        dt_block = core_piece[0]
        along = stepped * reach_of(piece[7], piece[8])
        a_acc = a_acc + jnp.sum(weighted * dt_block[:, :, None, :], axis=(0, 1))
        q_acc = q_acc + jnp.sum(along * dt_block[:, :, None, :], axis=1)
        return ((carry_out, a_acc, q_acc), terms + (along,))

    (edge_grad, a_local, q_total), (base_dt, base_act, base_b, grad_c_blocks, along_blocks) = (
        lax.scan(
            kept_back,
            (zero_state, zero_acc, zero_state),
            back_pieces + (cum_blocks, rest_blocks),
            reverse=True,
        )
    )
    _, after_grad = entering((through, edge_grad), "ctx", link, (one_state, zero_state), True)

    def adjust(piece):
        dt_block, act_block, b_block, cum_block, rest_block, along = piece
        extra = reach_of(cum_block, rest_block) * after_grad[:, None]
        along_b = jnp.sum(extra * b_block[:, :, :, None], axis=2)
        grad_dt = jnp.sum(along * after_grad[:, None] * a_neg, axis=2) + along_b * act_block
        grad_act = along_b * dt_block
        grad_b = jnp.sum(extra * (dt_block * act_block)[:, :, None, :], axis=3)
        return (grad_dt, grad_act, grad_b)

    add_dt, add_act, add_b = lax.map(
        adjust, (dt_blocks, act_blocks, b_blocks, cum_blocks, rest_blocks, along_blocks)
    )
    grad_dt_blocks = base_dt + add_dt
    grad_act_blocks = base_act + add_act
    grad_b_blocks = base_b + add_b
    a_total = a_local + jnp.sum(q_total * after_grad, axis=0)
    grad_lin = from_blocks(grad_dt_blocks) * jax.nn.sigmoid(dt_arg)
    grad_dtb = jnp.sum(grad_lin, axis=(0, 1))
    grad_lin_low = grad_lin.reshape(row_count, channels).astype(jnp.bfloat16)
    grad_dtw = jnp.einsum("rk,rc->kc", low_rank, grad_lin_low, preferred_element_type=jnp.float32)
    grad_rank = jnp.einsum("rc,kc->rk", grad_lin_low, dtw_full, preferred_element_type=jnp.float32)
    grad_mixed_part = jnp.concatenate(
        [
            grad_rank,
            from_blocks(grad_b_blocks).reshape(row_count, states),
            from_blocks(grad_c_blocks).reshape(row_count, states),
        ],
        axis=1,
    )
    grad_mixed = lax.psum(grad_mixed_part, "tp").astype(jnp.bfloat16)
    grad_xproj = jnp.einsum("rw,rc->wc", grad_mixed, act_flat, preferred_element_type=jnp.float32)
    grad_act_total = (
        grad_y * skip_vec
        + from_blocks(grad_act_blocks)
        + jnp.dot(grad_mixed, xproj_full, preferred_element_type=jnp.float32).reshape(
            seq_count, tok_count, channels
        )
    )
    grad_pre = grad_act_total * silu_slope(pre)
    grad_convb = jnp.sum(grad_pre, axis=(0, 1))
    tap_grads = [None] * kernel
    grad_inner = jnp.zeros((seq_count, tok_count, channels), jnp.float32)
    tail_grad = jnp.zeros((seq_count, conv_lag, channels), jnp.float32)
    for offset in range(kernel):
        weighted_pre = grad_pre * same_list[offset][:, :, None]
        tap_grads[conv_lag - offset] = jnp.sum(weighted_pre * windows[offset], axis=(0, 1))
        scaled_pre = weighted_pre * conv_taps[conv_lag - offset]
        if offset == 0:
            grad_inner = grad_inner + scaled_pre
        else:
            grad_inner = grad_inner + jnp.concatenate(
                [scaled_pre[:, offset:], jnp.zeros((seq_count, offset, channels), jnp.float32)],
                axis=1,
            )
            tail_grad = tail_grad.at[:, conv_lag - offset :].add(scaled_pre[:, :offset])
    grad_convw = jnp.stack(tap_grads)
    sent_back = from_behind(tail_grad, "ctx", -1)
    grad_inner = grad_inner.at[:, tok_count - conv_lag :].add(sent_back)
    grad_proj = jnp.stack(
        [
            grad_inner.astype(jnp.bfloat16).reshape(row_count, channels),
            grad_gate.reshape(row_count, channels),
        ]
    )
    grad_win = jnp.einsum("rd,krc->kdc", normed_flat, grad_proj, preferred_element_type=jnp.float32)
    grad_norm_part = jnp.einsum(
        "krc,kdc->rd", grad_proj, win_full, preferred_element_type=jnp.float32
    )
    grad_norm = lax.psum(grad_norm_part, "tp").reshape(seq_count, tok_count, model_width)
    grad_gain = jnp.sum(grad_norm * stream * rstd, axis=(0, 1))
    scaled = grad_norm * gain_vec
    stream_grad = (
        out_grad.astype(jnp.float32)
        + rstd * scaled
        - stream * (rstd * rstd * rstd) * jnp.mean(scaled * stream, axis=2, keepdims=True)
    )
    grad_alog = a_total * a_neg
    local_grads = (
        grad_gain,
        grad_win,
        grad_wout,
        grad_xproj,
        grad_dtw,
        grad_alog,
        grad_convw.reshape(kernel, 1, channels),
        grad_convb.reshape(1, channels),
        grad_dtb.reshape(1, channels),
        grad_skip.reshape(1, channels),
    )
    summed = lax.psum(
        (
            local_grads[0],
            local_grads[1],
            local_grads[2],
            local_grads[3],
            local_grads[4],
            local_grads[5],
            local_grads[6],
            local_grads[7],
            local_grads[8],
            local_grads[9],
        ),
        "ctx",
    )
    owned = (
        lax.psum_scatter(summed[0], "dp", scatter_dimension=0, tiled=True),
        lax.psum_scatter(summed[1], "dp", scatter_dimension=1, tiled=True),
        lax.psum_scatter(summed[2], "dp", scatter_dimension=1, tiled=True),
        lax.psum_scatter(summed[3], "dp", scatter_dimension=0, tiled=True),
        lax.psum_scatter(summed[4], "dp", scatter_dimension=0, tiled=True),
        lax.psum_scatter(summed[5], "dp", scatter_dimension=0, tiled=True),
        lax.psum_scatter(summed[6], "dp", scatter_dimension=2, tiled=True),
        lax.psum_scatter(summed[7], "dp", scatter_dimension=1, tiled=True),
        lax.psum_scatter(summed[8], "dp", scatter_dimension=1, tiled=True),
        lax.psum_scatter(summed[9], "dp", scatter_dimension=1, tiled=True),
    )
    return (
        stream_out,
        stream_grad,
        owned[0],
        owned[1],
        owned[2],
        owned[3],
        owned[4],
        owned[5],
        owned[6],
        owned[7],
        owned[8],
        owned[9],
    )


F32 = jnp.float32
BF16 = jnp.bfloat16
MESH = pl.DeviceIdType.MESH
LOG2E = math.log2(math.e)
LN2 = math.log(2.0)
KILL = 1e30
SUB = 8
LANES = 128
PAD = 24
ROWS = 64
XP, DTW, ALOG, ROWS_P = 0, 24, 40, 48
CONVW, CONVB, DTB, SKIP, GAIN = 0, 4, 5, 6, 7
A_DTW, A_ALOG, A_DTB, A_SKIP, A_ROWS = 0, 16, 20, 21, 24
B_XP, B_CONVW, B_CONVB, B_ROWS = 0, 24, 28, 32
NT = (((1,), (1,)), ((), ()))
TN = (((0,), (0,)), ((), ()))


def dot(a, b):
    return jnp.dot(a, b, preferred_element_type=F32)


def dot_nt(a, b):
    return lax.dot_general(a, b, NT, preferred_element_type=F32)


def dot_tn(a, b):
    return lax.dot_general(a, b, TN, preferred_element_type=F32)


def at8(start, size):
    return pl.ds(pl.multiple_of(start, 8), size)


def sigmoid(v):
    return 0.5 + 0.5 * jnp.tanh(0.5 * v)


def log_one_plus(v):
    series = v * (1.0 - v * (0.5 - v * (1.0 / 3.0 - v * 0.25)))
    return jnp.where(v < 0.01, series, jnp.log(1.0 + v))


def one_less_exp(v):
    series = v * (1.0 - v * (0.5 - v * (1.0 / 6.0 - v * (1.0 / 24.0 - v * (1.0 / 120.0)))))
    return jnp.where(v < 0.1, series, 1.0 - jnp.exp(-v))


def prefix_of(ends, prods):
    row = lax.broadcasted_iota(jnp.int32, ends.shape, 0)
    for gap in (1, 2, 4):
        ok = row >= gap
        ends = ends + prods * jnp.where(ok, pltpu.roll(ends, gap, 0), 0.0)
        prods = prods * jnp.where(ok, pltpu.roll(prods, gap, 0), 1.0)
    return jnp.where(row >= 1, pltpu.roll(ends, 1, 0), 0.0)


def suffix_of(ends, prods):
    row = lax.broadcasted_iota(jnp.int32, ends.shape, 0)
    for gap in (1, 2, 4):
        ok = row < SUB - gap
        ends = ends + prods * jnp.where(ok, pltpu.roll(ends, SUB - gap, 0), 0.0)
        prods = prods * jnp.where(ok, pltpu.roll(prods, SUB - gap, 0), 1.0)
    return jnp.where(row < SUB - 1, pltpu.roll(ends, SUB - 1, 0), 0.0)


def fused_kernel(
    x_ref, og_ref, win_ref, wout_ref, xproj_ref, dtw_ref, alog_ref, convw_ref, convb_ref, dtb_ref,
    skip_ref, gain_ref, seg_ref, mask_ref,
    so_out, sg_out, wg_out, wo_out, sm_out, cv_out, gg_out,
    x_half, og_half, xf, mg, w_s, wo_s, early, pk_f, pk_s, segs, segp, maskc, nat, inner, slope, act, gate, dt, yg, y,
    bc, h, a2b, st, gin, cum, alg, full, full2, mp, sum_a, recv_a, recv_b, xp, dtwp,
    big_send, big_keep, big_recv, big_rb, gpart, zrecv, gres, gnat, znat, spart, srecv, sfull, bpart, brecv, bfull, sown, ggs,
    sg_s, ssem, rsem, lsem,
):
    z, c, k = lax.axis_index("dp"), lax.axis_index("ctx"), lax.axis_index("tp")
    nz = lax.axis_size("dp")
    px, py = lax.rem(c, 2), c // 2
    sib = (z, c, 1 - k)
    plane = [None, py * 2 + (1 - px), (1 - py) * 2 + px, (1 - py) * 2 + (1 - px)]
    peers = [None] + [(z, plane[p], k) for p in (1, 2, 3)]
    toward = [None] + [lax.rem(z + d, nz) for d in (1, 2, 3)]
    behind = [None] + [lax.rem(z + nz - d, nz) for d in (1, 2, 3)]
    lines = [None] + [(toward[d], c, k) for d in (1, 2, 3)]
    count = [0]
    local_count = [0]
    pending = []

    def send(src, dst, device):
        i = count[0]
        count[0] += 1
        copy = pltpu.make_async_remote_copy(
            src_ref=src, dst_ref=dst, send_sem=ssem.at[i], recv_sem=rsem.at[i],
            device_id=device, device_id_type=MESH,
        )
        copy.start()
        pending.append(copy)
        return copy

    def local(src, dst):
        i = local_count[0]
        local_count[0] += 1
        copy = pltpu.make_async_copy(src, dst, lsem.at[i])
        copy.start()
        return copy

    def flush(copies):
        for copy in copies:
            copy.wait_send()
            pending[:] = [other for other in pending if other is not copy]

    tok = maskc.shape[0]
    half = tok // 2
    total = xf.shape[0]
    width = xf.shape[1]
    steps = total // SUB
    states = h.shape[1]
    wide = 2 * LANES
    block = w_s.shape[1] // 4
    tiles = (0, 1)
    rb = 128
    nblk = total // rb

    def lanes(t):
        return slice(t * LANES, (t + 1) * LANES)

    def blk(i):
        return pl.ds(pl.multiple_of(i * rb, rb), rb)

    wb = 512

    def wide_blk(i):
        return pl.ds(pl.multiple_of(i * wb, wb), wb)

    def tau_rows(tau):
        return at8(tau * SUB, SUB)

    def loop(n, body, unroll=1):
        def step(i, carry):
            body(i)
            return carry

        lax.fori_loop(0, n, step, 0, unroll=unroll)

    barrier = pltpu.get_barrier_semaphore()
    everyone = [sib] + peers[1:] + [(z, plane[p], 1 - k) for p in (1, 2, 3)] + lines[1:]
    for device in everyone:
        pl.semaphore_signal(barrier, inc=1, device_id=device, device_id_type=MESH)
    chans = pl.ds(pl.multiple_of(c * wide, wide), wide)
    spart[...] = jnp.zeros_like(spart)
    spart[0, XP : XP + 24, :] = xproj_ref[:, chans].astype(F32)
    spart[0, DTW : DTW + 16, :] = dtw_ref[:, chans].astype(F32)
    spart[0, ALOG : ALOG + 4, :] = alog_ref[:, chans].astype(F32)
    early[z, CONVW : CONVW + 4, :] = convw_ref[...].astype(F32)
    early[z, CONVB : CONVB + 1, :] = convb_ref[...].astype(F32)
    early[z, DTB : DTB + 1, :] = dtb_ref[...].astype(F32)
    early[z, SKIP : SKIP + 1, :] = skip_ref[...].astype(F32)
    early[z, GAIN : GAIN + 1, :] = gain_ref[...].astype(F32).reshape(1, block)
    pk_s[z] = spart[0, 0:ROWS_P, :].astype(BF16)
    segs[c] = jnp.broadcast_to(seg_ref[...], (SUB, tok))
    pl.semaphore_wait(barrier, len(everyone))

    s_early = [send(early.at[z], early.at[z], lines[d]) for d in (1, 2, 3)]
    s_seg = [send(segs.at[c], segs.at[c], peers[p]) for p in (1, 2, 3)]
    my_half = pl.ds(pl.multiple_of(c * tok + k * half, half), half)
    s_x = [send(x_ref.at[pl.ds(pl.multiple_of(k * half, half), half)], xf.at[my_half], peers[p]) for p in (3, 1, 2)]

    zrows = pl.ds(pl.multiple_of(z * block, block), block)

    def weight(which):
        return [
            send(win_ref.at[which, :, chans], w_s.at[which, zrows, :], lines[d]) for d in (1, 2, 3)
        ]

    s_wx = weight(0)
    s_pack = [send(pk_s.at[z], pk_s.at[z], lines[d]) for d in (1, 2, 3)]
    own_w = [local(win_ref.at[i, :, chans], w_s.at[i, zrows, :]) for i in (0, 1)]
    zcols = pl.ds(pl.multiple_of(z * block, block), block)
    own_wo = local(wout_ref.at[chans, :], wo_s.at[:, zcols])

    own_rows = pl.ds(pl.multiple_of(c * tok, tok), tok)
    half_rows = pl.ds(pl.multiple_of(k * half, half), half)
    own_x = local(x_ref, xf.at[own_rows, :])
    own_og = local(og_ref, mg.at[own_rows, :])
    own_half = [local(x_ref.at[half_rows, :], x_half), local(og_ref.at[half_rows, :], og_half)]
    mrow = mask_ref[...].astype(F32)
    for b in range(tok // LANES):
        rows = slice(b * LANES, (b + 1) * LANES)
        maskc[rows, :] = jnp.broadcast_to(mrow[:, rows], (LANES, LANES)).T
    mcol = jnp.concatenate([maskc[...]] * (width // LANES), axis=1)
    own_og.wait()
    mg[own_rows, :] = (mg[own_rows, :].astype(F32) * mcol).astype(BF16)

    for copy in s_early:
        copy.wait_recv()
    gain_row = jnp.concatenate([early[i, GAIN : GAIN + 1, :] for i in range(4)], axis=1)
    sown[...] = early[c]

    def param(row, t):
        return sown[row : row + 1, lanes(t)]

    for copy in s_seg:
        copy.wait_recv()
    for i in range(4):
        srow = segs[i, 0:1, :].astype(F32)
        for b in range(tok // LANES):
            rows = slice(b * LANES, (b + 1) * LANES)
            nat[0, i * tok + b * LANES : i * tok + (b + 1) * LANES, :] = jnp.broadcast_to(
                srow[:, rows], (LANES, LANES)
            ).T

    def seg_in(tau):
        segp[at8(PAD + tau * SUB, SUB), :] = nat[0, pl.ds(tau, SUB, stride=steps), :]

    loop(steps, seg_in, 8)
    sub_row = lax.broadcasted_iota(jnp.int32, (SUB, LANES), 0)

    def from_before(v, fill):
        return jnp.where(sub_row >= 1, pltpu.roll(v, 1, 0), fill)

    def from_after(v, fill):
        return jnp.where(sub_row < SUB - 1, pltpu.roll(v, SUB - 1, 0), fill)

    for j in range(3):
        segp[j * SUB : (j + 1) * SUB, :] = from_before(segp[total + j * SUB : total + (j + 1) * SUB, :], -1.0)
        segp[PAD + total + j * SUB : PAD + total + (j + 1) * SUB, :] = from_after(
            segp[PAD + j * SUB : PAD + (j + 1) * SUB, :], -2.0
        )

    def halves(copies, buf):
        relays = []
        for copy, p in zip(copies, (3, 1, 2)):
            copy.wait_recv()
            rows = pl.ds(pl.multiple_of(plane[p] * tok + k * half, half), half)
            relays.append(send(buf.at[rows], buf.at[rows], sib))
        return relays

    def norm(i):
        rows = pl.ds(pl.multiple_of(i * rb, rb), rb)
        v = xf[rows, :].astype(F32)
        r = lax.rsqrt(jnp.mean(v * v, axis=1, keepdims=True) + EPS)
        xf[rows, :] = (v * r * gain_row).astype(BF16)

    def project_block(i):
        rows = pl.ds(pl.multiple_of(i * tok, tok), tok)
        v = dot(xf[rows, :], w_s[0])
        for t in tiles:
            nat[t, rows, :] = v[:, lanes(t)]

    per = tok // rb
    own_x.wait()
    loop(per, lambda i: norm(c * per + i))
    r_x = halves(s_x, xf)
    for copy in s_wx:
        copy.wait_recv()
    own_w[0].wait()
    s_wz = weight(1)
    project_block(c)
    for copy, sent, p in zip(r_x, s_x, (3, 1, 2)):
        copy.wait_recv()
        flush([copy])
        loop(per, lambda i, p=p: norm(plane[p] * per + i))
        project_block(plane[p])

    def project(which, dst, off):
        def body(i):
            v = dot(xf[wide_blk(i), :], w_s[which])
            for t in tiles:
                nat[t, wide_blk(i), :] = v[:, lanes(t)]

        loop(total // wb, body)
        permute_in(dst, off, True)

    def permute_in(dst, off, rounded=False):
        def body(tau):
            for t in tiles:
                v = nat[t, pl.ds(tau, SUB, stride=steps), :]
                dst[t, at8(off + tau * SUB, SUB), :] = v.astype(BF16).astype(F32) if rounded else v

        loop(steps, body, 8)

    def permute_out(src, dst, which=tiles):
        def body(i):
            for s in range(SUB):
                for t in which:
                    nat[t, at8(s * steps + i * SUB, SUB), :] = src[t, pl.ds(i * SUB * SUB + s, SUB, stride=SUB), :]

        loop(steps // SUB, body)

        def cast(i):
            for t in which:
                dst[blk(i), lanes(t)] = nat[t, blk(i), :].astype(BF16)

        loop(nblk, cast)

    permute_in(inner, PAD, True)
    for t in tiles:
        for j in range(3):
            inner[t, j * SUB : (j + 1) * SUB, :] = from_before(inner[t, total + j * SUB : total + (j + 1) * SUB, :], 0.0)

    def conv(i):
        for t in tiles:
            mine = segp[at8(PAD + i * rb, rb), :]
            pre = jnp.zeros((rb, LANES), F32) + param(CONVB, t)
            for j in range(4):
                window = inner[t, at8(PAD + i * rb - j * SUB, rb), :]
                if j:
                    window = jnp.where(segp[at8(PAD + i * rb - j * SUB, rb), :] == mine, window, 0.0)
                pre = pre + param(CONVW + 3 - j, t) * window
            s = sigmoid(pre)
            act[t, blk(i), :] = (pre * s).astype(BF16).astype(F32)
            slope[t, blk(i), :] = s * (1.0 + pre * (1.0 - s))

    loop(nblk, conv)

    def tiles_bf(ref, i):
        return jnp.concatenate([ref[t, blk(i), :] for t in tiles], axis=1).astype(BF16)

    for copy in s_pack:
        copy.wait_recv()
    for i in range(4):
        pk_f[i] = pk_s[i].astype(F32)
    for i in range(4):
        alg[4 * i : 4 * i + 4, :] = pk_f[i, ALOG : ALOG + 4, :]
    xp_rows = jnp.concatenate([pk_f[i, XP : XP + 24, :] for i in range(4)] + [jnp.zeros((32, wide), F32)], axis=0)
    xp[...] = xp_rows.astype(BF16)
    dt_rows = jnp.concatenate([pk_f[i, DTW : DTW + 16, :] for i in range(4)] + [jnp.zeros((64, wide), F32)], axis=0)
    dtwp[...] = dt_rows.astype(BF16)
    a2v = -jnp.exp(alg[...]) * LOG2E
    for n in range(states):
        for t in tiles:
            a2b[t, n] = jnp.broadcast_to(a2v[n : n + 1, lanes(t)], (SUB, LANES))

    def mix(i):
        mp[i] = dot_nt(tiles_bf(act, i), xp[...])

    loop(nblk, mix)

    def plane_sum(out, between):
        first = send(mp.at[pl.ds((1 - k) * 4, 4)], recv_a, sib)
        between[0]()
        first.wait_recv()
        for i in range(4):
            sum_a[i] = (mp[k * 4 + i] + recv_a[i]).astype(BF16)
        second = [send(sum_a.at[plane[p]], recv_b.at[p - 1], peers[p]) for p in (3, 1, 2)]
        between[1]()
        for copy in second:
            copy.wait_recv()
        mine = k * 4 + c
        v = mp[mine] + recv_a[c]
        for p in range(3):
            v = v + recv_b[p].astype(F32)
        out[mine] = v.astype(BF16)
        third = [send(out.at[mine], out.at[mine], peers[p]) for p in (3, 1, 2)]
        third.append(send(out.at[mine], out.at[mine], sib))
        between[2]()
        fourth = []
        for copy, p in zip(third, (3, 1, 2)):
            copy.wait_recv()
            there = k * 4 + plane[p]
            fourth.append(send(out.at[there], out.at[there], sib))
        between[3]()
        for copy in [third[3]] + fourth:
            copy.wait_recv()
        return [first] + second

    late = {}

    def send_wo():
        for copy in s_wz:
            copy.wait_recv()
        own_w[1].wait()
        late["wo"] = [send(wout_ref.at[chans, :], wo_s.at[:, zcols], lines[d]) for d in (1, 2, 3)]

    def gates():
        project(1, gate, 0)

    def nothing():
        pass

    def send_mg():
        late["mg"] = [send(mg.at[my_half], mg.at[my_half], peers[p]) for p in (3, 1, 2)]

    def gap():
        send_mg()
        send_wo()
        gates()

    first_sum = plane_sum(full, [nothing, nothing, nothing, gap])

    def steps_of(i):
        arg = dot(full[i], dtwp[...])
        for t in tiles:
            v = arg[:, lanes(t)] + param(DTB, t)
            dt[t, blk(i), :] = jnp.maximum(v, 0.0) + log_one_plus(jnp.exp(-jnp.abs(v)))

    loop(nblk, steps_of)

    flat = full[...].reshape(total, LANES)
    row = lax.broadcasted_iota(jnp.int32, (LANES, wide), 0)
    col = lax.broadcasted_iota(jnp.int32, (LANES, wide), 1) // LANES
    for n in range(0, 2 * states, 2):
        v = dot(flat, jnp.where(row == 64 + n + col, 1.0, 0.0).astype(BF16))
        for t in tiles:
            bc[n + t] = v[:, lanes(t)]

    def dts(t, tau):
        v = dt[t, tau_rows(tau), :]
        r = at8(PAD + tau * SUB, SUB)
        p = at8(PAD + tau * SUB - SUB, SUB)
        return v, jnp.where(segp[r, :] == segp[p, :], v, KILL)

    for t in tiles:

        def ends(tau, carry, t=t):
            v, killed = dts(t, tau)
            drive = v * act[t, tau_rows(tau), :]
            new = [
                carry[n] * jnp.exp2(killed * a2b[t, n]) + drive * bc[n, tau_rows(tau), :] for n in range(states)
            ]
            return tuple(new) + (carry[states] + killed,)

        zero = jnp.zeros((SUB, LANES), F32)
        got = lax.fori_loop(0, steps, ends, (zero,) * (states + 1), unroll=8)
        cum[t] = got[states]
        for n in range(states):
            st[t, n] = prefix_of(got[n], jnp.exp2(got[states] * a2b[t, n]))

    for t in tiles:
        if t:
            late["mg"] = halves(late["mg"], mg)
        for n in range(states):
            h[t, n, 0:SUB, :] = st[t, n]

        def forward(tau, carry, t=t):
            v, killed = dts(t, tau)
            drive = v * act[t, tau_rows(tau), :]
            new, parts = [], [None] * 4
            for n in range(states):
                s = carry[n] * jnp.exp2(killed * a2b[t, n]) + drive * bc[n, tau_rows(tau), :]
                h[t, n, at8(tau * SUB + SUB, SUB), :] = s
                o = s * bc[states + n, tau_rows(tau), :]
                parts[n % 4] = o if parts[n % 4] is None else parts[n % 4] + o
                new.append(s)
            y[t, tau_rows(tau), :] = (parts[0] + parts[1]) + (parts[2] + parts[3])
            return tuple(new)

        lax.fori_loop(0, steps, forward, tuple(st[t, n] for n in range(states)), unroll=8)

    for copy in late["mg"] + late["wo"]:
        copy.wait_recv()
    own_wo.wait()

    def ograd(i):
        v = dot_nt(mg[wide_blk(i), :], wo_s[...])
        for t in tiles:
            nat[t, wide_blk(i), :] = v[:, lanes(t)]

    loop(total // wb, ograd)
    gb = SUB * SUB

    def strided(t, i):
        return jnp.concatenate([nat[t, pl.ds(i * SUB + u, SUB, stride=steps), :] for u in range(SUB)], axis=0)

    def gating(i, carry):
        new = []
        rows = pl.ds(pl.multiple_of(i * gb, gb), gb)
        for t in tiles:
            gv, ov, av = gate[t, rows, :], strided(t, i), act[t, rows, :]
            s = sigmoid(gv)
            ytot = y[t, rows, :] + param(SKIP, t) * av
            gy = ov * (gv * s)
            yg[t, rows, :] = gy
            y[t, rows, :] = ytot * (gv * s)
            gate[t, rows, :] = ov * ytot * (s * (1.0 + gv * (1.0 - s)))
            new.append(carry[t] + jnp.sum((gy * av).reshape(SUB, SUB, LANES), axis=0))
        return tuple(new)

    zero = jnp.zeros((SUB, LANES), F32)
    skip_sum = lax.fori_loop(0, total // gb, gating, (zero, zero))
    permute_out(y, gnat)
    permute_out(gate, znat)

    def owner_rows(i, q):
        return pl.ds(pl.multiple_of(i * tok + q * half, half), half)

    order = (3, 1, 2, 0)
    groups = width // wide
    turns = (0, 2, 1, 3)

    def fill(dst, j, q, lefts, right):
        cols = slice(j * wide, (j + 1) * wide)
        there = [plane[p] if p else c for p in order]
        rows = [jnp.concatenate([left[owner_rows(i, q), :] for i in there], axis=0) for left in lefts]
        v = right(rows, cols)
        for i, p in enumerate(order):
            dst[p, :, cols] = v[i * half : (i + 1) * half, :].astype(BF16)

    def start_rows(lefts, right):
        first = {}
        for j in turns:
            cols = slice(j * wide, (j + 1) * wide)
            fill(big_send, j, 1 - k, lefts, right)
            first[j] = send(big_send.at[:, :, cols], big_recv.at[:, :, cols], sib)
        return first

    def ways(j):
        return (1, 2) if j < groups // 2 else (2, 1)

    def middle_rows(first, lefts=None, right=None):
        second = {}
        for j in turns:
            cols = slice(j * wide, (j + 1) * wide)
            if lefts:
                fill(big_keep, j, k, lefts, right)
            first[j].wait_recv()
            for p in order:
                big_keep[p, :, cols] = (big_keep[p, :, cols].astype(F32) + big_recv[p, :, cols].astype(F32)).astype(BF16)
            near, far = ways(j)
            second[j] = [
                send(big_keep.at[3, :, cols], big_rb.at[1, :, cols], peers[near]),
                send(big_keep.at[near, :, cols], big_rb.at[0, :, cols], peers[near]),
            ]
        return second

    def pass_rows(second):
        third = []
        for j in turns:
            cols = slice(j * wide, (j + 1) * wide)
            near, far = ways(j)
            second[j][0].wait_recv()
            big_keep[far, :, cols] = (big_keep[far, :, cols].astype(F32) + big_rb[1, :, cols].astype(F32)).astype(BF16)
            third.append(send(big_keep.at[far, :, cols], big_rb.at[2, :, cols], peers[far]))
        return [second[j][1] for j in turns] + third, [second[j][0] for j in turns]

    def end_rows(second):
        for copy in second:
            copy.wait_recv()
        return big_keep[0].astype(F32) + big_rb[0].astype(F32) + big_rb[2].astype(F32)

    def branch_part(rows, cols):
        return dot(rows[0], wo_s[:, cols])

    branch_a = start_rows([gnat], branch_part)
    for j in range(groups):
        fill(big_keep, j, k, [gnat], branch_part)

    def weight_grad(slot, left, right):
        gpart[slot % 2] = dot_tn(left[...], right[...]).astype(BF16)

    def spread_grad(slot):
        return [
            send(
                gpart.at[slot % 2, :, pl.ds(pl.multiple_of(toward[d] * block, block), block)],
                zrecv.at[slot, d - 1],
                lines[d],
            )
            for d in (1, 2, 3)
        ]

    def owned_grad(slot, copies):
        for copy in copies:
            copy.wait_recv()
        v = gpart[slot % 2, :, zcols].astype(F32)
        for d in range(3):
            v = v + zrecv[slot, d].astype(F32)
        return v

    def share(slot, dst):
        return [local(gres.at[slot], dst)] + [send(gres.at[slot], dst, peers[p]) for p in (3, 1, 2)]

    weight_grad(2, gnat, mg)
    z_wo = spread_grad(2)
    weight_grad(1, znat, xf)

    for t in tiles:
        if t:
            branch_b = middle_rows(branch_a)

        def back_ends(i, carry, t=t):
            tau = steps - 1 - i
            _, killed = dts(t, tau)
            gy = yg[t, tau_rows(tau), :]
            return tuple(
                (carry[n] + gy * bc[states + n, tau_rows(tau), :]) * jnp.exp2(killed * a2b[t, n])
                for n in range(states)
            )

        got = lax.fori_loop(0, steps, back_ends, (zero,) * states, unroll=8)
        for n in range(states):
            gin[t, n] = suffix_of(got[n], jnp.exp2(cum[t] * a2b[t, n]))

    flush(branch_a.values())
    branch_b, branch_sent = pass_rows(branch_b)
    so_s = big_send.at[0]

    gsum, dsum = gate, y
    part = states // 2
    for lo in (0, part):
        names = list(range(lo, lo + part))
        if lo:
            z_wz = spread_grad(1)

        def back(i, carry, names=names, lo=lo):
            grads, acc = carry
            tau = steps - 1 - i
            r = tau_rows(tau)
            pair = [dts(t, tau) for t in tiles]
            drive = [pair[t][0] * act[t, r, :] for t in tiles]
            gy = [yg[t, r, :] for t in tiles]
            along = [None, None]
            down = [None, None]
            new_g, new_a = [], []
            for q, n in enumerate(names):
                bv, cv = bc[n, r, :], bc[states + n, r, :]
                pb = pc = None
                for t in tiles:
                    a2 = a2b[t, n]
                    decay = jnp.exp2(pair[t][1] * a2)
                    g = grads[2 * q + t] + gy[t] * cv
                    gb = g * bv
                    along[t] = gb if along[t] is None else along[t] + gb
                    v = g * drive[t]
                    pb = v if pb is None else pb + v
                    v = gy[t] * h[t, n, at8(tau * SUB + SUB, SUB), :]
                    pc = v if pc is None else pc + v
                    gd = g * decay
                    dla = gd * h[t, n, r, :]
                    v = dla * a2
                    down[t] = v if down[t] is None else down[t] + v
                    new_a.append(acc[2 * q + t] + dla * pair[t][0])
                    new_g.append(gd)
                bc[n, r, :] = pb
                bc[states + n, r, :] = pc
            for t in tiles:
                if lo == 0:
                    gsum[t, r, :] = along[t]
                    dsum[t, r, :] = down[t]
                else:
                    gsum[t, r, :] = gsum[t, r, :] + along[t]
                    dsum[t, r, :] = dsum[t, r, :] + down[t]
            return tuple(new_g), tuple(new_a)

        start = tuple(gin[t, n] for n in names for t in tiles)
        _, acc = lax.fori_loop(0, steps, back, (start, (zero,) * (2 * part)), unroll=4)
        for q, n in enumerate(names):
            for t in tiles:
                alg[n : n + 1, lanes(t)] = (
                    jnp.sum(acc[2 * q + t], axis=0, keepdims=True) * a2b[t, n][0:1, :] * LN2
                )

    gres[2] = owned_grad(2, z_wo).astype(BF16)
    late["gwo"] = share(2, wo_out.at[chans, :])

    def lin(i, carry):
        new = []
        rank = []
        for t in tiles:
            av, gv = act[t, blk(i), :], gsum[t, blk(i), :]
            v = (dsum[t, blk(i), :] * LN2 + av * gv) * one_less_exp(dt[t, blk(i), :])
            new.append(carry[t] + jnp.sum(v.reshape(rb // SUB, SUB, LANES), axis=0))
            low = v.astype(BF16)
            rank.append(low)
            dsum[t, blk(i), :] = low.astype(F32)
            gsum[t, blk(i), :] = dt[t, blk(i), :] * gv + param(SKIP, t) * yg[t, blk(i), :]
        mp[i] = dot_nt(jnp.concatenate(rank, axis=1), dtwp[...])
        return tuple(new)

    flush(first_sum)
    dtb_sum = lax.fori_loop(0, nblk, lin, (zero, zero))

    beside = lax.broadcasted_iota(jnp.int32, (wide, LANES), 1) - 64
    beside = beside - lax.broadcasted_iota(jnp.int32, (wide, LANES), 0) // LANES

    def collect(i):
        rows = pl.ds(pl.multiple_of(i * 2 * rb, 2 * rb), 2 * rb)
        v = jnp.concatenate([mp[2 * i], mp[2 * i + 1]], axis=0)
        for n in range(0, 2 * states, 2):
            pick = jnp.where(beside == n, 1.0, 0.0).astype(BF16)
            pair = jnp.concatenate([bc[n, rows, :], bc[n + 1, rows, :]], axis=1).astype(BF16)
            v = v + dot(pair, pick)
        mp[2 * i] = v[:rb, :]
        mp[2 * i + 1] = v[rb:, :]

    loop(nblk // 2, collect)

    def finish_early():
        v = end_rows(branch_b)
        mk = jnp.concatenate([maskc[half_rows, :]] * (width // LANES), axis=1)
        for copy in own_half:
            copy.wait()
        so_s[...] = (x_half[...].astype(F32) + mk * v).astype(BF16)
        late["so"] = [local(so_s, so_out.at[half_rows, :]), send(so_s, so_out.at[half_rows, :], sib)]

    def finish_z():
        v = owned_grad(1, z_wz).T
        gres[1] = v.astype(BF16)
        v = v * w_s[1, zrows, :].astype(F32)
        late["gain"] = v[:, :LANES] + v[:, LANES:]

    def small_a():
        low = jnp.concatenate([full[i] for i in range(nblk)], axis=0)
        linv = jnp.concatenate([tiles_bf(dsum, i) for i in range(nblk)], axis=0)
        g = dot_tn(low, linv)
        for i in range(4):
            spart[i, A_DTW : A_DTW + 16, :] = g[i * 16 : i * 16 + 16, :]
            spart[i, A_ALOG : A_ALOG + 4, :] = alg[i * 4 : i * 4 + 4, :]
            for t in tiles:
                spart[i, A_DTB : A_DTB + 1, lanes(t)] = jnp.sum(dtb_sum[t], axis=0, keepdims=True)
                spart[i, A_SKIP : A_SKIP + 1, lanes(t)] = jnp.sum(skip_sum[t], axis=0, keepdims=True)
        late["za"] = [
            send(spart.at[toward[d], pl.ds(0, A_ROWS)], srecv.at[d - 1], lines[d]) for d in (1, 2, 3)
        ]

    def shares():
        late["gwz"] = share(1, wg_out.at[1, :, chans])
        for copy in late["za"]:
            copy.wait_recv()
        sfull[c] = spart[z, 0:A_ROWS, :] + srecv[0] + srecv[1] + srecv[2]
        late["ga"] = [send(sfull.at[c], sfull.at[c], peers[p]) for p in (3, 1, 2)]

    second_sum = plane_sum(full2, [small_a, finish_early, finish_z, shares])

    pg = slope

    flush(z_wo)
    z_wx = []
    for t in tiles:

        def pre_grad(i, t=t):
            v = gsum[t, blk(i), :] + dot(full2[i], xp[:, lanes(t)])
            pg[t, blk(i), :] = v * pg[t, blk(i), :]

        loop(nblk, pre_grad)
        for j in range(3):
            pg[t, total + j * SUB : total + (j + 1) * SUB, :] = from_after(pg[t, j * SUB : (j + 1) * SUB, :], 0.0)

        def inner_grad(i, t=t):
            mine = segp[at8(PAD + i * rb, rb), :]
            v = pg[t, blk(i), :] * param(CONVW + 3, t)
            for j in range(1, 4):
                later = pg[t, at8(i * rb + j * SUB, rb), :]
                same = segp[at8(PAD + i * rb + j * SUB, rb), :] == mine
                v = v + jnp.where(same, later, 0.0) * param(CONVW + 3 - j, t)
            dsum[t, blk(i), :] = v

        loop(nblk, inner_grad)
        permute_out(dsum, gnat, (t,))
        gpart[0, lanes(t), :] = dot_tn(gnat[:, lanes(t)], xf[...]).astype(BF16)
        z_wx.append(
            [
                send(
                    gpart.at[0, pl.ds(t * LANES, LANES), pl.ds(pl.multiple_of(toward[d] * block, block), block)],
                    zrecv.at[0, d - 1, pl.ds(t * LANES, LANES)],
                    lines[d],
                )
                for d in (1, 2, 3)
            ]
        )

    flush(late["so"][1:] + branch_b + branch_sent)
    late["so"][0].wait()
    def norm_part(rows, cols):
        return dot_nt(rows[0], w_s[0, cols, :]) + dot_nt(rows[1], w_s[1, cols, :])

    norm_a = start_rows([gnat, znat], norm_part)
    norm_b = middle_rows(norm_a, [gnat, znat], norm_part)

    def conv_grad(i, carry):
        new = []
        mine = segp[at8(PAD + i * rb, rb), :]
        for t in tiles:
            v = pg[t, blk(i), :]
            new.append(carry[5 * t] + jnp.sum(v.reshape(rb // SUB, SUB, LANES), axis=0))
            for j in range(4):
                window = inner[t, at8(PAD + i * rb - j * SUB, rb), :]
                if j:
                    window = jnp.where(segp[at8(PAD + i * rb - j * SUB, rb), :] == mine, window, 0.0)
                new.append(carry[5 * t + 1 + j] + jnp.sum((v * window).reshape(rb // SUB, SUB, LANES), axis=0))
        return tuple(new)

    conv_sum = lax.fori_loop(0, nblk, conv_grad, (zero,) * 10)
    norm_b, _ = pass_rows(norm_b)
    mixv = jnp.concatenate([full2[i] for i in range(nblk)], axis=0)
    actv = jnp.concatenate([tiles_bf(act, i) for i in range(nblk)], axis=0)
    gx = dot_tn(mixv, actv)
    for i in range(4):
        conv_rows = [
            jnp.concatenate([jnp.sum(conv_sum[5 * t + j], axis=0, keepdims=True) for t in tiles], axis=1)
            for j in (4, 3, 2, 1, 0)
        ]
        bpart[i] = jnp.concatenate(
            [gx[i * 24 : i * 24 + 24, :]] + conv_rows + [jnp.zeros((3, wide), F32)], axis=0
        ).astype(BF16)
    z_b = [send(bpart.at[toward[d]], brecv.at[d - 1], lines[d]) for d in (1, 2, 3)]
    gain_sum = late["gain"]
    late["gwx"] = [[], []]

    def owned_half(q):
        for copy in z_wx[q]:
            copy.wait_recv()
        rows = slice(q * LANES, (q + 1) * LANES)
        v = gpart[0, rows, zcols].astype(F32)
        for d in range(3):
            v = v + zrecv[0, d, rows, :].astype(F32)
        v = v.T
        gres[0, :, rows] = v.astype(BF16)
        return v * w_s[0, zrows, rows].astype(F32)

    def share_half(q):
        rows = slice(q * LANES, (q + 1) * LANES)
        dst = wg_out.at[0, :, pl.ds(pl.multiple_of(c * wide + q * LANES, LANES), LANES)]
        late["gwx"][0].append(local(gres.at[0, :, rows], dst))
        late["gwx"][1].extend(send(gres.at[0, :, rows], dst, peers[p]) for p in (3, 1, 2))

    gain_sum = gain_sum + owned_half(0)
    share_half(0)
    for copy in z_b:
        copy.wait_recv()
    v = bpart[z].astype(F32)
    for d in range(3):
        v = v + brecv[d].astype(F32)
    bfull[c] = v.astype(BF16)
    g_b = [send(bfull.at[c], bfull.at[c], peers[p]) for p in (3, 1, 2)]
    ng = end_rows(norm_b)
    xv = x_half[...].astype(F32)
    r = lax.rsqrt(jnp.mean(xv * xv, axis=1, keepdims=True) + EPS)
    sg = ng * gain_row
    sg_s[...] = (
        og_half[...].astype(F32) + r * sg - xv * (r * r * r) * jnp.mean(sg * xv, axis=1, keepdims=True)
    )
    last = [local(sg_s, sg_out.at[half_rows, :]), send(sg_s, sg_out.at[half_rows, :], sib)]

    gain_sum = gain_sum + owned_half(1)
    for b in range(block // LANES):
        col = gain_sum[b * LANES : (b + 1) * LANES, :].T
        ggs[0, :, lanes(b)] = jnp.broadcast_to(jnp.sum(col, axis=0, keepdims=True), (SUB, LANES))
    s_gain = [send(ggs.at[0], ggs.at[p], peers[p]) for p in (1, 2, 3)]
    s_gain += [send(ggs.at[0], ggs.at[3 + p], (z, plane[p], 1 - k)) for p in (1, 2, 3)]
    s_gain.append(send(ggs.at[0], ggs.at[7], sib))
    share_half(1)

    for copy in late["ga"] + g_b:
        copy.wait_recv()
    for i in range(4):
        cols = slice(i * wide, (i + 1) * wide)
        sm_out[0:24, cols] = bfull[i, B_XP : B_XP + 24, :].astype(F32)
        sm_out[24:44, cols] = sfull[i, A_DTW : A_ALOG + 4, :]
    cv_out[0:5, :] = bfull[z, B_CONVW : B_CONVB + 1, :].astype(F32)
    cv_out[5:7, :] = sfull[z, A_DTB : A_SKIP + 1, :]
    for copy in s_gain:
        copy.wait_recv()
    v = ggs[0]
    for i in range(1, 8):
        v = v + ggs[i]
    gg_out[...] = v[0:1, :] / early[z, GAIN : GAIN + 1, :]

    late["so"][1].wait_recv()
    for name in ("gwo", "gwz"):
        late[name][0].wait()
        for copy in late[name][1:]:
            copy.wait_recv()
    for copy in late["gwx"][0]:
        copy.wait()
    for copy in late["gwx"][1]:
        copy.wait_recv()
    last[0].wait()
    last[1].wait_recv()
    flush(list(pending))


def fused(
    stream_in, norm_gain, in_weight, out_weight, xproj_weight, dt_weight, a_log, convolution_weight,
    convolution_bias, step_size_bias, skip_term_scale, seg_ids, pad_mask, out_grad,
):
    _, tok, width = stream_in.shape
    wide = 2 * LANES
    total = 4 * tok
    block = width // 4
    states = 4 * a_log.shape[0]
    vm = pl.BlockSpec(memory_space=pltpu.VMEM)
    hbm = pl.BlockSpec(memory_space=pl.ANY)
    f, b = (lambda *s: pltpu.VMEM(s, F32)), (lambda *s: pltpu.VMEM(s, BF16))
    scan = f(2, total, LANES)
    scratch = dict(
        x_half=b(tok // 2, width), og_half=b(tok // 2, width), xf=b(total, width), mg=b(total, width), w_s=b(2, width, wide), wo_s=b(wide, width),
        early=f(4, SUB, wide), pk_f=f(4, ROWS_P, wide), pk_s=b(4, ROWS_P, wide), segs=pltpu.VMEM((4, SUB, tok), jnp.int32),
        segp=f(total + 2 * PAD, LANES), maskc=f(tok, LANES), nat=scan, inner=f(2, total + PAD, LANES),
        slope=f(2, total + PAD, LANES), act=scan, gate=scan, dt=scan, yg=scan, y=scan,
        bc=f(2 * states, total, LANES), h=f(2, states, total + SUB, LANES), a2b=f(2, states, SUB, LANES),
        st=f(2, states, SUB, LANES), gin=f(2, states, SUB, LANES), cum=f(2, SUB, LANES), alg=f(states, wide),
        full=b(8, 128, LANES), full2=b(8, 128, LANES), mp=f(8, 128, LANES), sum_a=b(4, 128, LANES),
        recv_a=f(4, 128, LANES), recv_b=b(3, 128, LANES), xp=b(LANES, wide), dtwp=b(LANES, wide),
        big_send=b(4, tok // 2, width), big_keep=b(4, tok // 2, width),
        big_recv=b(4, tok // 2, width), big_rb=b(3, tok // 2, width), gpart=b(2, wide, width),
        zrecv=b(3, 3, wide, block), gres=b(3, block, wide), gnat=b(total, wide), znat=b(total, wide),
        spart=f(4, ROWS, wide), srecv=f(3, A_ROWS, wide), sfull=f(4, A_ROWS, wide),
        bpart=b(4, B_ROWS, wide), brecv=b(3, B_ROWS, wide), bfull=b(4, B_ROWS, wide), sown=f(SUB, wide),
        ggs=f(8, SUB, block), sg_s=f(tok // 2, width),
        ssem=pltpu.SemaphoreType.DMA((144,)), rsem=pltpu.SemaphoreType.DMA((144,)),
        lsem=pltpu.SemaphoreType.DMA((16,)),
    )
    outs = pl.pallas_call(
        fused_kernel,
        out_shape=[
            jax.ShapeDtypeStruct((tok, width), BF16),
            jax.ShapeDtypeStruct((tok, width), F32),
            jax.ShapeDtypeStruct((2, block, 4 * wide), BF16),
            jax.ShapeDtypeStruct((4 * wide, block), BF16),
            jax.ShapeDtypeStruct((48, 4 * wide), F32),
            jax.ShapeDtypeStruct((8, wide), F32),
            jax.ShapeDtypeStruct((1, block), F32),
        ],
        in_specs=[hbm] * 4 + [vm] * 10,
        out_specs=[hbm] * 4 + [vm] * 3,
        scratch_shapes=list(scratch.values()),
        compiler_params=pltpu.CompilerParams(
            collective_id=0, has_side_effects=True, vmem_limit_bytes=VMEM_LIMIT
        ),
    )(
        stream_in.reshape(tok, width), out_grad.reshape(tok, width), in_weight, out_weight, xproj_weight,
        dt_weight, a_log, convolution_weight.reshape(4, block), convolution_bias, step_size_bias,
        skip_term_scale, norm_gain, seg_ids, pad_mask,
    )
    steps = 2
    part = tok // steps

    def whole(*shape):
        return pl.BlockSpec(shape, lambda i: (0,) * len(shape))

    return pl.pallas_call(
        finish_kernel,
        grid=(steps,),
        out_shape=[
            jax.ShapeDtypeStruct((1, tok, width), BF16),
            jax.ShapeDtypeStruct((1, tok, width), F32),
            jax.ShapeDtypeStruct((block,), F32),
            jax.ShapeDtypeStruct((2, block, 4 * wide), F32),
            jax.ShapeDtypeStruct((4 * wide, block), F32),
            jax.ShapeDtypeStruct((24, 4 * wide), F32),
            jax.ShapeDtypeStruct((16, 4 * wide), F32),
            jax.ShapeDtypeStruct((4, 4 * wide), F32),
            jax.ShapeDtypeStruct((4, 1, wide), F32),
            jax.ShapeDtypeStruct((1, wide), F32),
            jax.ShapeDtypeStruct((1, wide), F32),
            jax.ShapeDtypeStruct((1, wide), F32),
        ],
        in_specs=[
            pl.BlockSpec((part, width), lambda i: (i, 0)),
            pl.BlockSpec((part, width), lambda i: (i, 0)),
            pl.BlockSpec((2, block // steps, 4 * wide), lambda i: (0, i, 0)),
            pl.BlockSpec((4 * wide // steps, block), lambda i: (i, 0)),
            whole(48, 4 * wide),
            whole(8, wide),
            whole(1, block),
        ],
        out_specs=[
            pl.BlockSpec((1, part, width), lambda i: (0, i, 0)),
            pl.BlockSpec((1, part, width), lambda i: (0, i, 0)),
            whole(block),
            pl.BlockSpec((2, block // steps, 4 * wide), lambda i: (0, i, 0)),
            pl.BlockSpec((4 * wide // steps, block), lambda i: (i, 0)),
            whole(24, 4 * wide),
            whole(16, 4 * wide),
            whole(4, 4 * wide),
            whole(4, 1, wide),
            whole(1, wide),
            whole(1, wide),
            whole(1, wide),
        ],
        compiler_params=pltpu.CompilerParams(vmem_limit_bytes=VMEM_LIMIT),
    )(*outs)


def finish_kernel(
    so_ref, sg_ref, wg_ref, wo_ref, sm_ref, cv_ref, gg_ref,
    so_out, sg_out, gg_out, wg_out, wo_out, xp_out, dtw_out, alog_out, cw_out, cb_out, dtb_out, skip_out,
):
    so_out[0] = so_ref[...]
    sg_out[0] = sg_ref[...]
    wg_out[...] = wg_ref[...].astype(F32)
    wo_out[...] = wo_ref[...].astype(F32)

    @pl.when(pl.program_id(0) == 0)
    def _():
        gg_out[...] = gg_ref[0]
        xp_out[...] = sm_ref[0:24, :]
        dtw_out[...] = sm_ref[24:40, :]
        alog_out[...] = sm_ref[40:44, :]
        for j in range(4):
            cw_out[j] = cv_ref[j : j + 1, :]
        cb_out[...] = cv_ref[4:5, :]
        dtb_out[...] = cv_ref[5:6, :]
        skip_out[...] = cv_ref[6:7, :]


def solution(mesh):
    in_specs = (
        P("dp", "ctx", None),
        P("dp"),
        P(None, "dp", "tp"),
        P("tp", "dp"),
        P("dp", "tp"),
        P("dp", "tp"),
        P("dp", "tp"),
        P(None, "tp", "dp"),
        P("tp", "dp"),
        P("tp", "dp"),
        P("tp", "dp"),
        P("dp", "ctx"),
        P("dp", "ctx"),
        P("dp", "ctx", None),
    )
    out_specs = (
        P("dp", "ctx", None),
        P("dp", "ctx", None),
        P("dp"),
        P(None, "dp", "tp"),
        P("tp", "dp"),
        P("dp", "tp"),
        P("dp", "tp"),
        P("dp", "tp"),
        P(None, "tp", "dp"),
        P("tp", "dp"),
        P("tp", "dp"),
        P("tp", "dp"),
    )

    def run(*args):
        stream, weight = args[0].shape, args[2].shape
        plane_fits = (mesh.shape["dp"], mesh.shape["ctx"], mesh.shape["tp"]) == (4, 4, 2)
        sizes_fit = stream == (4, 1024, 1024) and weight == (2, 1024, 2048)
        part = fused if plane_fits and sizes_fit else shards
        return jax.shard_map(
            part, mesh=mesh, in_specs=in_specs, out_specs=out_specs, check_vma=False
        )(*args)

    return run
```

```python
import math

import jax
import jax.numpy as jnp
from jax import lax
from jax.experimental import pallas as pl
from jax.experimental.pallas import tpu as pltpu
from jax.sharding import PartitionSpec as P

EPS = 1e-05
VMEM_LIMIT = 63 * 2**20


def from_behind(x, axis, by):
    count = lax.axis_size(axis)
    pairs = [(i, i + by) for i in range(count) if 0 <= i + by < count]
    return lax.ppermute(x, axis, pairs)


def entering(x, axis, combine, identity, reverse):
    count, position = (lax.axis_size(axis), lax.axis_index(axis))
    everything = jax.tree.map(
        lambda part, kind: lax.all_gather(part.astype(kind), axis), x, (jnp.bfloat16, jnp.bfloat16)
    )
    start = jax.tree.map(
        lambda part, zero: jnp.broadcast_to(jnp.asarray(zero, part.dtype), part.shape), x, identity
    )

    def step(k, before):
        at = count - 1 - k if reverse else k
        reached = at > position if reverse else at < position
        new = combine(
            before, jax.tree.map(lambda part, own: part[at].astype(own.dtype), everything, x)
        )
        return jax.tree.map(lambda a, b: jnp.where(reached, a, b), new, before)

    return lax.fori_loop(0, count, step, start)


def silu_slope(value):
    sigma = jax.nn.sigmoid(value)
    return sigma * (1.0 + value * (1.0 - sigma))


def link(first, second):
    return (first[0] * second[0], first[1] * second[0] + second[1])


def chain_prefix(decay, drive, backward):
    return lax.associative_scan(link, (decay, drive), reverse=backward, axis=1)


def shards(
    stream_in,
    norm_gain,
    in_weight,
    out_weight,
    xproj_weight,
    dt_weight,
    a_log,
    convolution_weight,
    convolution_bias,
    step_size_bias,
    skip_term_scale,
    seg_ids,
    pad_mask,
    out_grad,
):
    gathered = (
        lax.all_gather(norm_gain, "dp", axis=0, tiled=True),
        lax.all_gather(in_weight, "dp", axis=1, tiled=True),
        lax.all_gather(out_weight, "dp", axis=1, tiled=True),
        lax.all_gather(xproj_weight, "dp", axis=0, tiled=True),
        lax.all_gather(dt_weight, "dp", axis=0, tiled=True),
        lax.all_gather(a_log, "dp", axis=0, tiled=True),
        lax.all_gather(convolution_weight, "dp", axis=2, tiled=True),
        lax.all_gather(convolution_bias, "dp", axis=1, tiled=True),
        lax.all_gather(step_size_bias, "dp", axis=1, tiled=True),
        lax.all_gather(skip_term_scale, "dp", axis=1, tiled=True),
    )
    (
        gain_full,
        win_full,
        wout_full,
        xproj_full,
        dtw_full,
        alog_full,
        convw_full,
        convb_full,
        dtb_full,
        skip_full,
    ) = gathered
    seq_count, tok_count, model_width = stream_in.shape
    channels = win_full.shape[2]
    low_dims = dtw_full.shape[0]
    states = alog_full.shape[0]
    kernel = convw_full.shape[0]
    conv_lag = kernel - 1
    row_count = seq_count * tok_count
    block_len = math.gcd(tok_count, 128)
    block_count = tok_count // block_len
    gain_vec = gain_full.astype(jnp.float32)
    conv_taps = convw_full.reshape(kernel, channels).astype(jnp.float32)
    conv_shift = convb_full.reshape(channels).astype(jnp.float32)
    dt_shift = dtb_full.reshape(channels).astype(jnp.float32)
    skip_vec = skip_full.reshape(channels).astype(jnp.float32)
    a_neg = -jnp.exp(alog_full.astype(jnp.float32))

    def to_blocks(array):
        shaped = array.reshape((seq_count, block_count, block_len) + array.shape[2:])
        return jnp.moveaxis(shaped, 1, 0)

    def from_blocks(array):
        return jnp.moveaxis(array, 0, 1).reshape((seq_count, tok_count) + array.shape[3:])

    def decay_of(dt_block, keep_block):
        return jnp.exp(dt_block[:, :, None, :] * a_neg) * keep_block[:, :, None, None]

    def drive_of(dt_block, act_block, b_block):
        return (dt_block * act_block)[:, :, None, :] * b_block[:, :, :, None]

    def reverse_terms(decay, rhs, carry_in):
        shifted = jnp.concatenate([decay[:, 1:], jnp.zeros_like(decay[:, :1])], axis=1)
        rhs = rhs.at[:, -1].add(carry_in)
        _, grads = chain_prefix(shifted, rhs, True)
        return (grads, decay[:, 0] * grads[:, 0])

    stream = stream_in.astype(jnp.float32)
    rstd = lax.rsqrt(jnp.mean(stream * stream, axis=2, keepdims=True) + EPS)
    normed = (stream * rstd * gain_vec).astype(jnp.bfloat16)
    normed_flat = normed.reshape(row_count, model_width)
    projected = jnp.einsum(
        "rd,kdc->krc", normed_flat, win_full, preferred_element_type=jnp.float32
    ).astype(jnp.bfloat16)
    inner = projected[0].reshape(seq_count, tok_count, channels)
    gate_vals = projected[1].astype(jnp.float32).reshape(seq_count, tok_count, channels)
    seg_low = seg_ids.astype(jnp.bfloat16)
    prev_inner, prev_seg = from_behind(
        (inner[:, tok_count - conv_lag :], seg_low[:, tok_count - conv_lag :]), "ctx", 1
    )
    inner_vals = inner.astype(jnp.float32)
    prev_vals = prev_inner.astype(jnp.float32)
    seg_float = seg_ids.astype(jnp.float32)
    prev_segf = prev_seg.astype(jnp.float32)
    windows = []
    same_list = []
    pre = jnp.zeros((seq_count, tok_count, channels), jnp.float32) + conv_shift
    for offset in range(kernel):
        if offset == 0:
            window = inner_vals
            seg_window = seg_float
        else:
            window = jnp.concatenate(
                [prev_vals[:, conv_lag - offset :], inner_vals[:, : tok_count - offset]], axis=1
            )
            seg_window = jnp.concatenate(
                [prev_segf[:, conv_lag - offset :], seg_float[:, : tok_count - offset]], axis=1
            )
        same = (seg_window == seg_float).astype(jnp.float32)
        windows.append(window)
        same_list.append(same)
        pre = pre + conv_taps[conv_lag - offset] * window * same[:, :, None]
    keep = same_list[1]
    act = (pre * jax.nn.sigmoid(pre)).astype(jnp.bfloat16)
    act_flat = act.reshape(row_count, channels)
    act_vals = act.astype(jnp.float32)
    mixed_part = jnp.einsum("rc,wc->rw", act_flat, xproj_full, preferred_element_type=jnp.float32)
    mixed = lax.psum(mixed_part, "tp")
    low_rank = mixed[:, :low_dims].astype(jnp.bfloat16)
    b_in = mixed[:, low_dims : low_dims + states].reshape(seq_count, tok_count, states)
    c_out = mixed[:, low_dims + states :].reshape(seq_count, tok_count, states)
    dt_arg = (
        jnp.dot(low_rank, dtw_full, preferred_element_type=jnp.float32).reshape(
            seq_count, tok_count, channels
        )
        + dt_shift
    )
    dt_values = jax.nn.softplus(dt_arg)

    def forward_block(carry, piece):
        start, through = carry
        dt_block, act_block, b_block, c_block, keep_block = piece
        decay = decay_of(dt_block, keep_block)
        prods, local = chain_prefix(decay, drive_of(dt_block, act_block, b_block), False)
        hidden = local + prods * start[:, None]
        outputs = jnp.sum(c_block[:, :, :, None] * hidden, axis=2)
        return ((hidden[:, -1], through * prods[:, -1]), (outputs, start, through))

    zero_state = jnp.zeros((seq_count, states, channels), jnp.float32)
    one_state = jnp.ones_like(zero_state)
    dt_blocks = to_blocks(dt_values)
    act_blocks = to_blocks(act_vals)
    b_blocks = to_blocks(b_in)
    c_blocks = to_blocks(c_out)
    keep_blocks = to_blocks(keep)
    (last_state, through), (y_blocks, local_starts, befores) = lax.scan(
        forward_block,
        (zero_state, one_state),
        (dt_blocks, act_blocks, b_blocks, c_blocks, keep_blocks),
    )
    _, entry_state = entering((through, last_state), "ctx", link, (one_state, zero_state), False)
    cum_dt = jnp.cumsum(dt_values, axis=1)
    alive = jnp.cumprod(keep, axis=1)
    cum_blocks = to_blocks(cum_dt)

    def correct(piece):
        cum_block, c_block, alive_block = piece
        carried = jnp.exp(cum_block[:, :, None, :] * a_neg) * entry_state[:, None]
        return alive_block[:, :, None] * jnp.sum(c_block[:, :, :, None] * carried, axis=2)

    corrections = from_blocks(lax.map(correct, (cum_blocks, c_blocks, to_blocks(alive))))
    y_total = from_blocks(y_blocks) + corrections + skip_vec * act_vals
    gate_act = gate_vals * jax.nn.sigmoid(gate_vals)
    gated_flat = (y_total * gate_act).astype(jnp.bfloat16).reshape(row_count, channels)
    branch_part = jnp.dot(gated_flat, wout_full, preferred_element_type=jnp.float32)
    branch = (
        lax.psum(branch_part.astype(jnp.bfloat16), "tp")
        .astype(jnp.float32)
        .reshape(seq_count, tok_count, model_width)
    )
    mask_float = pad_mask.astype(jnp.float32)
    stream_out = (stream + mask_float[:, :, None] * branch).astype(jnp.bfloat16)
    masked_flat = (out_grad * pad_mask[:, :, None].astype(jnp.bfloat16)).reshape(
        row_count, model_width
    )
    grad_wout = jnp.einsum("rc,rd->cd", gated_flat, masked_flat, preferred_element_type=jnp.float32)
    grad_gated = jnp.einsum(
        "rd,cd->rc", masked_flat, wout_full, preferred_element_type=jnp.float32
    ).reshape(seq_count, tok_count, channels)
    grad_y = grad_gated * gate_act
    grad_gate = (grad_gated * y_total * silu_slope(gate_vals)).astype(jnp.bfloat16)
    grad_skip = jnp.sum(grad_y * act_vals, axis=(0, 1))
    gy_blocks = to_blocks(grad_y)
    true_starts = local_starts + befores * entry_state[None]

    def back_core(carry_in, piece):
        dt_block, act_block, b_block, c_block, keep_block, gy_block, start = piece
        decay = decay_of(dt_block, keep_block)
        prods, local = chain_prefix(decay, drive_of(dt_block, act_block, b_block), False)
        hidden = local + prods * start[:, None]
        earlier = jnp.concatenate([start[:, None], hidden[:, :-1]], axis=1)
        grads, carry_out = reverse_terms(
            decay, c_block[:, :, :, None] * gy_block[:, :, None, :], carry_in
        )
        stepped = earlier * decay
        weighted = grads * stepped
        along_b = jnp.sum(grads * b_block[:, :, :, None], axis=2)
        grad_dt = jnp.sum(weighted * a_neg, axis=2) + along_b * act_block
        grad_act = along_b * dt_block
        grad_b = jnp.sum(grads * (dt_block * act_block)[:, :, None, :], axis=3)
        grad_c = jnp.sum(gy_block[:, :, None, :] * hidden, axis=3)
        return (carry_out, weighted, stepped, (grad_dt, grad_act, grad_b, grad_c))

    back_pieces = (dt_blocks, act_blocks, b_blocks, c_blocks, keep_blocks, gy_blocks, true_starts)
    zero_acc = jnp.zeros((states, channels), jnp.float32)
    cum_end = cum_dt[:, -1]
    suffix = jnp.flip(jnp.cumprod(jnp.flip(keep, axis=1), axis=1), axis=1)
    rest = jnp.concatenate([suffix[:, 1:], jnp.ones((seq_count, 1), jnp.float32)], axis=1)
    rest_blocks = to_blocks(rest)

    def reach_of(cum_block, rest_block):
        return (
            jnp.exp((cum_end[:, None, None, :] - cum_block[:, :, None, :]) * a_neg)
            * rest_block[:, :, None, None]
        )

    def kept_back(carry, piece):
        carry_in, a_acc, q_acc = carry
        core_piece = piece[:7]
        carry_out, weighted, stepped, terms = back_core(carry_in, core_piece)
        dt_block = core_piece[0]
        along = stepped * reach_of(piece[7], piece[8])
        a_acc = a_acc + jnp.sum(weighted * dt_block[:, :, None, :], axis=(0, 1))
        q_acc = q_acc + jnp.sum(along * dt_block[:, :, None, :], axis=1)
        return ((carry_out, a_acc, q_acc), terms + (along,))

    (edge_grad, a_local, q_total), (base_dt, base_act, base_b, grad_c_blocks, along_blocks) = (
        lax.scan(
            kept_back,
            (zero_state, zero_acc, zero_state),
            back_pieces + (cum_blocks, rest_blocks),
            reverse=True,
        )
    )
    _, after_grad = entering((through, edge_grad), "ctx", link, (one_state, zero_state), True)

    def adjust(piece):
        dt_block, act_block, b_block, cum_block, rest_block, along = piece
        extra = reach_of(cum_block, rest_block) * after_grad[:, None]
        along_b = jnp.sum(extra * b_block[:, :, :, None], axis=2)
        grad_dt = jnp.sum(along * after_grad[:, None] * a_neg, axis=2) + along_b * act_block
        grad_act = along_b * dt_block
        grad_b = jnp.sum(extra * (dt_block * act_block)[:, :, None, :], axis=3)
        return (grad_dt, grad_act, grad_b)

    add_dt, add_act, add_b = lax.map(
        adjust, (dt_blocks, act_blocks, b_blocks, cum_blocks, rest_blocks, along_blocks)
    )
    grad_dt_blocks = base_dt + add_dt
    grad_act_blocks = base_act + add_act
    grad_b_blocks = base_b + add_b
    a_total = a_local + jnp.sum(q_total * after_grad, axis=0)
    grad_lin = from_blocks(grad_dt_blocks) * jax.nn.sigmoid(dt_arg)
    grad_dtb = jnp.sum(grad_lin, axis=(0, 1))
    grad_lin_low = grad_lin.reshape(row_count, channels).astype(jnp.bfloat16)
    grad_dtw = jnp.einsum("rk,rc->kc", low_rank, grad_lin_low, preferred_element_type=jnp.float32)
    grad_rank = jnp.einsum("rc,kc->rk", grad_lin_low, dtw_full, preferred_element_type=jnp.float32)
    grad_mixed_part = jnp.concatenate(
        [
            grad_rank,
            from_blocks(grad_b_blocks).reshape(row_count, states),
            from_blocks(grad_c_blocks).reshape(row_count, states),
        ],
        axis=1,
    )
    grad_mixed = lax.psum(grad_mixed_part, "tp").astype(jnp.bfloat16)
    grad_xproj = jnp.einsum("rw,rc->wc", grad_mixed, act_flat, preferred_element_type=jnp.float32)
    grad_act_total = (
        grad_y * skip_vec
        + from_blocks(grad_act_blocks)
        + jnp.dot(grad_mixed, xproj_full, preferred_element_type=jnp.float32).reshape(
            seq_count, tok_count, channels
        )
    )
    grad_pre = grad_act_total * silu_slope(pre)
    grad_convb = jnp.sum(grad_pre, axis=(0, 1))
    tap_grads = [None] * kernel
    grad_inner = jnp.zeros((seq_count, tok_count, channels), jnp.float32)
    tail_grad = jnp.zeros((seq_count, conv_lag, channels), jnp.float32)
    for offset in range(kernel):
        weighted_pre = grad_pre * same_list[offset][:, :, None]
        tap_grads[conv_lag - offset] = jnp.sum(weighted_pre * windows[offset], axis=(0, 1))
        scaled_pre = weighted_pre * conv_taps[conv_lag - offset]
        if offset == 0:
            grad_inner = grad_inner + scaled_pre
        else:
            grad_inner = grad_inner + jnp.concatenate(
                [scaled_pre[:, offset:], jnp.zeros((seq_count, offset, channels), jnp.float32)],
                axis=1,
            )
            tail_grad = tail_grad.at[:, conv_lag - offset :].add(scaled_pre[:, :offset])
    grad_convw = jnp.stack(tap_grads)
    sent_back = from_behind(tail_grad, "ctx", -1)
    grad_inner = grad_inner.at[:, tok_count - conv_lag :].add(sent_back)
    grad_proj = jnp.stack(
        [
            grad_inner.astype(jnp.bfloat16).reshape(row_count, channels),
            grad_gate.reshape(row_count, channels),
        ]
    )
    grad_win = jnp.einsum("rd,krc->kdc", normed_flat, grad_proj, preferred_element_type=jnp.float32)
    grad_norm_part = jnp.einsum(
        "krc,kdc->rd", grad_proj, win_full, preferred_element_type=jnp.float32
    )
    grad_norm = lax.psum(grad_norm_part, "tp").reshape(seq_count, tok_count, model_width)
    grad_gain = jnp.sum(grad_norm * stream * rstd, axis=(0, 1))
    scaled = grad_norm * gain_vec
    stream_grad = (
        out_grad.astype(jnp.float32)
        + rstd * scaled
        - stream * (rstd * rstd * rstd) * jnp.mean(scaled * stream, axis=2, keepdims=True)
    )
    grad_alog = a_total * a_neg
    local_grads = (
        grad_gain,
        grad_win,
        grad_wout,
        grad_xproj,
        grad_dtw,
        grad_alog,
        grad_convw.reshape(kernel, 1, channels),
        grad_convb.reshape(1, channels),
        grad_dtb.reshape(1, channels),
        grad_skip.reshape(1, channels),
    )
    summed = lax.psum(
        (
            local_grads[0],
            local_grads[1],
            local_grads[2],
            local_grads[3],
            local_grads[4],
            local_grads[5],
            local_grads[6],
            local_grads[7],
            local_grads[8],
            local_grads[9],
        ),
        "ctx",
    )
    owned = (
        lax.psum_scatter(summed[0], "dp", scatter_dimension=0, tiled=True),
        lax.psum_scatter(summed[1], "dp", scatter_dimension=1, tiled=True),
        lax.psum_scatter(summed[2], "dp", scatter_dimension=1, tiled=True),
        lax.psum_scatter(summed[3], "dp", scatter_dimension=0, tiled=True),
        lax.psum_scatter(summed[4], "dp", scatter_dimension=0, tiled=True),
        lax.psum_scatter(summed[5], "dp", scatter_dimension=0, tiled=True),
        lax.psum_scatter(summed[6], "dp", scatter_dimension=2, tiled=True),
        lax.psum_scatter(summed[7], "dp", scatter_dimension=1, tiled=True),
        lax.psum_scatter(summed[8], "dp", scatter_dimension=1, tiled=True),
        lax.psum_scatter(summed[9], "dp", scatter_dimension=1, tiled=True),
    )
    return (
        stream_out,
        stream_grad,
        owned[0],
        owned[1],
        owned[2],
        owned[3],
        owned[4],
        owned[5],
        owned[6],
        owned[7],
        owned[8],
        owned[9],
    )


F32 = jnp.float32
BF16 = jnp.bfloat16
MESH = pl.DeviceIdType.MESH
LOG2E = math.log2(math.e)
LN2 = math.log(2.0)
KILL = 1e30
SUB = 8
LANES = 128
PAD = 24
ROWS = 64
XP, DTW, ALOG, ROWS_P = 0, 24, 40, 48
CONVW, CONVB, DTB, SKIP, GAIN = 0, 4, 5, 6, 7
A_DTW, A_ALOG, A_DTB, A_SKIP, A_ROWS = 0, 16, 20, 21, 24
B_XP, B_CONVW, B_CONVB, B_ROWS = 0, 24, 28, 32
NT = (((1,), (1,)), ((), ()))
TN = (((0,), (0,)), ((), ()))


def dot(a, b):
    return jnp.dot(a, b, preferred_element_type=F32)


def dot_nt(a, b):
    return lax.dot_general(a, b, NT, preferred_element_type=F32)


def dot_tn(a, b):
    return lax.dot_general(a, b, TN, preferred_element_type=F32)


def at8(start, size):
    return pl.ds(pl.multiple_of(start, 8), size)


def sigmoid(v):
    return 0.5 + 0.5 * jnp.tanh(0.5 * v)


def log_one_plus(v):
    series = v * (1.0 - v * (0.5 - v * (1.0 / 3.0 - v * 0.25)))
    return jnp.where(v < 0.01, series, jnp.log(1.0 + v))


def one_less_exp(v):
    series = v * (1.0 - v * (0.5 - v * (1.0 / 6.0 - v * (1.0 / 24.0 - v * (1.0 / 120.0)))))
    return jnp.where(v < 0.1, series, 1.0 - jnp.exp(-v))


def prefix_of(ends, prods):
    row = lax.broadcasted_iota(jnp.int32, ends.shape, 0)
    for gap in (1, 2, 4):
        ok = row >= gap
        ends = ends + prods * jnp.where(ok, pltpu.roll(ends, gap, 0), 0.0)
        prods = prods * jnp.where(ok, pltpu.roll(prods, gap, 0), 1.0)
    return jnp.where(row >= 1, pltpu.roll(ends, 1, 0), 0.0)


def suffix_of(ends, prods):
    row = lax.broadcasted_iota(jnp.int32, ends.shape, 0)
    for gap in (1, 2, 4):
        ok = row < SUB - gap
        ends = ends + prods * jnp.where(ok, pltpu.roll(ends, SUB - gap, 0), 0.0)
        prods = prods * jnp.where(ok, pltpu.roll(prods, SUB - gap, 0), 1.0)
    return jnp.where(row < SUB - 1, pltpu.roll(ends, SUB - 1, 0), 0.0)


def fused_kernel(
    x_ref, og_ref, win_ref, wout_ref, xproj_ref, dtw_ref, alog_ref, convw_ref, convb_ref, dtb_ref,
    skip_ref, gain_ref, seg_ref, mask_ref,
    so_out, sg_out, wg_out, wo_out, sm_out, cv_out, gg_out,
    so_s, x_half, og_half, xf, mg, w_s, wo_s, early, pk_f, pk_s, segs, segp, maskc, nat, inner, slope, act, gate, dt, yg, y,
    bc, h, a2b, st, gin, cum, alg, full, full2, mp, sum_a, recv_a, recv_b, xp, dtwp,
    big_send, big_keep, big_recv, big_rb, gpart, zrecv, gres, gnat, znat, spart, srecv, sfull, bpart, brecv, bfull, sown, ggs,
    sg_s, ssem, rsem, lsem,
):
    z, c, k = lax.axis_index("dp"), lax.axis_index("ctx"), lax.axis_index("tp")
    nz = lax.axis_size("dp")
    px, py = lax.rem(c, 2), c // 2
    sib = (z, c, 1 - k)
    plane = [None, py * 2 + (1 - px), (1 - py) * 2 + px, (1 - py) * 2 + (1 - px)]
    peers = [None] + [(z, plane[p], k) for p in (1, 2, 3)]
    toward = [None] + [lax.rem(z + d, nz) for d in (1, 2, 3)]
    behind = [None] + [lax.rem(z + nz - d, nz) for d in (1, 2, 3)]
    lines = [None] + [(toward[d], c, k) for d in (1, 2, 3)]
    count = [0]
    local_count = [0]
    pending = []

    def send(src, dst, device):
        i = count[0]
        count[0] += 1
        copy = pltpu.make_async_remote_copy(
            src_ref=src, dst_ref=dst, send_sem=ssem.at[i], recv_sem=rsem.at[i],
            device_id=device, device_id_type=MESH,
        )
        copy.start()
        pending.append(copy)
        return copy

    def local(src, dst):
        i = local_count[0]
        local_count[0] += 1
        copy = pltpu.make_async_copy(src, dst, lsem.at[i])
        copy.start()
        return copy

    def flush(copies):
        for copy in copies:
            copy.wait_send()
            pending[:] = [other for other in pending if other is not copy]

    tok = maskc.shape[0]
    half = tok // 2
    total = xf.shape[0]
    width = xf.shape[1]
    steps = total // SUB
    states = h.shape[1]
    wide = 2 * LANES
    block = w_s.shape[1] // 4
    tiles = (0, 1)
    rb = 128
    nblk = total // rb

    def lanes(t):
        return slice(t * LANES, (t + 1) * LANES)

    def blk(i):
        return pl.ds(pl.multiple_of(i * rb, rb), rb)

    wb = 512

    def wide_blk(i):
        return pl.ds(pl.multiple_of(i * wb, wb), wb)

    def tau_rows(tau):
        return at8(tau * SUB, SUB)

    def loop(n, body, unroll=1):
        def step(i, carry):
            body(i)
            return carry

        lax.fori_loop(0, n, step, 0, unroll=unroll)

    barrier = pltpu.get_barrier_semaphore()
    everyone = [sib] + peers[1:] + [(z, plane[p], 1 - k) for p in (1, 2, 3)] + lines[1:]
    for device in everyone:
        pl.semaphore_signal(barrier, inc=1, device_id=device, device_id_type=MESH)
    chans = pl.ds(pl.multiple_of(c * wide, wide), wide)
    spart[...] = jnp.zeros_like(spart)
    spart[0, XP : XP + 24, :] = xproj_ref[:, chans].astype(F32)
    spart[0, DTW : DTW + 16, :] = dtw_ref[:, chans].astype(F32)
    spart[0, ALOG : ALOG + 4, :] = alog_ref[:, chans].astype(F32)
    early[z, CONVW : CONVW + 4, :] = convw_ref[...].astype(F32)
    early[z, CONVB : CONVB + 1, :] = convb_ref[...].astype(F32)
    early[z, DTB : DTB + 1, :] = dtb_ref[...].astype(F32)
    early[z, SKIP : SKIP + 1, :] = skip_ref[...].astype(F32)
    early[z, GAIN : GAIN + 1, :] = gain_ref[...].astype(F32).reshape(1, block)
    pk_s[z] = spart[0, 0:ROWS_P, :].astype(BF16)
    segs[c] = jnp.broadcast_to(seg_ref[...], (SUB, tok))
    pl.semaphore_wait(barrier, len(everyone))

    my_half = pl.ds(pl.multiple_of(c * tok + k * half, half), half)
    s_seg = [send(segs.at[c], segs.at[c], peers[p]) for p in (1, 2, 3)]
    s_x = [send(x_ref.at[pl.ds(pl.multiple_of(k * half, half), half)], xf.at[my_half], peers[p]) for p in (3, 1, 2)]
    s_early = [send(early.at[z], early.at[z], lines[d]) for d in (1, 2, 3)]

    zrows = pl.ds(pl.multiple_of(z * block, block), block)

    def weight(which):
        return [
            send(win_ref.at[which, :, chans], w_s.at[which, zrows, :], lines[d]) for d in (1, 2, 3)
        ]

    s_wx = weight(0)
    s_pack = [send(pk_s.at[z], pk_s.at[z], lines[d]) for d in (1, 2, 3)]
    own_w = [local(win_ref.at[i, :, chans], w_s.at[i, zrows, :]) for i in (0, 1)]
    zcols = pl.ds(pl.multiple_of(z * block, block), block)
    own_wo = local(wout_ref.at[chans, :], wo_s.at[:, zcols])

    own_rows = pl.ds(pl.multiple_of(c * tok, tok), tok)
    half_rows = pl.ds(pl.multiple_of(k * half, half), half)
    own_x = local(x_ref, xf.at[own_rows, :])
    own_og = local(og_ref, mg.at[own_rows, :])
    own_half = [local(x_ref.at[half_rows, :], x_half), local(og_ref.at[half_rows, :], og_half)]
    mrow = mask_ref[...].astype(F32)
    for b in range(tok // LANES):
        rows = slice(b * LANES, (b + 1) * LANES)
        maskc[rows, :] = jnp.broadcast_to(mrow[:, rows], (LANES, LANES)).T
    mcol = jnp.concatenate([maskc[...]] * (width // LANES), axis=1)
    own_og.wait()
    mg[own_rows, :] = (mg[own_rows, :].astype(F32) * mcol).astype(BF16)

    for copy in s_early:
        copy.wait_recv()
    gain_row = jnp.concatenate([early[i, GAIN : GAIN + 1, :] for i in range(4)], axis=1)
    sown[...] = early[c]

    def param(row, t):
        return sown[row : row + 1, lanes(t)]

    for copy in s_seg:
        copy.wait_recv()
    for i in range(4):
        srow = segs[i, 0:1, :].astype(F32)
        for b in range(tok // LANES):
            rows = slice(b * LANES, (b + 1) * LANES)
            nat[0, i * tok + b * LANES : i * tok + (b + 1) * LANES, :] = jnp.broadcast_to(
                srow[:, rows], (LANES, LANES)
            ).T

    def seg_in(tau):
        segp[at8(PAD + tau * SUB, SUB), :] = nat[0, pl.ds(tau, SUB, stride=steps), :]

    loop(steps, seg_in, 8)
    sub_row = lax.broadcasted_iota(jnp.int32, (SUB, LANES), 0)

    def from_before(v, fill):
        return jnp.where(sub_row >= 1, pltpu.roll(v, 1, 0), fill)

    def from_after(v, fill):
        return jnp.where(sub_row < SUB - 1, pltpu.roll(v, SUB - 1, 0), fill)

    for j in range(3):
        segp[j * SUB : (j + 1) * SUB, :] = from_before(segp[total + j * SUB : total + (j + 1) * SUB, :], -1.0)
        segp[PAD + total + j * SUB : PAD + total + (j + 1) * SUB, :] = from_after(
            segp[PAD + j * SUB : PAD + (j + 1) * SUB, :], -2.0
        )

    def halves(copies, buf):
        relays = []
        for copy, p in zip(copies, (3, 1, 2)):
            copy.wait_recv()
            rows = pl.ds(pl.multiple_of(plane[p] * tok + k * half, half), half)
            relays.append(send(buf.at[rows], buf.at[rows], sib))
        return relays

    def norm(i):
        rows = pl.ds(pl.multiple_of(i * rb, rb), rb)
        v = xf[rows, :].astype(F32)
        r = lax.rsqrt(jnp.mean(v * v, axis=1, keepdims=True) + EPS)
        xf[rows, :] = (v * r * gain_row).astype(BF16)

    def project_block(i):
        rows = pl.ds(pl.multiple_of(i * tok, tok), tok)
        v = dot(xf[rows, :], w_s[0])
        for t in tiles:
            nat[t, rows, :] = v[:, lanes(t)]

    per = tok // rb
    own_x.wait()
    loop(per, lambda i: norm(c * per + i))
    r_x = halves(s_x, xf)
    for copy in s_wx:
        copy.wait_recv()
    own_w[0].wait()
    s_wz = weight(1)
    project_block(c)
    for copy, sent, p in zip(r_x, s_x, (3, 1, 2)):
        copy.wait_recv()
        flush([copy])
        loop(per, lambda i, p=p: norm(plane[p] * per + i))
        project_block(plane[p])

    def project(which, dst, off):
        def body(i):
            v = dot(xf[wide_blk(i), :], w_s[which])
            for t in tiles:
                nat[t, wide_blk(i), :] = v[:, lanes(t)]

        loop(total // wb, body)
        permute_in(dst, off, True)

    def permute_in(dst, off, rounded=False):
        def body(tau):
            for t in tiles:
                v = nat[t, pl.ds(tau, SUB, stride=steps), :]
                dst[t, at8(off + tau * SUB, SUB), :] = v.astype(BF16).astype(F32) if rounded else v

        loop(steps, body, 8)

    def permute_out(src, dst, which=tiles):
        def body(i):
            for s in range(SUB):
                for t in which:
                    nat[t, at8(s * steps + i * SUB, SUB), :] = src[t, pl.ds(i * SUB * SUB + s, SUB, stride=SUB), :]

        loop(steps // SUB, body)

        def cast(i):
            for t in which:
                dst[blk(i), lanes(t)] = nat[t, blk(i), :].astype(BF16)

        loop(nblk, cast)

    permute_in(inner, PAD, True)
    for t in tiles:
        for j in range(3):
            inner[t, j * SUB : (j + 1) * SUB, :] = from_before(inner[t, total + j * SUB : total + (j + 1) * SUB, :], 0.0)

    def conv(i):
        for t in tiles:
            mine = segp[at8(PAD + i * rb, rb), :]
            pre = jnp.zeros((rb, LANES), F32) + param(CONVB, t)
            for j in range(4):
                window = inner[t, at8(PAD + i * rb - j * SUB, rb), :]
                if j:
                    window = jnp.where(segp[at8(PAD + i * rb - j * SUB, rb), :] == mine, window, 0.0)
                pre = pre + param(CONVW + 3 - j, t) * window
            s = sigmoid(pre)
            act[t, blk(i), :] = (pre * s).astype(BF16).astype(F32)
            slope[t, blk(i), :] = s * (1.0 + pre * (1.0 - s))

    loop(nblk, conv)

    def tiles_bf(ref, i):
        return jnp.concatenate([ref[t, blk(i), :] for t in tiles], axis=1).astype(BF16)

    for copy in s_pack:
        copy.wait_recv()
    for i in range(4):
        pk_f[i] = pk_s[i].astype(F32)
    for i in range(4):
        alg[4 * i : 4 * i + 4, :] = pk_f[i, ALOG : ALOG + 4, :]
    xp_rows = jnp.concatenate([pk_f[i, XP : XP + 24, :] for i in range(4)] + [jnp.zeros((32, wide), F32)], axis=0)
    xp[...] = xp_rows.astype(BF16)
    dt_rows = jnp.concatenate([pk_f[i, DTW : DTW + 16, :] for i in range(4)] + [jnp.zeros((64, wide), F32)], axis=0)
    dtwp[...] = dt_rows.astype(BF16)
    a2v = -jnp.exp(alg[...]) * LOG2E
    for n in range(states):
        for t in tiles:
            a2b[t, n] = jnp.broadcast_to(a2v[n : n + 1, lanes(t)], (SUB, LANES))

    def mix(i):
        mp[i] = dot_nt(tiles_bf(act, i), xp[...])

    loop(nblk, mix)

    def plane_sum(out, between):
        first = send(mp.at[pl.ds((1 - k) * 4, 4)], recv_a, sib)
        between[0]()
        first.wait_recv()
        for i in range(4):
            sum_a[i] = (mp[k * 4 + i] + recv_a[i]).astype(BF16)
        second = [send(sum_a.at[plane[p]], recv_b.at[p - 1], peers[p]) for p in (3, 1, 2)]
        between[1]()
        for copy in second:
            copy.wait_recv()
        mine = k * 4 + c
        v = mp[mine] + recv_a[c]
        for p in range(3):
            v = v + recv_b[p].astype(F32)
        out[mine] = v.astype(BF16)
        third = [send(out.at[mine], out.at[mine], peers[p]) for p in (3, 1, 2)]
        third.append(send(out.at[mine], out.at[mine], sib))
        between[2]()
        fourth = []
        for copy, p in zip(third, (3, 1, 2)):
            copy.wait_recv()
            there = k * 4 + plane[p]
            fourth.append(send(out.at[there], out.at[there], sib))
        between[3]()
        for copy in [third[3]] + fourth:
            copy.wait_recv()
        return [first] + second

    late = {}

    def send_wo():
        for copy in s_wz:
            copy.wait_recv()
        own_w[1].wait()
        late["wo"] = [send(wout_ref.at[chans, :], wo_s.at[:, zcols], lines[d]) for d in (1, 2, 3)]

    def gates():
        project(1, gate, 0)

    def nothing():
        pass

    def send_mg():
        late["mg"] = [send(mg.at[my_half], mg.at[my_half], peers[p]) for p in (3, 1, 2)]

    def gap():
        send_mg()
        send_wo()
        gates()

    first_sum = plane_sum(full, [nothing, nothing, nothing, gap])

    def steps_of(i):
        arg = dot(full[i], dtwp[...])
        for t in tiles:
            v = arg[:, lanes(t)] + param(DTB, t)
            dt[t, blk(i), :] = jnp.maximum(v, 0.0) + log_one_plus(jnp.exp(-jnp.abs(v)))

    loop(nblk, steps_of)

    flat = full[...].reshape(total, LANES)
    row = lax.broadcasted_iota(jnp.int32, (LANES, wide), 0)
    col = lax.broadcasted_iota(jnp.int32, (LANES, wide), 1) // LANES
    for n in range(0, 2 * states, 2):
        v = dot(flat, jnp.where(row == 64 + n + col, 1.0, 0.0).astype(BF16))
        for t in tiles:
            bc[n + t] = v[:, lanes(t)]

    def dts(t, tau):
        v = dt[t, tau_rows(tau), :]
        r = at8(PAD + tau * SUB, SUB)
        p = at8(PAD + tau * SUB - SUB, SUB)
        return v, jnp.where(segp[r, :] == segp[p, :], v, KILL)

    for t in tiles:

        def ends(tau, carry, t=t):
            v, killed = dts(t, tau)
            drive = v * act[t, tau_rows(tau), :]
            new = [
                carry[n] * jnp.exp2(killed * a2b[t, n]) + drive * bc[n, tau_rows(tau), :] for n in range(states)
            ]
            return tuple(new) + (carry[states] + killed,)

        zero = jnp.zeros((SUB, LANES), F32)
        got = lax.fori_loop(0, steps, ends, (zero,) * (states + 1), unroll=8)
        cum[t] = got[states]
        for n in range(states):
            st[t, n] = prefix_of(got[n], jnp.exp2(got[states] * a2b[t, n]))

    for t in tiles:
        if t:
            late["mg"] = halves(late["mg"], mg)
        for n in range(states):
            h[t, n, 0:SUB, :] = st[t, n]

        def forward(tau, carry, t=t):
            v, killed = dts(t, tau)
            drive = v * act[t, tau_rows(tau), :]
            new, parts = [], [None] * 4
            for n in range(states):
                s = carry[n] * jnp.exp2(killed * a2b[t, n]) + drive * bc[n, tau_rows(tau), :]
                h[t, n, at8(tau * SUB + SUB, SUB), :] = s
                o = s * bc[states + n, tau_rows(tau), :]
                parts[n % 4] = o if parts[n % 4] is None else parts[n % 4] + o
                new.append(s)
            y[t, tau_rows(tau), :] = (parts[0] + parts[1]) + (parts[2] + parts[3])
            return tuple(new)

        lax.fori_loop(0, steps, forward, tuple(st[t, n] for n in range(states)), unroll=8)

    for copy in late["mg"] + late["wo"]:
        copy.wait_recv()
    own_wo.wait()

    def ograd(i):
        v = dot_nt(mg[wide_blk(i), :], wo_s[...])
        for t in tiles:
            nat[t, wide_blk(i), :] = v[:, lanes(t)]

    loop(total // wb, ograd)
    gb = SUB * SUB

    def strided(t, i):
        return jnp.concatenate([nat[t, pl.ds(i * SUB + u, SUB, stride=steps), :] for u in range(SUB)], axis=0)

    def gating(i, carry):
        new = []
        rows = pl.ds(pl.multiple_of(i * gb, gb), gb)
        for t in tiles:
            gv, ov, av = gate[t, rows, :], strided(t, i), act[t, rows, :]
            s = sigmoid(gv)
            ytot = y[t, rows, :] + param(SKIP, t) * av
            gy = ov * (gv * s)
            yg[t, rows, :] = gy
            y[t, rows, :] = ytot * (gv * s)
            gate[t, rows, :] = ov * ytot * (s * (1.0 + gv * (1.0 - s)))
            new.append(carry[t] + jnp.sum((gy * av).reshape(SUB, SUB, LANES), axis=0))
        return tuple(new)

    zero = jnp.zeros((SUB, LANES), F32)
    skip_sum = lax.fori_loop(0, total // gb, gating, (zero, zero))
    permute_out(y, gnat)
    permute_out(gate, znat)

    def owner_rows(i, q):
        return pl.ds(pl.multiple_of(i * tok + q * half, half), half)

    order = (3, 1, 2, 0)
    groups = width // wide
    turns = (0, 2, 1, 3)

    def fill(dst, j, q, lefts, right, more=False):
        cols = slice(j * wide, (j + 1) * wide)
        there = [plane[p] if p else c for p in order]
        rows = [jnp.concatenate([left[owner_rows(i, q), :] for i in there], axis=0) for left in lefts]
        v = right(rows, cols)
        for i, p in enumerate(order):
            piece = v[i * half : (i + 1) * half, :]
            if more:
                piece = piece + dst[p, :, cols].astype(F32)
            dst[p, :, cols] = piece.astype(BF16)

    def start_rows(lefts, right, more=False):
        first = {}
        for j in turns:
            cols = slice(j * wide, (j + 1) * wide)
            fill(big_send, j, 1 - k, lefts, right, more)
            first[j] = send(big_send.at[:, :, cols], big_recv.at[:, :, cols], sib)
        return first

    def ways(j):
        return (1, 2) if j < groups // 2 else (2, 1)

    def middle_rows(first, lefts=None, right=None):
        second = {}
        for j in turns:
            cols = slice(j * wide, (j + 1) * wide)
            if lefts:
                fill(big_keep, j, k, lefts, right, True)
            first[j].wait_recv()
            for p in order:
                big_keep[p, :, cols] = (big_keep[p, :, cols].astype(F32) + big_recv[p, :, cols].astype(F32)).astype(BF16)
            near, far = ways(j)
            second[j] = [
                send(big_keep.at[3, :, cols], big_rb.at[1, :, cols], peers[near]),
                send(big_keep.at[near, :, cols], big_rb.at[0, :, cols], peers[near]),
            ]
        return second

    def pass_rows(second):
        third = []
        for j in turns:
            cols = slice(j * wide, (j + 1) * wide)
            near, far = ways(j)
            second[j][0].wait_recv()
            big_keep[far, :, cols] = (big_keep[far, :, cols].astype(F32) + big_rb[1, :, cols].astype(F32)).astype(BF16)
            third.append(send(big_keep.at[far, :, cols], big_rb.at[2, :, cols], peers[far]))
        return [second[j][1] for j in turns] + third, [second[j][0] for j in turns]

    def end_rows(second):
        for copy in second:
            copy.wait_recv()
        return big_keep[0].astype(F32) + big_rb[0].astype(F32) + big_rb[2].astype(F32)

    def branch_part(rows, cols):
        return dot(rows[0], wo_s[:, cols])

    branch_a = start_rows([gnat], branch_part)
    for j in range(groups):
        fill(big_keep, j, k, [gnat], branch_part)

    def weight_grad(slot, left, right):
        gpart[slot % 2] = dot_tn(left[...], right[...]).astype(BF16)

    def spread_grad(slot):
        return [
            send(
                gpart.at[slot % 2, :, pl.ds(pl.multiple_of(toward[d] * block, block), block)],
                zrecv.at[slot, d - 1],
                lines[d],
            )
            for d in (1, 2, 3)
        ]

    def owned_grad(slot, copies):
        for copy in copies:
            copy.wait_recv()
        v = gpart[slot % 2, :, zcols].astype(F32)
        for d in range(3):
            v = v + zrecv[slot, d].astype(F32)
        return v

    def share(slot, dst):
        return [local(gres.at[slot], dst)] + [send(gres.at[slot], dst, peers[p]) for p in (3, 1, 2)]

    weight_grad(2, gnat, mg)
    z_wo = spread_grad(2)
    weight_grad(1, znat, xf)

    for t in tiles:
        if t:
            branch_b = middle_rows(branch_a)

        def back_ends(i, carry, t=t):
            tau = steps - 1 - i
            _, killed = dts(t, tau)
            gy = yg[t, tau_rows(tau), :]
            return tuple(
                (carry[n] + gy * bc[states + n, tau_rows(tau), :]) * jnp.exp2(killed * a2b[t, n])
                for n in range(states)
            )

        got = lax.fori_loop(0, steps, back_ends, (zero,) * states, unroll=8)
        for n in range(states):
            gin[t, n] = suffix_of(got[n], jnp.exp2(cum[t] * a2b[t, n]))

    flush(branch_a.values())
    branch_b, branch_sent = pass_rows(branch_b)

    gsum, dsum = gate, y
    part = states // 2
    for lo in (0, part):
        names = list(range(lo, lo + part))
        if lo:
            z_wz = spread_grad(1)

        def back(i, carry, names=names, lo=lo):
            grads, acc = carry
            tau = steps - 1 - i
            r = tau_rows(tau)
            pair = [dts(t, tau) for t in tiles]
            drive = [pair[t][0] * act[t, r, :] for t in tiles]
            gy = [yg[t, r, :] for t in tiles]
            along = [None, None]
            down = [None, None]
            new_g, new_a = [], []
            for q, n in enumerate(names):
                bv, cv = bc[n, r, :], bc[states + n, r, :]
                pb = pc = None
                for t in tiles:
                    a2 = a2b[t, n]
                    decay = jnp.exp2(pair[t][1] * a2)
                    g = grads[2 * q + t] + gy[t] * cv
                    gb = g * bv
                    along[t] = gb if along[t] is None else along[t] + gb
                    v = g * drive[t]
                    pb = v if pb is None else pb + v
                    v = gy[t] * h[t, n, at8(tau * SUB + SUB, SUB), :]
                    pc = v if pc is None else pc + v
                    gd = g * decay
                    dla = gd * h[t, n, r, :]
                    v = dla * a2
                    down[t] = v if down[t] is None else down[t] + v
                    new_a.append(acc[2 * q + t] + dla * pair[t][0])
                    new_g.append(gd)
                bc[n, r, :] = pb
                bc[states + n, r, :] = pc
            for t in tiles:
                if lo == 0:
                    gsum[t, r, :] = along[t]
                    dsum[t, r, :] = down[t]
                else:
                    gsum[t, r, :] = gsum[t, r, :] + along[t]
                    dsum[t, r, :] = dsum[t, r, :] + down[t]
            return tuple(new_g), tuple(new_a)

        start = tuple(gin[t, n] for n in names for t in tiles)
        _, acc = lax.fori_loop(0, steps, back, (start, (zero,) * (2 * part)), unroll=4)
        for q, n in enumerate(names):
            for t in tiles:
                alg[n : n + 1, lanes(t)] = (
                    jnp.sum(acc[2 * q + t], axis=0, keepdims=True) * a2b[t, n][0:1, :] * LN2
                )

    gres[2] = owned_grad(2, z_wo).astype(BF16)
    late["gwo"] = share(2, wo_out.at[chans, :])

    def lin(i, carry):
        new = []
        rank = []
        for t in tiles:
            av, gv = act[t, blk(i), :], gsum[t, blk(i), :]
            v = (dsum[t, blk(i), :] * LN2 + av * gv) * one_less_exp(dt[t, blk(i), :])
            new.append(carry[t] + jnp.sum(v.reshape(rb // SUB, SUB, LANES), axis=0))
            low = v.astype(BF16)
            rank.append(low)
            dsum[t, blk(i), :] = low.astype(F32)
            gsum[t, blk(i), :] = dt[t, blk(i), :] * gv + param(SKIP, t) * yg[t, blk(i), :]
        mp[i] = dot_nt(jnp.concatenate(rank, axis=1), dtwp[...])
        return tuple(new)

    flush(first_sum)
    dtb_sum = lax.fori_loop(0, nblk, lin, (zero, zero))

    beside = lax.broadcasted_iota(jnp.int32, (wide, LANES), 1) - 64
    beside = beside - lax.broadcasted_iota(jnp.int32, (wide, LANES), 0) // LANES

    def collect(i):
        rows = pl.ds(pl.multiple_of(i * 2 * rb, 2 * rb), 2 * rb)
        v = jnp.concatenate([mp[2 * i], mp[2 * i + 1]], axis=0)
        for n in range(0, 2 * states, 2):
            pick = jnp.where(beside == n, 1.0, 0.0).astype(BF16)
            pair = jnp.concatenate([bc[n, rows, :], bc[n + 1, rows, :]], axis=1).astype(BF16)
            v = v + dot(pair, pick)
        mp[2 * i] = v[:rb, :]
        mp[2 * i + 1] = v[rb:, :]

    loop(nblk // 2, collect)

    def finish_early():
        v = end_rows(branch_b)
        mk = jnp.concatenate([maskc[half_rows, :]] * (width // LANES), axis=1)
        for copy in own_half:
            copy.wait()
        so_s[...] = (x_half[...].astype(F32) + mk * v).astype(BF16)
        late["so"] = [local(so_s, so_out.at[half_rows, :]), send(so_s, so_out.at[half_rows, :], sib)]

    def finish_z():
        v = owned_grad(1, z_wz).T
        gres[1] = v.astype(BF16)
        v = v * w_s[1, zrows, :].astype(F32)
        late["gain"] = v[:, :LANES] + v[:, LANES:]

    def small_a():
        low = jnp.concatenate([full[i] for i in range(nblk)], axis=0)
        linv = jnp.concatenate([tiles_bf(dsum, i) for i in range(nblk)], axis=0)
        g = dot_tn(low, linv)
        for i in range(4):
            spart[i, A_DTW : A_DTW + 16, :] = g[i * 16 : i * 16 + 16, :]
            spart[i, A_ALOG : A_ALOG + 4, :] = alg[i * 4 : i * 4 + 4, :]
            for t in tiles:
                spart[i, A_DTB : A_DTB + 1, lanes(t)] = jnp.sum(dtb_sum[t], axis=0, keepdims=True)
                spart[i, A_SKIP : A_SKIP + 1, lanes(t)] = jnp.sum(skip_sum[t], axis=0, keepdims=True)
        late["za"] = [
            send(spart.at[toward[d], pl.ds(0, A_ROWS)], srecv.at[d - 1], lines[d]) for d in (1, 2, 3)
        ]

    def shares():
        late["gwz"] = share(1, wg_out.at[1, :, chans])
        for copy in late["za"]:
            copy.wait_recv()
        sfull[c] = spart[z, 0:A_ROWS, :] + srecv[0] + srecv[1] + srecv[2]
        late["ga"] = [send(sfull.at[c], sfull.at[c], peers[p]) for p in (3, 1, 2)]

    def norm_z():
        finish_z()
        for dst, q in ((big_send, 1 - k), (big_keep, k)):
            for j in turns:
                fill(dst, j, q, [znat], lambda rows, cols: dot_nt(rows[0], w_s[1, cols, :]))

    flush(branch_b + branch_sent)
    second_sum = plane_sum(full2, [small_a, finish_early, norm_z, shares])

    pg = slope

    flush(z_wo)
    z_wx = []
    for t in tiles:

        def pre_grad(i, t=t):
            v = gsum[t, blk(i), :] + dot(full2[i], xp[:, lanes(t)])
            pg[t, blk(i), :] = v * pg[t, blk(i), :]

        loop(nblk, pre_grad)
        for j in range(3):
            pg[t, total + j * SUB : total + (j + 1) * SUB, :] = from_after(pg[t, j * SUB : (j + 1) * SUB, :], 0.0)

        def inner_grad(i, t=t):
            mine = segp[at8(PAD + i * rb, rb), :]
            v = pg[t, blk(i), :] * param(CONVW + 3, t)
            for j in range(1, 4):
                later = pg[t, at8(i * rb + j * SUB, rb), :]
                same = segp[at8(PAD + i * rb + j * SUB, rb), :] == mine
                v = v + jnp.where(same, later, 0.0) * param(CONVW + 3 - j, t)
            dsum[t, blk(i), :] = v

        loop(nblk, inner_grad)
        permute_out(dsum, gnat, (t,))
        gpart[0, lanes(t), :] = dot_tn(gnat[:, lanes(t)], xf[...]).astype(BF16)
        z_wx.append(
            [
                send(
                    gpart.at[0, pl.ds(t * LANES, LANES), pl.ds(pl.multiple_of(toward[d] * block, block), block)],
                    zrecv.at[0, d - 1, pl.ds(t * LANES, LANES)],
                    lines[d],
                )
                for d in (1, 2, 3)
            ]
        )

    flush(late["so"][1:])
    late["so"][0].wait()
    def norm_part(rows, cols):
        return dot_nt(rows[0], w_s[0, cols, :])

    norm_a = start_rows([gnat], norm_part, True)
    norm_b = middle_rows(norm_a, [gnat], norm_part)

    def conv_grad(i, carry):
        new = []
        mine = segp[at8(PAD + i * rb, rb), :]
        for t in tiles:
            v = pg[t, blk(i), :]
            new.append(carry[5 * t] + jnp.sum(v.reshape(rb // SUB, SUB, LANES), axis=0))
            for j in range(4):
                window = inner[t, at8(PAD + i * rb - j * SUB, rb), :]
                if j:
                    window = jnp.where(segp[at8(PAD + i * rb - j * SUB, rb), :] == mine, window, 0.0)
                new.append(carry[5 * t + 1 + j] + jnp.sum((v * window).reshape(rb // SUB, SUB, LANES), axis=0))
        return tuple(new)

    conv_sum = lax.fori_loop(0, nblk, conv_grad, (zero,) * 10)
    norm_b, _ = pass_rows(norm_b)
    mixv = jnp.concatenate([full2[i] for i in range(nblk)], axis=0)
    actv = jnp.concatenate([tiles_bf(act, i) for i in range(nblk)], axis=0)
    gx = dot_tn(mixv, actv)
    for i in range(4):
        conv_rows = [
            jnp.concatenate([jnp.sum(conv_sum[5 * t + j], axis=0, keepdims=True) for t in tiles], axis=1)
            for j in (4, 3, 2, 1, 0)
        ]
        bpart[i] = jnp.concatenate(
            [gx[i * 24 : i * 24 + 24, :]] + conv_rows + [jnp.zeros((3, wide), F32)], axis=0
        ).astype(BF16)
    z_b = [send(bpart.at[toward[d]], brecv.at[d - 1], lines[d]) for d in (1, 2, 3)]
    gain_sum = late["gain"]
    late["gwx"] = [[], []]

    def owned_half(q):
        for copy in z_wx[q]:
            copy.wait_recv()
        rows = slice(q * LANES, (q + 1) * LANES)
        v = gpart[0, rows, zcols].astype(F32)
        for d in range(3):
            v = v + zrecv[0, d, rows, :].astype(F32)
        v = v.T
        gres[0, :, rows] = v.astype(BF16)
        return v * w_s[0, zrows, rows].astype(F32)

    def share_half(q):
        rows = slice(q * LANES, (q + 1) * LANES)
        dst = wg_out.at[0, :, pl.ds(pl.multiple_of(c * wide + q * LANES, LANES), LANES)]
        late["gwx"][0].append(local(gres.at[0, :, rows], dst))
        late["gwx"][1].extend(send(gres.at[0, :, rows], dst, peers[p]) for p in (3, 1, 2))

    gain_sum = gain_sum + owned_half(0)
    share_half(0)
    for copy in z_b:
        copy.wait_recv()
    v = bpart[z].astype(F32)
    for d in range(3):
        v = v + brecv[d].astype(F32)
    bfull[c] = v.astype(BF16)
    g_b = [send(bfull.at[c], bfull.at[c], peers[p]) for p in (3, 1, 2)]
    ng = end_rows(norm_b)
    xv = x_half[...].astype(F32)
    r = lax.rsqrt(jnp.mean(xv * xv, axis=1, keepdims=True) + EPS)
    sg = ng * gain_row
    sg_s[...] = (
        og_half[...].astype(F32) + r * sg - xv * (r * r * r) * jnp.mean(sg * xv, axis=1, keepdims=True)
    )
    last = [local(sg_s, sg_out.at[half_rows, :]), send(sg_s, sg_out.at[half_rows, :], sib)]

    gain_sum = gain_sum + owned_half(1)
    for b in range(block // LANES):
        col = gain_sum[b * LANES : (b + 1) * LANES, :].T
        ggs[0, :, lanes(b)] = jnp.broadcast_to(jnp.sum(col, axis=0, keepdims=True), (SUB, LANES))
    s_gain = [send(ggs.at[0], ggs.at[p], peers[p]) for p in (1, 2, 3)]
    s_gain += [send(ggs.at[0], ggs.at[3 + p], (z, plane[p], 1 - k)) for p in (1, 2, 3)]
    s_gain.append(send(ggs.at[0], ggs.at[7], sib))
    share_half(1)

    for copy in late["ga"] + g_b:
        copy.wait_recv()
    for i in range(4):
        cols = slice(i * wide, (i + 1) * wide)
        sm_out[0:24, cols] = bfull[i, B_XP : B_XP + 24, :].astype(F32)
        sm_out[24:44, cols] = sfull[i, A_DTW : A_ALOG + 4, :]
    cv_out[0:5, :] = bfull[z, B_CONVW : B_CONVB + 1, :].astype(F32)
    cv_out[5:7, :] = sfull[z, A_DTB : A_SKIP + 1, :]
    for copy in s_gain:
        copy.wait_recv()
    v = ggs[0]
    for i in range(1, 8):
        v = v + ggs[i]
    gg_out[...] = v[0:1, :] / early[z, GAIN : GAIN + 1, :]

    late["so"][1].wait_recv()
    for name in ("gwo", "gwz"):
        late[name][0].wait()
        for copy in late[name][1:]:
            copy.wait_recv()
    for copy in late["gwx"][0]:
        copy.wait()
    for copy in late["gwx"][1]:
        copy.wait_recv()
    last[0].wait()
    last[1].wait_recv()
    flush(list(pending))


def fused(
    stream_in, norm_gain, in_weight, out_weight, xproj_weight, dt_weight, a_log, convolution_weight,
    convolution_bias, step_size_bias, skip_term_scale, seg_ids, pad_mask, out_grad,
):
    _, tok, width = stream_in.shape
    wide = 2 * LANES
    total = 4 * tok
    block = width // 4
    states = 4 * a_log.shape[0]
    vm = pl.BlockSpec(memory_space=pltpu.VMEM)
    hbm = pl.BlockSpec(memory_space=pl.ANY)
    f, b = (lambda *s: pltpu.VMEM(s, F32)), (lambda *s: pltpu.VMEM(s, BF16))
    scan = f(2, total, LANES)
    scratch = dict(
        so_s=b(tok // 2, width), x_half=b(tok // 2, width), og_half=b(tok // 2, width), xf=b(total, width), mg=b(total, width), w_s=b(2, width, wide), wo_s=b(wide, width),
        early=f(4, SUB, wide), pk_f=f(4, ROWS_P, wide), pk_s=b(4, ROWS_P, wide), segs=pltpu.VMEM((4, SUB, tok), jnp.int32),
        segp=f(total + 2 * PAD, LANES), maskc=f(tok, LANES), nat=scan, inner=f(2, total + PAD, LANES),
        slope=f(2, total + PAD, LANES), act=scan, gate=scan, dt=scan, yg=scan, y=scan,
        bc=f(2 * states, total, LANES), h=f(2, states, total + SUB, LANES), a2b=f(2, states, SUB, LANES),
        st=f(2, states, SUB, LANES), gin=f(2, states, SUB, LANES), cum=f(2, SUB, LANES), alg=f(states, wide),
        full=b(8, 128, LANES), full2=b(8, 128, LANES), mp=f(8, 128, LANES), sum_a=b(4, 128, LANES),
        recv_a=f(4, 128, LANES), recv_b=b(3, 128, LANES), xp=b(LANES, wide), dtwp=b(LANES, wide),
        big_send=b(4, tok // 2, width), big_keep=b(4, tok // 2, width),
        big_recv=b(4, tok // 2, width), big_rb=b(3, tok // 2, width), gpart=b(2, wide, width),
        zrecv=b(3, 3, wide, block), gres=b(3, block, wide), gnat=b(total, wide), znat=b(total, wide),
        spart=f(4, ROWS, wide), srecv=f(3, A_ROWS, wide), sfull=f(4, A_ROWS, wide),
        bpart=b(4, B_ROWS, wide), brecv=b(3, B_ROWS, wide), bfull=b(4, B_ROWS, wide), sown=f(SUB, wide),
        ggs=f(8, SUB, block), sg_s=f(tok // 2, width),
        ssem=pltpu.SemaphoreType.DMA((144,)), rsem=pltpu.SemaphoreType.DMA((144,)),
        lsem=pltpu.SemaphoreType.DMA((16,)),
    )
    outs = pl.pallas_call(
        fused_kernel,
        out_shape=[
            jax.ShapeDtypeStruct((tok, width), BF16),
            jax.ShapeDtypeStruct((tok, width), F32),
            jax.ShapeDtypeStruct((2, block, 4 * wide), BF16),
            jax.ShapeDtypeStruct((4 * wide, block), BF16),
            jax.ShapeDtypeStruct((48, 4 * wide), F32),
            jax.ShapeDtypeStruct((8, wide), F32),
            jax.ShapeDtypeStruct((1, block), F32),
        ],
        in_specs=[hbm] * 4 + [vm] * 10,
        out_specs=[hbm] * 4 + [vm] * 3,
        scratch_shapes=list(scratch.values()),
        compiler_params=pltpu.CompilerParams(
            collective_id=0, has_side_effects=True, vmem_limit_bytes=VMEM_LIMIT
        ),
    )(
        stream_in.reshape(tok, width), out_grad.reshape(tok, width), in_weight, out_weight, xproj_weight,
        dt_weight, a_log, convolution_weight.reshape(4, block), convolution_bias, step_size_bias,
        skip_term_scale, norm_gain, seg_ids, pad_mask,
    )
    steps = 2
    part = tok // steps

    def whole(*shape):
        return pl.BlockSpec(shape, lambda i: (0,) * len(shape))

    return pl.pallas_call(
        finish_kernel,
        grid=(steps,),
        out_shape=[
            jax.ShapeDtypeStruct((1, tok, width), BF16),
            jax.ShapeDtypeStruct((1, tok, width), F32),
            jax.ShapeDtypeStruct((block,), F32),
            jax.ShapeDtypeStruct((2, block, 4 * wide), F32),
            jax.ShapeDtypeStruct((4 * wide, block), F32),
            jax.ShapeDtypeStruct((24, 4 * wide), F32),
            jax.ShapeDtypeStruct((16, 4 * wide), F32),
            jax.ShapeDtypeStruct((4, 4 * wide), F32),
            jax.ShapeDtypeStruct((4, 1, wide), F32),
            jax.ShapeDtypeStruct((1, wide), F32),
            jax.ShapeDtypeStruct((1, wide), F32),
            jax.ShapeDtypeStruct((1, wide), F32),
        ],
        in_specs=[
            pl.BlockSpec((part, width), lambda i: (i, 0)),
            pl.BlockSpec((part, width), lambda i: (i, 0)),
            pl.BlockSpec((2, block // steps, 4 * wide), lambda i: (0, i, 0)),
            pl.BlockSpec((4 * wide // steps, block), lambda i: (i, 0)),
            whole(48, 4 * wide),
            whole(8, wide),
            whole(1, block),
        ],
        out_specs=[
            pl.BlockSpec((1, part, width), lambda i: (0, i, 0)),
            pl.BlockSpec((1, part, width), lambda i: (0, i, 0)),
            whole(block),
            pl.BlockSpec((2, block // steps, 4 * wide), lambda i: (0, i, 0)),
            pl.BlockSpec((4 * wide // steps, block), lambda i: (i, 0)),
            whole(24, 4 * wide),
            whole(16, 4 * wide),
            whole(4, 4 * wide),
            whole(4, 1, wide),
            whole(1, wide),
            whole(1, wide),
            whole(1, wide),
        ],
        compiler_params=pltpu.CompilerParams(vmem_limit_bytes=VMEM_LIMIT),
    )(*outs)


def finish_kernel(
    so_ref, sg_ref, wg_ref, wo_ref, sm_ref, cv_ref, gg_ref,
    so_out, sg_out, gg_out, wg_out, wo_out, xp_out, dtw_out, alog_out, cw_out, cb_out, dtb_out, skip_out,
):
    so_out[0] = so_ref[...]
    sg_out[0] = sg_ref[...]
    wg_out[...] = wg_ref[...].astype(F32)
    wo_out[...] = wo_ref[...].astype(F32)

    @pl.when(pl.program_id(0) == 0)
    def _():
        gg_out[...] = gg_ref[0]
        xp_out[...] = sm_ref[0:24, :]
        dtw_out[...] = sm_ref[24:40, :]
        alog_out[...] = sm_ref[40:44, :]
        for j in range(4):
            cw_out[j] = cv_ref[j : j + 1, :]
        cb_out[...] = cv_ref[4:5, :]
        dtb_out[...] = cv_ref[5:6, :]
        skip_out[...] = cv_ref[6:7, :]


def solution(mesh):
    in_specs = (
        P("dp", "ctx", None),
        P("dp"),
        P(None, "dp", "tp"),
        P("tp", "dp"),
        P("dp", "tp"),
        P("dp", "tp"),
        P("dp", "tp"),
        P(None, "tp", "dp"),
        P("tp", "dp"),
        P("tp", "dp"),
        P("tp", "dp"),
        P("dp", "ctx"),
        P("dp", "ctx"),
        P("dp", "ctx", None),
    )
    out_specs = (
        P("dp", "ctx", None),
        P("dp", "ctx", None),
        P("dp"),
        P(None, "dp", "tp"),
        P("tp", "dp"),
        P("dp", "tp"),
        P("dp", "tp"),
        P("dp", "tp"),
        P(None, "tp", "dp"),
        P("tp", "dp"),
        P("tp", "dp"),
        P("tp", "dp"),
    )

    def run(*args):
        stream, weight = args[0].shape, args[2].shape
        plane_fits = (mesh.shape["dp"], mesh.shape["ctx"], mesh.shape["tp"]) == (4, 4, 2)
        sizes_fit = stream == (4, 1024, 1024) and weight == (2, 1024, 2048)
        part = fused if plane_fits and sizes_fit else shards
        return jax.shard_map(
            part, mesh=mesh, in_specs=in_specs, out_specs=out_specs, check_vma=False
        )(*args)

    return run
```

```python
import math

import jax
import jax.numpy as jnp
from jax import lax
from jax.experimental import pallas as pl
from jax.experimental.pallas import tpu as pltpu
from jax.sharding import PartitionSpec as P

EPS = 1e-05
VMEM_LIMIT = 63 * 2**20


def from_behind(x, axis, by):
    count = lax.axis_size(axis)
    pairs = [(i, i + by) for i in range(count) if 0 <= i + by < count]
    return lax.ppermute(x, axis, pairs)


def entering(x, axis, combine, identity, reverse):
    count, position = (lax.axis_size(axis), lax.axis_index(axis))
    everything = jax.tree.map(
        lambda part, kind: lax.all_gather(part.astype(kind), axis), x, (jnp.bfloat16, jnp.bfloat16)
    )
    start = jax.tree.map(
        lambda part, zero: jnp.broadcast_to(jnp.asarray(zero, part.dtype), part.shape), x, identity
    )

    def step(k, before):
        at = count - 1 - k if reverse else k
        reached = at > position if reverse else at < position
        new = combine(
            before, jax.tree.map(lambda part, own: part[at].astype(own.dtype), everything, x)
        )
        return jax.tree.map(lambda a, b: jnp.where(reached, a, b), new, before)

    return lax.fori_loop(0, count, step, start)


def silu_slope(value):
    sigma = jax.nn.sigmoid(value)
    return sigma * (1.0 + value * (1.0 - sigma))


def link(first, second):
    return (first[0] * second[0], first[1] * second[0] + second[1])


def chain_prefix(decay, drive, backward):
    return lax.associative_scan(link, (decay, drive), reverse=backward, axis=1)


def shards(
    stream_in,
    norm_gain,
    in_weight,
    out_weight,
    xproj_weight,
    dt_weight,
    a_log,
    convolution_weight,
    convolution_bias,
    step_size_bias,
    skip_term_scale,
    seg_ids,
    pad_mask,
    out_grad,
):
    gathered = (
        lax.all_gather(norm_gain, "dp", axis=0, tiled=True),
        lax.all_gather(in_weight, "dp", axis=1, tiled=True),
        lax.all_gather(out_weight, "dp", axis=1, tiled=True),
        lax.all_gather(xproj_weight, "dp", axis=0, tiled=True),
        lax.all_gather(dt_weight, "dp", axis=0, tiled=True),
        lax.all_gather(a_log, "dp", axis=0, tiled=True),
        lax.all_gather(convolution_weight, "dp", axis=2, tiled=True),
        lax.all_gather(convolution_bias, "dp", axis=1, tiled=True),
        lax.all_gather(step_size_bias, "dp", axis=1, tiled=True),
        lax.all_gather(skip_term_scale, "dp", axis=1, tiled=True),
    )
    (
        gain_full,
        win_full,
        wout_full,
        xproj_full,
        dtw_full,
        alog_full,
        convw_full,
        convb_full,
        dtb_full,
        skip_full,
    ) = gathered
    seq_count, tok_count, model_width = stream_in.shape
    channels = win_full.shape[2]
    low_dims = dtw_full.shape[0]
    states = alog_full.shape[0]
    kernel = convw_full.shape[0]
    conv_lag = kernel - 1
    row_count = seq_count * tok_count
    block_len = math.gcd(tok_count, 128)
    block_count = tok_count // block_len
    gain_vec = gain_full.astype(jnp.float32)
    conv_taps = convw_full.reshape(kernel, channels).astype(jnp.float32)
    conv_shift = convb_full.reshape(channels).astype(jnp.float32)
    dt_shift = dtb_full.reshape(channels).astype(jnp.float32)
    skip_vec = skip_full.reshape(channels).astype(jnp.float32)
    a_neg = -jnp.exp(alog_full.astype(jnp.float32))

    def to_blocks(array):
        shaped = array.reshape((seq_count, block_count, block_len) + array.shape[2:])
        return jnp.moveaxis(shaped, 1, 0)

    def from_blocks(array):
        return jnp.moveaxis(array, 0, 1).reshape((seq_count, tok_count) + array.shape[3:])

    def decay_of(dt_block, keep_block):
        return jnp.exp(dt_block[:, :, None, :] * a_neg) * keep_block[:, :, None, None]

    def drive_of(dt_block, act_block, b_block):
        return (dt_block * act_block)[:, :, None, :] * b_block[:, :, :, None]

    def reverse_terms(decay, rhs, carry_in):
        shifted = jnp.concatenate([decay[:, 1:], jnp.zeros_like(decay[:, :1])], axis=1)
        rhs = rhs.at[:, -1].add(carry_in)
        _, grads = chain_prefix(shifted, rhs, True)
        return (grads, decay[:, 0] * grads[:, 0])

    stream = stream_in.astype(jnp.float32)
    rstd = lax.rsqrt(jnp.mean(stream * stream, axis=2, keepdims=True) + EPS)
    normed = (stream * rstd * gain_vec).astype(jnp.bfloat16)
    normed_flat = normed.reshape(row_count, model_width)
    projected = jnp.einsum(
        "rd,kdc->krc", normed_flat, win_full, preferred_element_type=jnp.float32
    ).astype(jnp.bfloat16)
    inner = projected[0].reshape(seq_count, tok_count, channels)
    gate_vals = projected[1].astype(jnp.float32).reshape(seq_count, tok_count, channels)
    seg_low = seg_ids.astype(jnp.bfloat16)
    prev_inner, prev_seg = from_behind(
        (inner[:, tok_count - conv_lag :], seg_low[:, tok_count - conv_lag :]), "ctx", 1
    )
    inner_vals = inner.astype(jnp.float32)
    prev_vals = prev_inner.astype(jnp.float32)
    seg_float = seg_ids.astype(jnp.float32)
    prev_segf = prev_seg.astype(jnp.float32)
    windows = []
    same_list = []
    pre = jnp.zeros((seq_count, tok_count, channels), jnp.float32) + conv_shift
    for offset in range(kernel):
        if offset == 0:
            window = inner_vals
            seg_window = seg_float
        else:
            window = jnp.concatenate(
                [prev_vals[:, conv_lag - offset :], inner_vals[:, : tok_count - offset]], axis=1
            )
            seg_window = jnp.concatenate(
                [prev_segf[:, conv_lag - offset :], seg_float[:, : tok_count - offset]], axis=1
            )
        same = (seg_window == seg_float).astype(jnp.float32)
        windows.append(window)
        same_list.append(same)
        pre = pre + conv_taps[conv_lag - offset] * window * same[:, :, None]
    keep = same_list[1]
    act = (pre * jax.nn.sigmoid(pre)).astype(jnp.bfloat16)
    act_flat = act.reshape(row_count, channels)
    act_vals = act.astype(jnp.float32)
    mixed_part = jnp.einsum("rc,wc->rw", act_flat, xproj_full, preferred_element_type=jnp.float32)
    mixed = lax.psum(mixed_part, "tp")
    low_rank = mixed[:, :low_dims].astype(jnp.bfloat16)
    b_in = mixed[:, low_dims : low_dims + states].reshape(seq_count, tok_count, states)
    c_out = mixed[:, low_dims + states :].reshape(seq_count, tok_count, states)
    dt_arg = (
        jnp.dot(low_rank, dtw_full, preferred_element_type=jnp.float32).reshape(
            seq_count, tok_count, channels
        )
        + dt_shift
    )
    dt_values = jax.nn.softplus(dt_arg)

    def forward_block(carry, piece):
        start, through = carry
        dt_block, act_block, b_block, c_block, keep_block = piece
        decay = decay_of(dt_block, keep_block)
        prods, local = chain_prefix(decay, drive_of(dt_block, act_block, b_block), False)
        hidden = local + prods * start[:, None]
        outputs = jnp.sum(c_block[:, :, :, None] * hidden, axis=2)
        return ((hidden[:, -1], through * prods[:, -1]), (outputs, start, through))

    zero_state = jnp.zeros((seq_count, states, channels), jnp.float32)
    one_state = jnp.ones_like(zero_state)
    dt_blocks = to_blocks(dt_values)
    act_blocks = to_blocks(act_vals)
    b_blocks = to_blocks(b_in)
    c_blocks = to_blocks(c_out)
    keep_blocks = to_blocks(keep)
    (last_state, through), (y_blocks, local_starts, befores) = lax.scan(
        forward_block,
        (zero_state, one_state),
        (dt_blocks, act_blocks, b_blocks, c_blocks, keep_blocks),
    )
    _, entry_state = entering((through, last_state), "ctx", link, (one_state, zero_state), False)
    cum_dt = jnp.cumsum(dt_values, axis=1)
    alive = jnp.cumprod(keep, axis=1)
    cum_blocks = to_blocks(cum_dt)

    def correct(piece):
        cum_block, c_block, alive_block = piece
        carried = jnp.exp(cum_block[:, :, None, :] * a_neg) * entry_state[:, None]
        return alive_block[:, :, None] * jnp.sum(c_block[:, :, :, None] * carried, axis=2)

    corrections = from_blocks(lax.map(correct, (cum_blocks, c_blocks, to_blocks(alive))))
    y_total = from_blocks(y_blocks) + corrections + skip_vec * act_vals
    gate_act = gate_vals * jax.nn.sigmoid(gate_vals)
    gated_flat = (y_total * gate_act).astype(jnp.bfloat16).reshape(row_count, channels)
    branch_part = jnp.dot(gated_flat, wout_full, preferred_element_type=jnp.float32)
    branch = (
        lax.psum(branch_part.astype(jnp.bfloat16), "tp")
        .astype(jnp.float32)
        .reshape(seq_count, tok_count, model_width)
    )
    mask_float = pad_mask.astype(jnp.float32)
    stream_out = (stream + mask_float[:, :, None] * branch).astype(jnp.bfloat16)
    masked_flat = (out_grad * pad_mask[:, :, None].astype(jnp.bfloat16)).reshape(
        row_count, model_width
    )
    grad_wout = jnp.einsum("rc,rd->cd", gated_flat, masked_flat, preferred_element_type=jnp.float32)
    grad_gated = jnp.einsum(
        "rd,cd->rc", masked_flat, wout_full, preferred_element_type=jnp.float32
    ).reshape(seq_count, tok_count, channels)
    grad_y = grad_gated * gate_act
    grad_gate = (grad_gated * y_total * silu_slope(gate_vals)).astype(jnp.bfloat16)
    grad_skip = jnp.sum(grad_y * act_vals, axis=(0, 1))
    gy_blocks = to_blocks(grad_y)
    true_starts = local_starts + befores * entry_state[None]

    def back_core(carry_in, piece):
        dt_block, act_block, b_block, c_block, keep_block, gy_block, start = piece
        decay = decay_of(dt_block, keep_block)
        prods, local = chain_prefix(decay, drive_of(dt_block, act_block, b_block), False)
        hidden = local + prods * start[:, None]
        earlier = jnp.concatenate([start[:, None], hidden[:, :-1]], axis=1)
        grads, carry_out = reverse_terms(
            decay, c_block[:, :, :, None] * gy_block[:, :, None, :], carry_in
        )
        stepped = earlier * decay
        weighted = grads * stepped
        along_b = jnp.sum(grads * b_block[:, :, :, None], axis=2)
        grad_dt = jnp.sum(weighted * a_neg, axis=2) + along_b * act_block
        grad_act = along_b * dt_block
        grad_b = jnp.sum(grads * (dt_block * act_block)[:, :, None, :], axis=3)
        grad_c = jnp.sum(gy_block[:, :, None, :] * hidden, axis=3)
        return (carry_out, weighted, stepped, (grad_dt, grad_act, grad_b, grad_c))

    back_pieces = (dt_blocks, act_blocks, b_blocks, c_blocks, keep_blocks, gy_blocks, true_starts)
    zero_acc = jnp.zeros((states, channels), jnp.float32)
    cum_end = cum_dt[:, -1]
    suffix = jnp.flip(jnp.cumprod(jnp.flip(keep, axis=1), axis=1), axis=1)
    rest = jnp.concatenate([suffix[:, 1:], jnp.ones((seq_count, 1), jnp.float32)], axis=1)
    rest_blocks = to_blocks(rest)

    def reach_of(cum_block, rest_block):
        return (
            jnp.exp((cum_end[:, None, None, :] - cum_block[:, :, None, :]) * a_neg)
            * rest_block[:, :, None, None]
        )

    def kept_back(carry, piece):
        carry_in, a_acc, q_acc = carry
        core_piece = piece[:7]
        carry_out, weighted, stepped, terms = back_core(carry_in, core_piece)
        dt_block = core_piece[0]
        along = stepped * reach_of(piece[7], piece[8])
        a_acc = a_acc + jnp.sum(weighted * dt_block[:, :, None, :], axis=(0, 1))
        q_acc = q_acc + jnp.sum(along * dt_block[:, :, None, :], axis=1)
        return ((carry_out, a_acc, q_acc), terms + (along,))

    (edge_grad, a_local, q_total), (base_dt, base_act, base_b, grad_c_blocks, along_blocks) = (
        lax.scan(
            kept_back,
            (zero_state, zero_acc, zero_state),
            back_pieces + (cum_blocks, rest_blocks),
            reverse=True,
        )
    )
    _, after_grad = entering((through, edge_grad), "ctx", link, (one_state, zero_state), True)

    def adjust(piece):
        dt_block, act_block, b_block, cum_block, rest_block, along = piece
        extra = reach_of(cum_block, rest_block) * after_grad[:, None]
        along_b = jnp.sum(extra * b_block[:, :, :, None], axis=2)
        grad_dt = jnp.sum(along * after_grad[:, None] * a_neg, axis=2) + along_b * act_block
        grad_act = along_b * dt_block
        grad_b = jnp.sum(extra * (dt_block * act_block)[:, :, None, :], axis=3)
        return (grad_dt, grad_act, grad_b)

    add_dt, add_act, add_b = lax.map(
        adjust, (dt_blocks, act_blocks, b_blocks, cum_blocks, rest_blocks, along_blocks)
    )
    grad_dt_blocks = base_dt + add_dt
    grad_act_blocks = base_act + add_act
    grad_b_blocks = base_b + add_b
    a_total = a_local + jnp.sum(q_total * after_grad, axis=0)
    grad_lin = from_blocks(grad_dt_blocks) * jax.nn.sigmoid(dt_arg)
    grad_dtb = jnp.sum(grad_lin, axis=(0, 1))
    grad_lin_low = grad_lin.reshape(row_count, channels).astype(jnp.bfloat16)
    grad_dtw = jnp.einsum("rk,rc->kc", low_rank, grad_lin_low, preferred_element_type=jnp.float32)
    grad_rank = jnp.einsum("rc,kc->rk", grad_lin_low, dtw_full, preferred_element_type=jnp.float32)
    grad_mixed_part = jnp.concatenate(
        [
            grad_rank,
            from_blocks(grad_b_blocks).reshape(row_count, states),
            from_blocks(grad_c_blocks).reshape(row_count, states),
        ],
        axis=1,
    )
    grad_mixed = lax.psum(grad_mixed_part, "tp").astype(jnp.bfloat16)
    grad_xproj = jnp.einsum("rw,rc->wc", grad_mixed, act_flat, preferred_element_type=jnp.float32)
    grad_act_total = (
        grad_y * skip_vec
        + from_blocks(grad_act_blocks)
        + jnp.dot(grad_mixed, xproj_full, preferred_element_type=jnp.float32).reshape(
            seq_count, tok_count, channels
        )
    )
    grad_pre = grad_act_total * silu_slope(pre)
    grad_convb = jnp.sum(grad_pre, axis=(0, 1))
    tap_grads = [None] * kernel
    grad_inner = jnp.zeros((seq_count, tok_count, channels), jnp.float32)
    tail_grad = jnp.zeros((seq_count, conv_lag, channels), jnp.float32)
    for offset in range(kernel):
        weighted_pre = grad_pre * same_list[offset][:, :, None]
        tap_grads[conv_lag - offset] = jnp.sum(weighted_pre * windows[offset], axis=(0, 1))
        scaled_pre = weighted_pre * conv_taps[conv_lag - offset]
        if offset == 0:
            grad_inner = grad_inner + scaled_pre
        else:
            grad_inner = grad_inner + jnp.concatenate(
                [scaled_pre[:, offset:], jnp.zeros((seq_count, offset, channels), jnp.float32)],
                axis=1,
            )
            tail_grad = tail_grad.at[:, conv_lag - offset :].add(scaled_pre[:, :offset])
    grad_convw = jnp.stack(tap_grads)
    sent_back = from_behind(tail_grad, "ctx", -1)
    grad_inner = grad_inner.at[:, tok_count - conv_lag :].add(sent_back)
    grad_proj = jnp.stack(
        [
            grad_inner.astype(jnp.bfloat16).reshape(row_count, channels),
            grad_gate.reshape(row_count, channels),
        ]
    )
    grad_win = jnp.einsum("rd,krc->kdc", normed_flat, grad_proj, preferred_element_type=jnp.float32)
    grad_norm_part = jnp.einsum(
        "krc,kdc->rd", grad_proj, win_full, preferred_element_type=jnp.float32
    )
    grad_norm = lax.psum(grad_norm_part, "tp").reshape(seq_count, tok_count, model_width)
    grad_gain = jnp.sum(grad_norm * stream * rstd, axis=(0, 1))
    scaled = grad_norm * gain_vec
    stream_grad = (
        out_grad.astype(jnp.float32)
        + rstd * scaled
        - stream * (rstd * rstd * rstd) * jnp.mean(scaled * stream, axis=2, keepdims=True)
    )
    grad_alog = a_total * a_neg
    local_grads = (
        grad_gain,
        grad_win,
        grad_wout,
        grad_xproj,
        grad_dtw,
        grad_alog,
        grad_convw.reshape(kernel, 1, channels),
        grad_convb.reshape(1, channels),
        grad_dtb.reshape(1, channels),
        grad_skip.reshape(1, channels),
    )
    summed = lax.psum(
        (
            local_grads[0],
            local_grads[1],
            local_grads[2],
            local_grads[3],
            local_grads[4],
            local_grads[5],
            local_grads[6],
            local_grads[7],
            local_grads[8],
            local_grads[9],
        ),
        "ctx",
    )
    owned = (
        lax.psum_scatter(summed[0], "dp", scatter_dimension=0, tiled=True),
        lax.psum_scatter(summed[1], "dp", scatter_dimension=1, tiled=True),
        lax.psum_scatter(summed[2], "dp", scatter_dimension=1, tiled=True),
        lax.psum_scatter(summed[3], "dp", scatter_dimension=0, tiled=True),
        lax.psum_scatter(summed[4], "dp", scatter_dimension=0, tiled=True),
        lax.psum_scatter(summed[5], "dp", scatter_dimension=0, tiled=True),
        lax.psum_scatter(summed[6], "dp", scatter_dimension=2, tiled=True),
        lax.psum_scatter(summed[7], "dp", scatter_dimension=1, tiled=True),
        lax.psum_scatter(summed[8], "dp", scatter_dimension=1, tiled=True),
        lax.psum_scatter(summed[9], "dp", scatter_dimension=1, tiled=True),
    )
    return (
        stream_out,
        stream_grad,
        owned[0],
        owned[1],
        owned[2],
        owned[3],
        owned[4],
        owned[5],
        owned[6],
        owned[7],
        owned[8],
        owned[9],
    )


F32 = jnp.float32
BF16 = jnp.bfloat16
MESH = pl.DeviceIdType.MESH
LOG2E = math.log2(math.e)
LN2 = math.log(2.0)
KILL = 1e30
SUB = 8
LANES = 128
PAD = 24
ROWS = 64
XP, DTW, ALOG, ROWS_P = 0, 24, 40, 48
CONVW, CONVB, DTB, SKIP, GAIN = 0, 4, 5, 6, 7
A_DTW, A_ALOG, A_DTB, A_SKIP, A_ROWS = 0, 16, 20, 21, 24
B_XP, B_CONVW, B_CONVB, B_ROWS = 0, 24, 28, 32
NT = (((1,), (1,)), ((), ()))
TN = (((0,), (0,)), ((), ()))


def dot(a, b):
    return jnp.dot(a, b, preferred_element_type=F32)


def dot_nt(a, b):
    return lax.dot_general(a, b, NT, preferred_element_type=F32)


def dot_tn(a, b):
    return lax.dot_general(a, b, TN, preferred_element_type=F32)


def at8(start, size):
    return pl.ds(pl.multiple_of(start, 8), size)


def sigmoid(v):
    return 0.5 + 0.5 * jnp.tanh(0.5 * v)


def log_one_plus(v):
    series = v * (1.0 - v * (0.5 - v * (1.0 / 3.0 - v * 0.25)))
    return jnp.where(v < 0.01, series, jnp.log(1.0 + v))


def one_less_exp(v):
    series = v * (1.0 - v * (0.5 - v * (1.0 / 6.0 - v * (1.0 / 24.0 - v * (1.0 / 120.0)))))
    return jnp.where(v < 0.1, series, 1.0 - jnp.exp(-v))


def prefix_of(ends, prods):
    row = lax.broadcasted_iota(jnp.int32, ends.shape, 0)
    for gap in (1, 2, 4):
        ok = row >= gap
        ends = ends + prods * jnp.where(ok, pltpu.roll(ends, gap, 0), 0.0)
        prods = prods * jnp.where(ok, pltpu.roll(prods, gap, 0), 1.0)
    return jnp.where(row >= 1, pltpu.roll(ends, 1, 0), 0.0)


def suffix_of(ends, prods):
    row = lax.broadcasted_iota(jnp.int32, ends.shape, 0)
    for gap in (1, 2, 4):
        ok = row < SUB - gap
        ends = ends + prods * jnp.where(ok, pltpu.roll(ends, SUB - gap, 0), 0.0)
        prods = prods * jnp.where(ok, pltpu.roll(prods, SUB - gap, 0), 1.0)
    return jnp.where(row < SUB - 1, pltpu.roll(ends, SUB - 1, 0), 0.0)


def fused_kernel(
    x_ref, og_ref, win_ref, wout_ref, xproj_ref, dtw_ref, alog_ref, convw_ref, convb_ref, dtb_ref,
    skip_ref, gain_ref, seg_ref, mask_ref,
    so_out, sg_out, wg_out, wo_out, sm_out, cv_out, gg_out,
    so_s, x_half, og_half, xf, mg, w_s, wo_s, early, pk_f, pk_s, segs, segp, maskc, nat, inner, slope, act, gate, dt, yg, y,
    bc, h, a2b, st, gin, cum, alg, full, full2, mp, sum_a, recv_a, recv_b, xp, dtwp,
    big_send, big_keep, big_recv, big_rb, gpart, zrecv, gres, gnat, znat, spart, srecv, sfull, bpart, brecv, bfull, sown, ggs,
    sg_s, ssem, rsem, lsem,
):
    z, c, k = lax.axis_index("dp"), lax.axis_index("ctx"), lax.axis_index("tp")
    nz = lax.axis_size("dp")
    px, py = lax.rem(c, 2), c // 2
    sib = (z, c, 1 - k)
    plane = [None, py * 2 + (1 - px), (1 - py) * 2 + px, (1 - py) * 2 + (1 - px)]
    peers = [None] + [(z, plane[p], k) for p in (1, 2, 3)]
    toward = [None] + [lax.rem(z + d, nz) for d in (1, 2, 3)]
    behind = [None] + [lax.rem(z + nz - d, nz) for d in (1, 2, 3)]
    lines = [None] + [(toward[d], c, k) for d in (1, 2, 3)]
    count = [0]
    local_count = [0]
    pending = []

    def send(src, dst, device):
        i = count[0]
        count[0] += 1
        copy = pltpu.make_async_remote_copy(
            src_ref=src, dst_ref=dst, send_sem=ssem.at[i], recv_sem=rsem.at[i],
            device_id=device, device_id_type=MESH,
        )
        copy.start()
        pending.append(copy)
        return copy

    def local(src, dst):
        i = local_count[0]
        local_count[0] += 1
        copy = pltpu.make_async_copy(src, dst, lsem.at[i])
        copy.start()
        return copy

    def flush(copies):
        for copy in copies:
            copy.wait_send()
            pending[:] = [other for other in pending if other is not copy]

    tok = maskc.shape[0]
    half = tok // 2
    total = xf.shape[0]
    width = xf.shape[1]
    steps = total // SUB
    states = h.shape[1]
    wide = 2 * LANES
    block = w_s.shape[1] // 4
    tiles = (0, 1)
    rb = 128
    nblk = total // rb

    def lanes(t):
        return slice(t * LANES, (t + 1) * LANES)

    def blk(i):
        return pl.ds(pl.multiple_of(i * rb, rb), rb)

    wb = 512

    def wide_blk(i):
        return pl.ds(pl.multiple_of(i * wb, wb), wb)

    def tau_rows(tau):
        return at8(tau * SUB, SUB)

    def loop(n, body, unroll=1):
        def step(i, carry):
            body(i)
            return carry

        lax.fori_loop(0, n, step, 0, unroll=unroll)

    barrier = pltpu.get_barrier_semaphore()
    everyone = [sib] + peers[1:] + [(z, plane[p], 1 - k) for p in (1, 2, 3)] + lines[1:]
    for device in everyone:
        pl.semaphore_signal(barrier, inc=1, device_id=device, device_id_type=MESH)
    chans = pl.ds(pl.multiple_of(c * wide, wide), wide)
    spart[...] = jnp.zeros_like(spart)
    spart[0, XP : XP + 24, :] = xproj_ref[:, chans].astype(F32)
    spart[0, DTW : DTW + 16, :] = dtw_ref[:, chans].astype(F32)
    spart[0, ALOG : ALOG + 4, :] = alog_ref[:, chans].astype(F32)
    early[z, CONVW : CONVW + 4, :] = convw_ref[...].astype(F32)
    early[z, CONVB : CONVB + 1, :] = convb_ref[...].astype(F32)
    early[z, DTB : DTB + 1, :] = dtb_ref[...].astype(F32)
    early[z, SKIP : SKIP + 1, :] = skip_ref[...].astype(F32)
    early[z, GAIN : GAIN + 1, :] = gain_ref[...].astype(F32).reshape(1, block)
    pk_s[z] = spart[0, 0:ROWS_P, :].astype(BF16)
    segs[c] = jnp.broadcast_to(seg_ref[...], (SUB, tok))
    pl.semaphore_wait(barrier, len(everyone))

    my_half = pl.ds(pl.multiple_of(c * tok + k * half, half), half)
    s_seg = [send(segs.at[c], segs.at[c], peers[p]) for p in (1, 2, 3)]
    s_x = [send(x_ref.at[pl.ds(pl.multiple_of(k * half, half), half)], xf.at[my_half], peers[p]) for p in (3, 1, 2)]
    s_early = [send(early.at[z], early.at[z], lines[d]) for d in (1, 2, 3)]

    zrows = pl.ds(pl.multiple_of(z * block, block), block)

    def weight(which):
        return [
            send(win_ref.at[which, :, chans], w_s.at[which, zrows, :], lines[d]) for d in (1, 2, 3)
        ]

    s_wx = weight(0)
    s_pack = [send(pk_s.at[z], pk_s.at[z], lines[d]) for d in (1, 2, 3)]
    own_w = [local(win_ref.at[i, :, chans], w_s.at[i, zrows, :]) for i in (0, 1)]
    zcols = pl.ds(pl.multiple_of(z * block, block), block)
    own_wo = local(wout_ref.at[chans, :], wo_s.at[:, zcols])

    own_rows = pl.ds(pl.multiple_of(c * tok, tok), tok)
    half_rows = pl.ds(pl.multiple_of(k * half, half), half)
    own_x = local(x_ref, xf.at[own_rows, :])
    own_og = local(og_ref, mg.at[own_rows, :])
    own_half = [local(x_ref.at[half_rows, :], x_half), local(og_ref.at[half_rows, :], og_half)]
    mrow = mask_ref[...].astype(F32)
    for b in range(tok // LANES):
        rows = slice(b * LANES, (b + 1) * LANES)
        maskc[rows, :] = jnp.broadcast_to(mrow[:, rows], (LANES, LANES)).T
    mcol = jnp.concatenate([maskc[...]] * (width // LANES), axis=1)
    own_og.wait()
    mg[own_rows, :] = (mg[own_rows, :].astype(F32) * mcol).astype(BF16)

    for copy in s_early:
        copy.wait_recv()
    gain_row = jnp.concatenate([early[i, GAIN : GAIN + 1, :] for i in range(4)], axis=1)
    sown[...] = early[c]

    def param(row, t):
        return sown[row : row + 1, lanes(t)]

    for copy in s_seg:
        copy.wait_recv()
    for i in range(4):
        srow = segs[i, 0:1, :].astype(F32)
        for b in range(tok // LANES):
            rows = slice(b * LANES, (b + 1) * LANES)
            nat[0, i * tok + b * LANES : i * tok + (b + 1) * LANES, :] = jnp.broadcast_to(
                srow[:, rows], (LANES, LANES)
            ).T

    def seg_in(tau):
        segp[at8(PAD + tau * SUB, SUB), :] = nat[0, pl.ds(tau, SUB, stride=steps), :]

    loop(steps, seg_in, 8)
    sub_row = lax.broadcasted_iota(jnp.int32, (SUB, LANES), 0)

    def from_before(v, fill):
        return jnp.where(sub_row >= 1, pltpu.roll(v, 1, 0), fill)

    def from_after(v, fill):
        return jnp.where(sub_row < SUB - 1, pltpu.roll(v, SUB - 1, 0), fill)

    for j in range(3):
        segp[j * SUB : (j + 1) * SUB, :] = from_before(segp[total + j * SUB : total + (j + 1) * SUB, :], -1.0)
        segp[PAD + total + j * SUB : PAD + total + (j + 1) * SUB, :] = from_after(
            segp[PAD + j * SUB : PAD + (j + 1) * SUB, :], -2.0
        )

    def halves(copies, buf):
        relays = []
        for copy, p in zip(copies, (3, 1, 2)):
            copy.wait_recv()
            rows = pl.ds(pl.multiple_of(plane[p] * tok + k * half, half), half)
            relays.append(send(buf.at[rows], buf.at[rows], sib))
        return relays

    def norm(i):
        rows = pl.ds(pl.multiple_of(i * rb, rb), rb)
        v = xf[rows, :].astype(F32)
        r = lax.rsqrt(jnp.mean(v * v, axis=1, keepdims=True) + EPS)
        xf[rows, :] = (v * r * gain_row).astype(BF16)

    def project_block(i):
        rows = pl.ds(pl.multiple_of(i * tok, tok), tok)
        v = dot(xf[rows, :], w_s[0])
        for t in tiles:
            nat[t, rows, :] = v[:, lanes(t)]

    per = tok // rb
    own_x.wait()
    loop(per, lambda i: norm(c * per + i))
    r_x = halves(s_x, xf)
    for copy in s_wx:
        copy.wait_recv()
    own_w[0].wait()
    s_wz = weight(1)
    project_block(c)
    for copy, sent, p in zip(r_x, s_x, (3, 1, 2)):
        copy.wait_recv()
        flush([copy])
        loop(per, lambda i, p=p: norm(plane[p] * per + i))
        project_block(plane[p])

    def project(which, dst, off):
        def body(i):
            v = dot(xf[wide_blk(i), :], w_s[which])
            for t in tiles:
                nat[t, wide_blk(i), :] = v[:, lanes(t)]

        loop(total // wb, body)
        permute_in(dst, off, True)

    def permute_in(dst, off, rounded=False):
        def body(tau):
            for t in tiles:
                v = nat[t, pl.ds(tau, SUB, stride=steps), :]
                dst[t, at8(off + tau * SUB, SUB), :] = v.astype(BF16).astype(F32) if rounded else v

        loop(steps, body, 8)

    def permute_out(src, dst, which=tiles):
        def body(i):
            for s in range(SUB):
                for t in which:
                    nat[t, at8(s * steps + i * SUB, SUB), :] = src[t, pl.ds(i * SUB * SUB + s, SUB, stride=SUB), :]

        loop(steps // SUB, body)

        def cast(i):
            for t in which:
                dst[blk(i), lanes(t)] = nat[t, blk(i), :].astype(BF16)

        loop(nblk, cast)

    permute_in(inner, PAD, True)
    for t in tiles:
        for j in range(3):
            inner[t, j * SUB : (j + 1) * SUB, :] = from_before(inner[t, total + j * SUB : total + (j + 1) * SUB, :], 0.0)

    def conv(i):
        for t in tiles:
            mine = segp[at8(PAD + i * rb, rb), :]
            pre = jnp.zeros((rb, LANES), F32) + param(CONVB, t)
            for j in range(4):
                window = inner[t, at8(PAD + i * rb - j * SUB, rb), :]
                if j:
                    window = jnp.where(segp[at8(PAD + i * rb - j * SUB, rb), :] == mine, window, 0.0)
                pre = pre + param(CONVW + 3 - j, t) * window
            s = sigmoid(pre)
            act[t, blk(i), :] = (pre * s).astype(BF16).astype(F32)
            slope[t, blk(i), :] = s * (1.0 + pre * (1.0 - s))

    loop(nblk, conv)

    def tiles_bf(ref, i):
        return jnp.concatenate([ref[t, blk(i), :] for t in tiles], axis=1).astype(BF16)

    for copy in s_pack:
        copy.wait_recv()
    for i in range(4):
        pk_f[i] = pk_s[i].astype(F32)
    for i in range(4):
        alg[4 * i : 4 * i + 4, :] = pk_f[i, ALOG : ALOG + 4, :]
    xp_rows = jnp.concatenate([pk_f[i, XP : XP + 24, :] for i in range(4)] + [jnp.zeros((32, wide), F32)], axis=0)
    xp[...] = xp_rows.astype(BF16)
    dt_rows = jnp.concatenate([pk_f[i, DTW : DTW + 16, :] for i in range(4)] + [jnp.zeros((64, wide), F32)], axis=0)
    dtwp[...] = dt_rows.astype(BF16)
    a2v = -jnp.exp(alg[...]) * LOG2E
    for n in range(states):
        for t in tiles:
            a2b[t, n] = jnp.broadcast_to(a2v[n : n + 1, lanes(t)], (SUB, LANES))

    def mix(i):
        mp[i] = dot_nt(tiles_bf(act, i), xp[...])

    loop(nblk, mix)

    def plane_sum(out, between):
        first = send(mp.at[pl.ds((1 - k) * 4, 4)], recv_a, sib)
        between[0]()
        first.wait_recv()
        for i in range(4):
            sum_a[i] = (mp[k * 4 + i] + recv_a[i]).astype(BF16)
        second = [send(sum_a.at[plane[p]], recv_b.at[p - 1], peers[p]) for p in (3, 1, 2)]
        between[1]()
        for copy in second:
            copy.wait_recv()
        mine = k * 4 + c
        v = mp[mine] + recv_a[c]
        for p in range(3):
            v = v + recv_b[p].astype(F32)
        out[mine] = v.astype(BF16)
        third = [send(out.at[mine], out.at[mine], peers[p]) for p in (3, 1, 2)]
        third.append(send(out.at[mine], out.at[mine], sib))
        between[2]()
        fourth = []
        for copy, p in zip(third, (3, 1, 2)):
            copy.wait_recv()
            there = k * 4 + plane[p]
            fourth.append(send(out.at[there], out.at[there], sib))
        between[3]()
        for copy in [third[3]] + fourth:
            copy.wait_recv()
        return [first] + second

    late = {}

    def send_wo():
        for copy in s_wz:
            copy.wait_recv()
        own_w[1].wait()
        late["wo"] = [send(wout_ref.at[chans, :], wo_s.at[:, zcols], lines[d]) for d in (1, 2, 3)]

    def gates():
        project(1, gate, 0)

    def nothing():
        pass

    def send_mg():
        late["mg"] = [send(mg.at[my_half], mg.at[my_half], peers[p]) for p in (3, 1, 2)]

    def gap():
        send_mg()
        send_wo()
        gates()

    first_sum = plane_sum(full, [nothing, nothing, nothing, gap])

    def steps_of(i):
        arg = dot(full[i], dtwp[...])
        for t in tiles:
            v = arg[:, lanes(t)] + param(DTB, t)
            dt[t, blk(i), :] = jnp.maximum(v, 0.0) + log_one_plus(jnp.exp(-jnp.abs(v)))

    loop(nblk, steps_of)

    flat = full[...].reshape(total, LANES)
    row = lax.broadcasted_iota(jnp.int32, (LANES, wide), 0)
    col = lax.broadcasted_iota(jnp.int32, (LANES, wide), 1) // LANES
    for n in range(0, 2 * states, 2):
        v = dot(flat, jnp.where(row == 64 + n + col, 1.0, 0.0).astype(BF16))
        for t in tiles:
            bc[n + t] = v[:, lanes(t)]

    def dts(t, tau):
        v = dt[t, tau_rows(tau), :]
        r = at8(PAD + tau * SUB, SUB)
        p = at8(PAD + tau * SUB - SUB, SUB)
        return v, jnp.where(segp[r, :] == segp[p, :], v, KILL)

    for t in tiles:

        def ends(tau, carry, t=t):
            v, killed = dts(t, tau)
            drive = v * act[t, tau_rows(tau), :]
            new = [
                carry[n] * jnp.exp2(killed * a2b[t, n]) + drive * bc[n, tau_rows(tau), :] for n in range(states)
            ]
            return tuple(new) + (carry[states] + killed,)

        zero = jnp.zeros((SUB, LANES), F32)
        got = lax.fori_loop(0, steps, ends, (zero,) * (states + 1), unroll=8)
        cum[t] = got[states]
        for n in range(states):
            st[t, n] = prefix_of(got[n], jnp.exp2(got[states] * a2b[t, n]))

    for t in tiles:
        if t:
            late["mg"] = halves(late["mg"], mg)
        for n in range(states):
            h[t, n, 0:SUB, :] = st[t, n]

        def forward(tau, carry, t=t):
            v, killed = dts(t, tau)
            drive = v * act[t, tau_rows(tau), :]
            new, parts = [], [None] * 4
            for n in range(states):
                s = carry[n] * jnp.exp2(killed * a2b[t, n]) + drive * bc[n, tau_rows(tau), :]
                h[t, n, at8(tau * SUB + SUB, SUB), :] = s
                o = s * bc[states + n, tau_rows(tau), :]
                parts[n % 4] = o if parts[n % 4] is None else parts[n % 4] + o
                new.append(s)
            y[t, tau_rows(tau), :] = (parts[0] + parts[1]) + (parts[2] + parts[3])
            return tuple(new)

        lax.fori_loop(0, steps, forward, tuple(st[t, n] for n in range(states)), unroll=8)

    for copy in late["mg"] + late["wo"]:
        copy.wait_recv()
    own_wo.wait()

    def ograd(i):
        v = dot_nt(mg[wide_blk(i), :], wo_s[...])
        for t in tiles:
            nat[t, wide_blk(i), :] = v[:, lanes(t)]

    loop(total // wb, ograd)
    gb = SUB * SUB

    def strided(t, i):
        return jnp.concatenate([nat[t, pl.ds(i * SUB + u, SUB, stride=steps), :] for u in range(SUB)], axis=0)

    def gating(i, carry):
        new = []
        rows = pl.ds(pl.multiple_of(i * gb, gb), gb)
        for t in tiles:
            gv, ov, av = gate[t, rows, :], strided(t, i), act[t, rows, :]
            s = sigmoid(gv)
            ytot = y[t, rows, :] + param(SKIP, t) * av
            gy = ov * (gv * s)
            yg[t, rows, :] = gy
            y[t, rows, :] = ytot * (gv * s)
            gate[t, rows, :] = ov * ytot * (s * (1.0 + gv * (1.0 - s)))
            new.append(carry[t] + jnp.sum((gy * av).reshape(SUB, SUB, LANES), axis=0))
        return tuple(new)

    zero = jnp.zeros((SUB, LANES), F32)
    skip_sum = lax.fori_loop(0, total // gb, gating, (zero, zero))
    permute_out(y, gnat)
    permute_out(gate, znat)

    def owner_rows(i, q):
        return pl.ds(pl.multiple_of(i * tok + q * half, half), half)

    order = (3, 1, 2, 0)
    groups = width // wide
    turns = (0, 2, 1, 3)

    def fill(dst, j, q, lefts, right, more=False):
        cols = slice(j * wide, (j + 1) * wide)
        there = [plane[p] if p else c for p in order]
        rows = [jnp.concatenate([left[owner_rows(i, q), :] for i in there], axis=0) for left in lefts]
        v = right(rows, cols)
        for i, p in enumerate(order):
            piece = v[i * half : (i + 1) * half, :]
            if more:
                piece = piece + dst[p, :, cols].astype(F32)
            dst[p, :, cols] = piece.astype(BF16)

    def start_rows(lefts, right, more=False):
        first = {}
        for j in turns:
            cols = slice(j * wide, (j + 1) * wide)
            fill(big_send, j, 1 - k, lefts, right, more)
            first[j] = send(big_send.at[:, :, cols], big_recv.at[:, :, cols], sib)
        return first

    def ways(j):
        return (1, 2) if j < groups // 2 else (2, 1)

    def middle_rows(first, lefts=None, right=None):
        second = {}
        for j in turns:
            cols = slice(j * wide, (j + 1) * wide)
            if lefts:
                fill(big_keep, j, k, lefts, right, True)
            first[j].wait_recv()
            for p in order:
                big_keep[p, :, cols] = (big_keep[p, :, cols].astype(F32) + big_recv[p, :, cols].astype(F32)).astype(BF16)
            near, far = ways(j)
            second[j] = [
                send(big_keep.at[3, :, cols], big_rb.at[1, :, cols], peers[near]),
                send(big_keep.at[near, :, cols], big_rb.at[0, :, cols], peers[near]),
            ]
        return second

    def pass_rows(second):
        third = []
        for j in turns:
            cols = slice(j * wide, (j + 1) * wide)
            near, far = ways(j)
            second[j][0].wait_recv()
            big_keep[far, :, cols] = (big_keep[far, :, cols].astype(F32) + big_rb[1, :, cols].astype(F32)).astype(BF16)
            third.append(send(big_keep.at[far, :, cols], big_rb.at[2, :, cols], peers[far]))
        return [second[j][1] for j in turns] + third, [second[j][0] for j in turns]

    def end_rows(second):
        for copy in second:
            copy.wait_recv()
        return big_keep[0].astype(F32) + big_rb[0].astype(F32) + big_rb[2].astype(F32)

    def branch_part(rows, cols):
        return dot(rows[0], wo_s[:, cols])

    branch_a = start_rows([gnat], branch_part)
    for j in range(groups):
        fill(big_keep, j, k, [gnat], branch_part)

    def weight_grad(slot, left, right):
        gpart[slot % 2] = dot_tn(left[...], right[...]).astype(BF16)

    def spread_grad(slot):
        return [
            send(
                gpart.at[slot % 2, :, pl.ds(pl.multiple_of(toward[d] * block, block), block)],
                zrecv.at[slot, d - 1],
                lines[d],
            )
            for d in (1, 2, 3)
        ]

    def owned_grad(slot, copies):
        for copy in copies:
            copy.wait_recv()
        v = gpart[slot % 2, :, zcols].astype(F32)
        for d in range(3):
            v = v + zrecv[slot, d].astype(F32)
        return v

    def share(slot, dst):
        return [local(gres.at[slot], dst)] + [send(gres.at[slot], dst, peers[p]) for p in (3, 1, 2)]

    weight_grad(2, gnat, mg)
    z_wo = spread_grad(2)
    weight_grad(1, znat, xf)

    for t in tiles:
        if t:
            branch_b = middle_rows(branch_a)

        def back_ends(i, carry, t=t):
            tau = steps - 1 - i
            _, killed = dts(t, tau)
            gy = yg[t, tau_rows(tau), :]
            return tuple(
                (carry[n] + gy * bc[states + n, tau_rows(tau), :]) * jnp.exp2(killed * a2b[t, n])
                for n in range(states)
            )

        got = lax.fori_loop(0, steps, back_ends, (zero,) * states, unroll=8)
        for n in range(states):
            gin[t, n] = suffix_of(got[n], jnp.exp2(cum[t] * a2b[t, n]))

    flush(branch_a.values())
    branch_b, branch_sent = pass_rows(branch_b)

    gsum, dsum = gate, y
    part = states // 2
    for lo in (0, part):
        names = list(range(lo, lo + part))
        if lo:
            z_wz = spread_grad(1)

        def back(i, carry, names=names, lo=lo):
            grads, acc = carry
            tau = steps - 1 - i
            r = tau_rows(tau)
            pair = [dts(t, tau) for t in tiles]
            drive = [pair[t][0] * act[t, r, :] for t in tiles]
            gy = [yg[t, r, :] for t in tiles]
            along = [None, None]
            down = [None, None]
            new_g, new_a = [], []
            for q, n in enumerate(names):
                bv, cv = bc[n, r, :], bc[states + n, r, :]
                pb = pc = None
                for t in tiles:
                    a2 = a2b[t, n]
                    decay = jnp.exp2(pair[t][1] * a2)
                    g = grads[2 * q + t] + gy[t] * cv
                    gb = g * bv
                    along[t] = gb if along[t] is None else along[t] + gb
                    v = g * drive[t]
                    pb = v if pb is None else pb + v
                    v = gy[t] * h[t, n, at8(tau * SUB + SUB, SUB), :]
                    pc = v if pc is None else pc + v
                    gd = g * decay
                    dla = gd * h[t, n, r, :]
                    v = dla * a2
                    down[t] = v if down[t] is None else down[t] + v
                    new_a.append(acc[2 * q + t] + dla * pair[t][0])
                    new_g.append(gd)
                bc[n, r, :] = pb
                bc[states + n, r, :] = pc
            for t in tiles:
                if lo == 0:
                    gsum[t, r, :] = along[t]
                    dsum[t, r, :] = down[t]
                else:
                    gsum[t, r, :] = gsum[t, r, :] + along[t]
                    dsum[t, r, :] = dsum[t, r, :] + down[t]
            return tuple(new_g), tuple(new_a)

        start = tuple(gin[t, n] for n in names for t in tiles)
        _, acc = lax.fori_loop(0, steps, back, (start, (zero,) * (2 * part)), unroll=4)
        for q, n in enumerate(names):
            for t in tiles:
                alg[n : n + 1, lanes(t)] = (
                    jnp.sum(acc[2 * q + t], axis=0, keepdims=True) * a2b[t, n][0:1, :] * LN2
                )

    gres[2] = owned_grad(2, z_wo).astype(BF16)
    late["gwo"] = share(2, wo_out.at[chans, :])

    def lin(i, carry):
        new = []
        rank = []
        for t in tiles:
            av, gv = act[t, blk(i), :], gsum[t, blk(i), :]
            v = (dsum[t, blk(i), :] * LN2 + av * gv) * one_less_exp(dt[t, blk(i), :])
            new.append(carry[t] + jnp.sum(v.reshape(rb // SUB, SUB, LANES), axis=0))
            low = v.astype(BF16)
            rank.append(low)
            dsum[t, blk(i), :] = low.astype(F32)
            gsum[t, blk(i), :] = dt[t, blk(i), :] * gv + param(SKIP, t) * yg[t, blk(i), :]
        mp[i] = dot_nt(jnp.concatenate(rank, axis=1), dtwp[...])
        return tuple(new)

    flush(first_sum)
    dtb_sum = lax.fori_loop(0, nblk, lin, (zero, zero))

    beside = lax.broadcasted_iota(jnp.int32, (wide, LANES), 1) - 64
    beside = beside - lax.broadcasted_iota(jnp.int32, (wide, LANES), 0) // LANES

    def collect(i):
        rows = pl.ds(pl.multiple_of(i * 2 * rb, 2 * rb), 2 * rb)
        v = jnp.concatenate([mp[2 * i], mp[2 * i + 1]], axis=0)
        for n in range(0, 2 * states, 2):
            pick = jnp.where(beside == n, 1.0, 0.0).astype(BF16)
            pair = jnp.concatenate([bc[n, rows, :], bc[n + 1, rows, :]], axis=1).astype(BF16)
            v = v + dot(pair, pick)
        mp[2 * i] = v[:rb, :]
        mp[2 * i + 1] = v[rb:, :]

    loop(nblk // 2, collect)

    def finish_early():
        v = end_rows(branch_b)
        mk = jnp.concatenate([maskc[half_rows, :]] * (width // LANES), axis=1)
        for copy in own_half:
            copy.wait()
        so_s[...] = (x_half[...].astype(F32) + mk * v).astype(BF16)
        late["so"] = [local(so_s, so_out.at[half_rows, :]), send(so_s, so_out.at[half_rows, :], sib)]

    def finish_z():
        v = owned_grad(1, z_wz).T
        gres[1] = v.astype(BF16)
        v = v * w_s[1, zrows, :].astype(F32)
        late["gain"] = v[:, :LANES] + v[:, LANES:]

    def small_a():
        low = jnp.concatenate([full[i] for i in range(nblk)], axis=0)
        linv = jnp.concatenate([tiles_bf(dsum, i) for i in range(nblk)], axis=0)
        g = dot_tn(low, linv)
        for i in range(4):
            spart[i, A_DTW : A_DTW + 16, :] = g[i * 16 : i * 16 + 16, :]
            spart[i, A_ALOG : A_ALOG + 4, :] = alg[i * 4 : i * 4 + 4, :]
            for t in tiles:
                spart[i, A_DTB : A_DTB + 1, lanes(t)] = jnp.sum(dtb_sum[t], axis=0, keepdims=True)
                spart[i, A_SKIP : A_SKIP + 1, lanes(t)] = jnp.sum(skip_sum[t], axis=0, keepdims=True)
        late["za"] = [
            send(spart.at[toward[d], pl.ds(0, A_ROWS)], srecv.at[d - 1], lines[d]) for d in (1, 2, 3)
        ]

    def shares():
        late["gwz"] = share(1, wg_out.at[1, :, chans])
        for copy in late["za"]:
            copy.wait_recv()
        sfull[c] = spart[z, 0:A_ROWS, :] + srecv[0] + srecv[1] + srecv[2]
        late["ga"] = [send(sfull.at[c], sfull.at[c], peers[p]) for p in (3, 1, 2)]

    def norm_z():
        finish_z()
        for dst, q in ((big_send, 1 - k), (big_keep, k)):
            for j in turns:
                fill(dst, j, q, [znat], lambda rows, cols: dot_nt(rows[0], w_s[1, cols, :]))

    flush(branch_b + branch_sent)
    second_sum = plane_sum(full2, [small_a, finish_early, norm_z, shares])

    pg = slope

    flush(z_wo)
    z_wx = []
    for t in tiles:

        def pre_grad(i, t=t):
            v = gsum[t, blk(i), :] + dot(full2[i], xp[:, lanes(t)])
            pg[t, blk(i), :] = v * pg[t, blk(i), :]

        loop(nblk, pre_grad)
        for j in range(3):
            pg[t, total + j * SUB : total + (j + 1) * SUB, :] = from_after(pg[t, j * SUB : (j + 1) * SUB, :], 0.0)

        def inner_grad(i, t=t):
            mine = segp[at8(PAD + i * rb, rb), :]
            v = pg[t, blk(i), :] * param(CONVW + 3, t)
            for j in range(1, 4):
                later = pg[t, at8(i * rb + j * SUB, rb), :]
                same = segp[at8(PAD + i * rb + j * SUB, rb), :] == mine
                v = v + jnp.where(same, later, 0.0) * param(CONVW + 3 - j, t)
            dsum[t, blk(i), :] = v

        loop(nblk, inner_grad)
        permute_out(dsum, gnat, (t,))
        gpart[0, lanes(t), :] = dot_tn(gnat[:, lanes(t)], xf[...]).astype(BF16)
        z_wx.append(
            [
                send(
                    gpart.at[0, pl.ds(t * LANES, LANES), pl.ds(pl.multiple_of(toward[d] * block, block), block)],
                    zrecv.at[0, d - 1, pl.ds(t * LANES, LANES)],
                    lines[d],
                )
                for d in (1, 2, 3)
            ]
        )

    flush(late["so"][1:])
    late["so"][0].wait()
    def norm_part(rows, cols):
        return dot_nt(rows[0], w_s[0, cols, :])

    norm_a = start_rows([gnat], norm_part, True)
    norm_b = middle_rows(norm_a, [gnat], norm_part)

    def conv_grad(i, carry):
        new = []
        mine = segp[at8(PAD + i * rb, rb), :]
        for t in tiles:
            v = pg[t, blk(i), :]
            new.append(carry[5 * t] + jnp.sum(v.reshape(rb // SUB, SUB, LANES), axis=0))
            for j in range(4):
                window = inner[t, at8(PAD + i * rb - j * SUB, rb), :]
                if j:
                    window = jnp.where(segp[at8(PAD + i * rb - j * SUB, rb), :] == mine, window, 0.0)
                new.append(carry[5 * t + 1 + j] + jnp.sum((v * window).reshape(rb // SUB, SUB, LANES), axis=0))
        return tuple(new)

    conv_sum = lax.fori_loop(0, nblk, conv_grad, (zero,) * 10)
    norm_b, _ = pass_rows(norm_b)
    mixv = jnp.concatenate([full2[i] for i in range(nblk)], axis=0)
    actv = jnp.concatenate([tiles_bf(act, i) for i in range(nblk)], axis=0)
    gx = dot_tn(mixv, actv)
    for i in range(4):
        conv_rows = [
            jnp.concatenate([jnp.sum(conv_sum[5 * t + j], axis=0, keepdims=True) for t in tiles], axis=1)
            for j in (4, 3, 2, 1, 0)
        ]
        bpart[i] = jnp.concatenate(
            [gx[i * 24 : i * 24 + 24, :]] + conv_rows + [jnp.zeros((3, wide), F32)], axis=0
        ).astype(BF16)
    z_b = [send(bpart.at[toward[d]], brecv.at[d - 1], lines[d]) for d in (1, 2, 3)]
    gain_sum = late["gain"]
    late["gwx"] = [[], []]

    def owned_half(q):
        for copy in z_wx[q]:
            copy.wait_recv()
        rows = slice(q * LANES, (q + 1) * LANES)
        v = gpart[0, rows, zcols].astype(F32)
        for d in range(3):
            v = v + zrecv[0, d, rows, :].astype(F32)
        v = v.T
        gres[0, :, rows] = v.astype(BF16)
        return v * w_s[0, zrows, rows].astype(F32)

    def share_half(q):
        rows = slice(q * LANES, (q + 1) * LANES)
        dst = wg_out.at[0, :, pl.ds(pl.multiple_of(c * wide + q * LANES, LANES), LANES)]
        late["gwx"][0].append(local(gres.at[0, :, rows], dst))
        late["gwx"][1].extend(send(gres.at[0, :, rows], dst, peers[p]) for p in (3, 1, 2))

    gain_sum = gain_sum + owned_half(0)
    share_half(0)
    for copy in z_b:
        copy.wait_recv()
    v = bpart[z].astype(F32)
    for d in range(3):
        v = v + brecv[d].astype(F32)
    bfull[c] = v.astype(BF16)
    g_b = [send(bfull.at[c], bfull.at[c], peers[p]) for p in (3, 1, 2)]
    for copy in norm_b:
        copy.wait_recv()
    last = []
    for q in range(2):
        part = slice(q * half // 2, (q + 1) * half // 2)
        ng = big_keep[0, part, :].astype(F32) + big_rb[0, part, :].astype(F32) + big_rb[2, part, :].astype(F32)
        xv = x_half[part, :].astype(F32)
        r = lax.rsqrt(jnp.mean(xv * xv, axis=1, keepdims=True) + EPS)
        sg = ng * gain_row
        sg_s[part, :] = (
            og_half[part, :].astype(F32) + r * sg - xv * (r * r * r) * jnp.mean(sg * xv, axis=1, keepdims=True)
        )
        there = sg_out.at[pl.ds(pl.multiple_of(k * half + q * half // 2, half // 2), half // 2), :]
        last.append((local(sg_s.at[part, :], there), send(sg_s.at[part, :], there, sib)))

    gain_sum = gain_sum + owned_half(1)
    for b in range(block // LANES):
        col = gain_sum[b * LANES : (b + 1) * LANES, :].T
        ggs[0, :, lanes(b)] = jnp.broadcast_to(jnp.sum(col, axis=0, keepdims=True), (SUB, LANES))
    s_gain = [send(ggs.at[0], ggs.at[p], peers[p]) for p in (1, 2, 3)]
    s_gain += [send(ggs.at[0], ggs.at[3 + p], (z, plane[p], 1 - k)) for p in (1, 2, 3)]
    s_gain.append(send(ggs.at[0], ggs.at[7], sib))
    share_half(1)

    for copy in late["ga"] + g_b:
        copy.wait_recv()
    for i in range(4):
        cols = slice(i * wide, (i + 1) * wide)
        sm_out[0:24, cols] = bfull[i, B_XP : B_XP + 24, :].astype(F32)
        sm_out[24:44, cols] = sfull[i, A_DTW : A_ALOG + 4, :]
    cv_out[0:5, :] = bfull[z, B_CONVW : B_CONVB + 1, :].astype(F32)
    cv_out[5:7, :] = sfull[z, A_DTB : A_SKIP + 1, :]
    for copy in s_gain:
        copy.wait_recv()
    v = ggs[0]
    for i in range(1, 8):
        v = v + ggs[i]
    gg_out[...] = v[0:1, :] / early[z, GAIN : GAIN + 1, :]

    late["so"][1].wait_recv()
    for name in ("gwo", "gwz"):
        late[name][0].wait()
        for copy in late[name][1:]:
            copy.wait_recv()
    for copy in late["gwx"][0]:
        copy.wait()
    for copy in late["gwx"][1]:
        copy.wait_recv()
    for copy, sent in last:
        copy.wait()
        sent.wait_recv()
    flush(list(pending))


def fused(
    stream_in, norm_gain, in_weight, out_weight, xproj_weight, dt_weight, a_log, convolution_weight,
    convolution_bias, step_size_bias, skip_term_scale, seg_ids, pad_mask, out_grad,
):
    _, tok, width = stream_in.shape
    wide = 2 * LANES
    total = 4 * tok
    block = width // 4
    states = 4 * a_log.shape[0]
    vm = pl.BlockSpec(memory_space=pltpu.VMEM)
    hbm = pl.BlockSpec(memory_space=pl.ANY)
    f, b = (lambda *s: pltpu.VMEM(s, F32)), (lambda *s: pltpu.VMEM(s, BF16))
    scan = f(2, total, LANES)
    scratch = dict(
        so_s=b(tok // 2, width), x_half=b(tok // 2, width), og_half=b(tok // 2, width), xf=b(total, width), mg=b(total, width), w_s=b(2, width, wide), wo_s=b(wide, width),
        early=f(4, SUB, wide), pk_f=f(4, ROWS_P, wide), pk_s=b(4, ROWS_P, wide), segs=pltpu.VMEM((4, SUB, tok), jnp.int32),
        segp=f(total + 2 * PAD, LANES), maskc=f(tok, LANES), nat=scan, inner=f(2, total + PAD, LANES),
        slope=f(2, total + PAD, LANES), act=scan, gate=scan, dt=scan, yg=scan, y=scan,
        bc=f(2 * states, total, LANES), h=f(2, states, total + SUB, LANES), a2b=f(2, states, SUB, LANES),
        st=f(2, states, SUB, LANES), gin=f(2, states, SUB, LANES), cum=f(2, SUB, LANES), alg=f(states, wide),
        full=b(8, 128, LANES), full2=b(8, 128, LANES), mp=f(8, 128, LANES), sum_a=b(4, 128, LANES),
        recv_a=f(4, 128, LANES), recv_b=b(3, 128, LANES), xp=b(LANES, wide), dtwp=b(LANES, wide),
        big_send=b(4, tok // 2, width), big_keep=b(4, tok // 2, width),
        big_recv=b(4, tok // 2, width), big_rb=b(3, tok // 2, width), gpart=b(2, wide, width),
        zrecv=b(3, 3, wide, block), gres=b(3, block, wide), gnat=b(total, wide), znat=b(total, wide),
        spart=f(4, ROWS, wide), srecv=f(3, A_ROWS, wide), sfull=f(4, A_ROWS, wide),
        bpart=b(4, B_ROWS, wide), brecv=b(3, B_ROWS, wide), bfull=b(4, B_ROWS, wide), sown=f(SUB, wide),
        ggs=f(8, SUB, block), sg_s=f(tok // 2, width),
        ssem=pltpu.SemaphoreType.DMA((144,)), rsem=pltpu.SemaphoreType.DMA((144,)),
        lsem=pltpu.SemaphoreType.DMA((16,)),
    )
    outs = pl.pallas_call(
        fused_kernel,
        out_shape=[
            jax.ShapeDtypeStruct((tok, width), BF16),
            jax.ShapeDtypeStruct((tok, width), F32),
            jax.ShapeDtypeStruct((2, block, 4 * wide), BF16),
            jax.ShapeDtypeStruct((4 * wide, block), BF16),
            jax.ShapeDtypeStruct((48, 4 * wide), F32),
            jax.ShapeDtypeStruct((8, wide), F32),
            jax.ShapeDtypeStruct((1, block), F32),
        ],
        in_specs=[hbm] * 4 + [vm] * 10,
        out_specs=[hbm] * 4 + [vm] * 3,
        scratch_shapes=list(scratch.values()),
        compiler_params=pltpu.CompilerParams(
            collective_id=0, has_side_effects=True, vmem_limit_bytes=VMEM_LIMIT
        ),
    )(
        stream_in.reshape(tok, width), out_grad.reshape(tok, width), in_weight, out_weight, xproj_weight,
        dt_weight, a_log, convolution_weight.reshape(4, block), convolution_bias, step_size_bias,
        skip_term_scale, norm_gain, seg_ids, pad_mask,
    )
    steps = 2
    part = tok // steps

    def whole(*shape):
        return pl.BlockSpec(shape, lambda i: (0,) * len(shape))

    return pl.pallas_call(
        finish_kernel,
        grid=(steps,),
        out_shape=[
            jax.ShapeDtypeStruct((1, tok, width), BF16),
            jax.ShapeDtypeStruct((1, tok, width), F32),
            jax.ShapeDtypeStruct((block,), F32),
            jax.ShapeDtypeStruct((2, block, 4 * wide), F32),
            jax.ShapeDtypeStruct((4 * wide, block), F32),
            jax.ShapeDtypeStruct((24, 4 * wide), F32),
            jax.ShapeDtypeStruct((16, 4 * wide), F32),
            jax.ShapeDtypeStruct((4, 4 * wide), F32),
            jax.ShapeDtypeStruct((4, 1, wide), F32),
            jax.ShapeDtypeStruct((1, wide), F32),
            jax.ShapeDtypeStruct((1, wide), F32),
            jax.ShapeDtypeStruct((1, wide), F32),
        ],
        in_specs=[
            pl.BlockSpec((part, width), lambda i: (i, 0)),
            pl.BlockSpec((part, width), lambda i: (i, 0)),
            pl.BlockSpec((2, block // steps, 4 * wide), lambda i: (0, i, 0)),
            pl.BlockSpec((4 * wide // steps, block), lambda i: (i, 0)),
            whole(48, 4 * wide),
            whole(8, wide),
            whole(1, block),
        ],
        out_specs=[
            pl.BlockSpec((1, part, width), lambda i: (0, i, 0)),
            pl.BlockSpec((1, part, width), lambda i: (0, i, 0)),
            whole(block),
            pl.BlockSpec((2, block // steps, 4 * wide), lambda i: (0, i, 0)),
            pl.BlockSpec((4 * wide // steps, block), lambda i: (i, 0)),
            whole(24, 4 * wide),
            whole(16, 4 * wide),
            whole(4, 4 * wide),
            whole(4, 1, wide),
            whole(1, wide),
            whole(1, wide),
            whole(1, wide),
        ],
        compiler_params=pltpu.CompilerParams(vmem_limit_bytes=VMEM_LIMIT),
    )(*outs)


def finish_kernel(
    so_ref, sg_ref, wg_ref, wo_ref, sm_ref, cv_ref, gg_ref,
    so_out, sg_out, gg_out, wg_out, wo_out, xp_out, dtw_out, alog_out, cw_out, cb_out, dtb_out, skip_out,
):
    so_out[0] = so_ref[...]
    sg_out[0] = sg_ref[...]
    wg_out[...] = wg_ref[...].astype(F32)
    wo_out[...] = wo_ref[...].astype(F32)

    @pl.when(pl.program_id(0) == 0)
    def _():
        gg_out[...] = gg_ref[0]
        xp_out[...] = sm_ref[0:24, :]
        dtw_out[...] = sm_ref[24:40, :]
        alog_out[...] = sm_ref[40:44, :]
        for j in range(4):
            cw_out[j] = cv_ref[j : j + 1, :]
        cb_out[...] = cv_ref[4:5, :]
        dtb_out[...] = cv_ref[5:6, :]
        skip_out[...] = cv_ref[6:7, :]


def solution(mesh):
    in_specs = (
        P("dp", "ctx", None),
        P("dp"),
        P(None, "dp", "tp"),
        P("tp", "dp"),
        P("dp", "tp"),
        P("dp", "tp"),
        P("dp", "tp"),
        P(None, "tp", "dp"),
        P("tp", "dp"),
        P("tp", "dp"),
        P("tp", "dp"),
        P("dp", "ctx"),
        P("dp", "ctx"),
        P("dp", "ctx", None),
    )
    out_specs = (
        P("dp", "ctx", None),
        P("dp", "ctx", None),
        P("dp"),
        P(None, "dp", "tp"),
        P("tp", "dp"),
        P("dp", "tp"),
        P("dp", "tp"),
        P("dp", "tp"),
        P(None, "tp", "dp"),
        P("tp", "dp"),
        P("tp", "dp"),
        P("tp", "dp"),
    )

    def run(*args):
        stream, weight = args[0].shape, args[2].shape
        plane_fits = (mesh.shape["dp"], mesh.shape["ctx"], mesh.shape["tp"]) == (4, 4, 2)
        sizes_fit = stream == (4, 1024, 1024) and weight == (2, 1024, 2048)
        part = fused if plane_fits and sizes_fit else shards
        return jax.shard_map(
            part, mesh=mesh, in_specs=in_specs, out_specs=out_specs, check_vma=False
        )(*args)

    return run
```
